128 devices in a mesh: dom: 128 (over z, x, y, core).
Axes of the slice: x: 4, y: 4, z: 4, core: 2. Of those that a mesh axis runs over, the one named last changes fastest.
Arguments:
- state: float32 [6144, 2048], P('dom'), may hold values from -6 to 6
- cotangent: float32 [6144, 2048], P('dom'), may hold values from -6 to 6
- elem_count: int32 [128], P('dom'), may hold values from 24 to 48, as said below
- face_src: int32 [36864], P('dom'), may hold values from 0 to 543, as said below
- face_orient: int32 [36864], P('dom'), may hold values from 0 to 7
- send_face: int32 [32768], P('dom'), may hold values from -1 to 287, as said below
- vol_weight: float32 [2, 3, 32, 32], replicated, may hold values from -0.15625 to 0.15625
- flux_w1: float32 [2, 64, 64], replicated, may hold values from -0.75 to 0.75
- flux_b1: float32 [2, 64], replicated, may hold values from -3 to 3
- flux_w2: float32 [2, 64, 32], replicated, may hold values from -0.75 to 0.75
Outputs:
- grad_state: float32 [6144, 2048], P('dom')
- grad_w1: float32 [2, 64, 64], replicated
- grad_b1: float32 [2, 64], replicated
- grad_w2: float32 [2, 64, 32], replicated
The draws below stay inside these ranges and needn't reach their ends.
Inputs may be any that keep to these rules, and one draw needn't show every extreme that they name: `elem_count`: one partition holds exactly 48 live elements; the others at least half of that. `send_face`: block o of a partition's 2 * 4 * 32 slots goes to the partition at offset d (as in the reference program); slot c of a block is filled (a local face, each face at most once) exactly when c is below the number of faces shared with that partition, else -1. Partitions at offsets 1 and 4 share exactly 32 faces where they exist; the counts are symmetric between two partitions. `face_src`: A value of 288 or more always names a slot that its sender fills, and the face it appears on is the face that the partition sends into the mirrored slot; faces are otherwise paired within the partition or are their own partners.
All inputs are finite; a program needn't handle non-finite values.
Results may differ from the reference program's by a relative error of at most 0.00011.
Values sent between devices are 32-bit elements; how exact they have to be, the bound alone decides.
A program may use at most 128 MiB of HBM per device.

```python
import jax
import jax.numpy as jnp
import numpy as np
from jax import lax

ELEM_DEV = 48
CH = 32
FH = 64
CAP = 32
NEIGH = 4
LAYERS = 2
ELEMENTS = 6144
N_DOM = 128


def offset_values():
    return [level + 1 for level in range(NEIGH)] + [-(level + 1) for level in range(NEIGH)]


def face_tables(key):
    face_count = 6 * ELEM_DEV
    slot_count = 2 * NEIGH * CAP
    count_key, perm_key = jax.random.split(key)
    nearby = jax.random.randint(count_key, (N_DOM, NEIGH), 1, CAP + 1)
    nearby = nearby.at[:, 0].set(CAP).at[:, NEIGH - 1].set(CAP)
    device = jnp.arange(N_DOM, dtype=jnp.int32)
    columns = []
    for offset in offset_values():
        reach = abs(offset) - 1
        if offset > 0:
            holder = device
        else:
            holder = device + offset
        inside = (device + offset >= 0) & (device + offset < N_DOM)
        columns.append(jnp.where(inside, nearby[jnp.clip(holder, 0, N_DOM - 1), reach], 0))
    counts = jnp.stack(columns, axis=1)
    filled = (jnp.arange(CAP)[None, None, :] < counts[:, :, None]).reshape(N_DOM, slot_count)
    order = jnp.cumsum(filled.astype(jnp.int32), axis=1) - 1
    perms = jax.vmap(lambda subkey: jax.random.permutation(subkey, face_count))(jax.random.split(perm_key, N_DOM)).astype(jnp.int32)
    sends = jnp.where(filled, jnp.take_along_axis(perms, jnp.clip(order, 0, face_count - 1), axis=1), -1).astype(jnp.int32)
    used = jnp.sum(filled.astype(jnp.int32), axis=1)
    place = jnp.arange(face_count, dtype=jnp.int32)[None, :]
    remain = place - used[:, None]
    mate = used[:, None] + jnp.bitwise_xor(jnp.maximum(remain, 0), 1)
    mate = jnp.where(mate < face_count, mate, place)
    partner = jnp.take_along_axis(perms, mate, axis=1)
    sources = jnp.zeros((N_DOM, face_count), jnp.int32).at[device[:, None], perms].set(partner)
    slot = jnp.arange(slot_count, dtype=jnp.int32)
    mirror = (slot // CAP + NEIGH) % (2 * NEIGH) * CAP + slot % CAP
    target = jnp.where(sends >= 0, sends, face_count)
    values = jnp.broadcast_to(face_count + mirror[None, :], (N_DOM, slot_count)).astype(jnp.int32)
    sources = sources.at[device[:, None], target].set(values, mode='drop')
    return (sources, sends)


def draw_face_src(key, part):
    return face_tables(key)[0].reshape(-1).astype(jnp.int32)


def draw_send_face(key, part):
    return face_tables(key)[1].reshape(-1).astype(jnp.int32)


def draw_elem_count(key, part):
    key = jax.random.fold_in(key, 7)
    count_key, full_key = jax.random.split(key)
    counts = jax.random.randint(count_key, (N_DOM,), ELEM_DEV // 2, ELEM_DEV + 1)
    fullest = jax.random.randint(full_key, (), 0, N_DOM)
    return counts.at[fullest].set(ELEM_DEV).astype(jnp.int32)


def with_ends(drawn, stream_key, least, top_value):
    longest = drawn.shape.index(max(drawn.shape))
    spots = []
    for shift in (0, 1):
        where = [jax.random.randint(jax.random.fold_in(stream_key, axis), (), 0, length) for axis, length in enumerate(drawn.shape)]
        where[longest] = (where[longest] + shift) % drawn.shape[longest]
        spots.append(tuple(where))
    return drawn.at[spots[0]].set(least).at[spots[1]].set(top_value)


def levels(rng, extent, pieces, low, high):
    factor_of = 1.0
    for dim, parts in pieces:
        draws = jax.random.uniform(jax.random.fold_in(jax.random.fold_in(rng, 6), dim), (parts,), jnp.float32, low / len(pieces), high / len(pieces))
        factor_of = factor_of * jnp.repeat(jnp.exp(draws), extent[dim] // parts).reshape((-1,) + (1,) * (len(extent) - 1 - dim))
    return factor_of


def gaussian(stream_key, extent, scale, bound, cuts=(), held_as=jnp.bfloat16):
    values = scale * jax.random.normal(stream_key, extent, jnp.float32)
    if cuts:
        values = values * levels(stream_key, extent, cuts, -0.22, 0.18)
    return jnp.clip(values, -bound, bound).astype(held_as)


def setup_inputs(seed: int = 0) -> dict:
    seeds = jax.random.split(jax.random.key(seed), 11)
    return {
        "state": gaussian(seeds[0], (ELEMENTS, 64 * CH), 1.0, 6.0, ((0, 128),), jnp.float32),
        "cotangent": gaussian(seeds[1], (ELEMENTS, 64 * CH), 1.0, 6.0, ((0, 128),), jnp.float32),
        "elem_count": draw_elem_count(jax.random.fold_in(seeds[10], 71), 0),
        "face_src": draw_face_src(jax.random.fold_in(seeds[10], 71), 0),
        "face_orient": with_ends(jax.random.randint(seeds[4], (N_DOM * 6 * ELEM_DEV,), 0, 8), jax.random.fold_in(seeds[4], 1), 0, 7).astype(jnp.int32),
        "send_face": draw_send_face(jax.random.fold_in(seeds[10], 71), 0),
        "vol_weight": gaussian(seeds[6], (LAYERS, 3, CH, CH), (48 * CH) ** -0.5, 0.15625, (), jnp.float32),
        "flux_w1": gaussian(seeds[7], (LAYERS, 2 * CH, FH), (2 * CH) ** -0.5, 0.75, (), jnp.float32),
        "flux_b1": gaussian(seeds[8], (LAYERS, FH), 0.5, 3.0, (), jnp.float32),
        "flux_w2": gaussian(seeds[9], (LAYERS, FH, CH), FH ** -0.5, 0.75, (), jnp.float32),
    }


HIGHEST = lax.Precision.HIGHEST
STEP_SIZE = 0.25

def neighbour_offsets():
    return [level + 1 for level in range(NEIGH)] + [-(level + 1) for level in range(NEIGH)]

def face_nodes():
    table = np.zeros((6, 16), np.int32)
    for facet in range(6):
        fixed_value = 0 if facet % 2 == 0 else 3
        for first in range(4):
            for second in range(4):
                if facet < 2:
                    coords = (fixed_value, first, second)
                elif facet < 4:
                    coords = (first, fixed_value, second)
                else:
                    coords = (first, second, fixed_value)
                table[facet, 4 * first + second] = 16 * coords[0] + 4 * coords[1] + coords[2]
    return table

def select_matrix():
    matrix = np.zeros((96, 64), np.float32)
    nodes = face_nodes()
    for facet in range(6):
        for member in range(16):
            matrix[16 * facet + member, nodes[facet, member]] = 1.0
    return matrix

def orient_table():
    table = np.zeros((8, 16), np.int32)
    for variant in range(8):
        for member in range(16):
            first, second = (member // 4, member % 4)
            if variant >= 4:
                first, second = (second, first)
            for turn in range(variant % 4):
                first, second = (second, 3 - first)
            table[variant, member] = 4 * first + second
    return table

def deriv_matrix():
    points = np.array([-1.0, -np.sqrt(0.2), np.sqrt(0.2), 1.0])
    weights = np.array([np.prod([points[row_at] - points[other] for other in range(4) if other != row_at]) for row_at in range(4)])
    matrix = np.zeros((4, 4))
    for row_at in range(4):
        for column in range(4):
            if row_at != column:
                matrix[row_at, column] = weights[row_at] / weights[column] / (points[row_at] - points[column])
        matrix[row_at, row_at] = -np.sum(matrix[row_at])
    return matrix

def orient_index(face_orient):
    table = jnp.asarray(orient_table(), jnp.int32)
    match = face_orient[:, None] == jnp.arange(8, dtype=jnp.int32)[None, :]
    return lax.optimization_barrier(jnp.sum(jnp.where(match[:, :, None], table[None, :, :], 0), axis=1)).astype(jnp.int32)

def face_traces(field):
    row_count = field.shape[0]
    width = field.shape[1] // 64
    select = jnp.asarray(select_matrix(), jnp.float32)
    nodes = field.reshape(row_count, 64, width)
    return jnp.einsum('qn,enc->eqc', select, nodes, precision=HIGHEST).reshape(row_count * 6, 16 * width)

def outer_traces(pool, source_rows, orient_rows):
    width = pool.shape[1] // 16
    tiles = pool[source_rows].reshape(-1, 16, width)
    turned = jnp.take_along_axis(tiles, orient_rows[:, :, None], axis=1)
    return turned.reshape(-1, 16 * width)

def flux_step(field, inner, outer, vol_w, weight_one, bias_one, weight_two):
    row_count = field.shape[0]
    width = weight_two.shape[1]
    deriv = jnp.asarray(deriv_matrix(), jnp.float32)
    select = jnp.asarray(select_matrix(), jnp.float32)
    cube = field.reshape(row_count, 4, 4, 4, width)
    along_i = jnp.einsum('ai,eijkc->eajkc', deriv, cube, precision=HIGHEST)
    along_j = jnp.einsum('aj,eijkc->eiakc', deriv, cube, precision=HIGHEST)
    along_k = jnp.einsum('ak,eijkc->eijac', deriv, cube, precision=HIGHEST)
    volume = jnp.einsum('eijkc,cd->eijkd', along_i, vol_w[0], precision=HIGHEST)
    volume = volume + jnp.einsum('eijkc,cd->eijkd', along_j, vol_w[1], precision=HIGHEST)
    volume = volume + jnp.einsum('eijkc,cd->eijkd', along_k, vol_w[2], precision=HIGHEST)
    inner_rows = inner.reshape(-1, width)
    outer_rows = outer.reshape(-1, width)
    hidden = jnp.tanh(jnp.dot(inner_rows, weight_one[:width], precision=HIGHEST) + jnp.dot(outer_rows, weight_one[width:], precision=HIGHEST) + bias_one)
    flux = jnp.dot(hidden, weight_two, precision=HIGHEST).reshape(row_count, 96, width)
    lifted = jnp.einsum('qn,eqc->enc', select, flux, precision=HIGHEST)
    change = lifted - volume.reshape(row_count, 64, width)
    return field + STEP_SIZE * change.reshape(row_count, 64 * width)

def reference(state, cotangent, elem_count, face_src, face_orient, send_face, vol_weight, flux_w1, flux_b1, flux_w2):
    total = state.shape[0]
    face_count = 6 * ELEM_DEV
    slot_count = 2 * NEIGH * CAP
    element_ids = jnp.arange(total, dtype=jnp.int32)
    alive_mask = (element_ids % ELEM_DEV < elem_count[element_ids // ELEM_DEV]).astype(jnp.float32)[:, None]
    face_ids = jnp.arange(N_DOM * face_count, dtype=jnp.int32)
    owner = face_ids // face_count
    offsets = jnp.asarray(neighbour_offsets(), jnp.int32)
    slot = jnp.clip(face_src - face_count, 0, slot_count - 1).astype(jnp.int32)
    sender = jnp.clip(owner - offsets[slot // CAP], 0, N_DOM - 1).astype(jnp.int32)
    sender_face = send_face.reshape(N_DOM, slot_count)[sender, slot]
    source_rows = jnp.where(face_src < face_count, owner * face_count + face_src, sender * face_count + sender_face).astype(jnp.int32)
    orient_rows = orient_index(face_orient)
    stepper = jax.checkpoint(flux_step)

    def forward(start, weight_one, bias_one, weight_two):
        field = start * alive_mask
        for layer in range(LAYERS):
            inner = face_traces(field)
            outer = outer_traces(inner, source_rows, orient_rows)
            field = stepper(field, inner, outer, vol_weight[layer], weight_one[layer], bias_one[layer], weight_two[layer])
        return field
    result, backward = jax.vjp(forward, state, flux_w1, flux_b1, flux_w2)
    grad_field, grad_one, grad_bias, grad_two = backward(cotangent)
    factor = (96.0 * total) ** (-0.5)
    return (grad_field, grad_one * factor, grad_bias * factor, grad_two * factor)
```

```python
import functools

import jax
import jax.numpy as jnp
import numpy as np
from jax import lax
from jax.experimental import pallas as pl
from jax.experimental.pallas import tpu as pltpu
from jax.sharding import PartitionSpec as P

MESH = pl.DeviceIdType.MESH
HIGHEST = lax.Precision.HIGHEST
F32 = jnp.float32
BF16 = jnp.bfloat16
I32 = jnp.int32
NEIGH = 4
BLOCKS = 2 * NEIGH
CAP = 32
SLOTS = BLOCKS * CAP
STEP_SIZE = 0.25
E = 48
FACES = 6 * E
OFFSETS = [level + 1 for level in range(NEIGH)] + [-(level + 1) for level in range(NEIGH)]


def deriv_matrix():
    points = np.array([-1.0, -np.sqrt(0.2), np.sqrt(0.2), 1.0])
    weights = np.array(
        [np.prod([points[r] - points[o] for o in range(4) if o != r]) for r in range(4)]
    )
    matrix = np.zeros((4, 4))
    for r in range(4):
        for c in range(4):
            if r != c:
                matrix[r, c] = weights[r] / weights[c] / (points[r] - points[c])
        matrix[r, r] = -np.sum(matrix[r])
    return matrix


DERIV = deriv_matrix()


def iota(shape, dim):
    return lax.broadcasted_iota(I32, shape, dim)


def dot(a, b):
    return jnp.dot(a, b, preferred_element_type=F32)


def dot_nt(a, b):
    return lax.dot_general(a, b, (((1,), (1,)), ((), ())), preferred_element_type=F32)


def dot_tn(a, b):
    return lax.dot_general(a, b, (((0,), (0,)), ((), ())), preferred_element_type=F32)


def dot_full(a, b):
    return jnp.dot(a, b, preferred_element_type=F32, precision=HIGHEST)


def split(x):
    high = x.astype(BF16)
    return high, (x - high.astype(F32)).astype(BF16)


def three(op, a, b):
    return op(a[0], b[0]) + op(a[1], b[0]) + op(a[0], b[1])


def lanes(a):
    return pl.ds(pl.multiple_of(a * 128, 128), 128)


def ones_where(match, dtype=F32):
    return jnp.where(match, 1.0, 0.0).astype(dtype)


def kernel(
    count,
    state_ref, cot_ref, live_ref, src_ref, orient_ref, send_ref, vol_ref, w1_ref, b1_ref, w2_ref, deriv_ref,
    out_ref, out_w1, out_b1, out_w2,
    field, grad, volume, vol_y, vol_xh, vol_xl,
    trace_h, trace_l, raw, pair_h, pair_l, hid, flux, gflux_h, gflux_l, gpre_h, gpre_l, gin, gout, turn_h, turn_l,
    sel, sel_t, loc, rem, loc_t, rem_t, masks,
    w1h, w1l, w2h, w2l, vh, vl, vth, vtl, bias,
    sent, got, packed, part, part_sum, total,
    send_sem, recv_sem, ar_send, ar_recv,
):
    me = lax.axis_index("dom")
    group = 16
    others = count // group
    base = (me // group) * group
    mine = lax.rem(me, group)
    rank = me // group

    def neighbour(offset):
        return lax.rem(me + offset + count, count)

    def in_group(step):
        return base + lax.rem(mine + step, group)

    def across(step):
        return lax.rem(rank + step, others) * group + mine

    barrier = pltpu.get_barrier_semaphore()
    partners = [neighbour(o) for o in OFFSETS]
    partners += [in_group(s) for s in range(1, group)]
    partners += [across(s) for s in range(1, others)]
    for device in partners:
        pl.semaphore_signal(barrier, inc=1, device_id=(device,), device_id_type=MESH)

    def exchange(which, sign):
        copies = []
        for block in (3, 7, 2, 6, 1, 5, 0, 4):
            rows = pl.ds(block * CAP, CAP)
            copies.append(
                pltpu.make_async_remote_copy(
                    src_ref=sent.at[which, rows],
                    dst_ref=got.at[which, rows],
                    send_sem=send_sem.at[which, block],
                    recv_sem=recv_sem.at[which, block],
                    device_id=(neighbour(sign * OFFSETS[block]),),
                    device_id_type=MESH,
                )
            )
        for copy in copies:
            copy.start()
        return copies

    for f in range(6):
        sel_t[f * E : (f + 1) * E, :] = ones_where(6 * iota((E, SLOTS), 0) + f == send_ref[...], BF16)
    eye = ones_where(iota((SLOTS, SLOTS), 0) == iota((SLOTS, SLOTS), 1), BF16)
    sel[...] = dot_nt(eye, sel_t[...]).astype(BF16)

    def tile(ref, n):
        return ref[:, n * 128 : (n + 1) * 128]

    group_of_lane = iota((E, 128), 1) >> 5

    def traces(ref, emit):
        for a in range(4):
            emit(0, a, tile(ref, a))
            emit(1, a, tile(ref, 12 + a))
            emit(2, a, tile(ref, 4 * a))
            emit(3, a, tile(ref, 4 * a + 3))
            first = tile(ref, 4 * a)
            last = pltpu.roll(tile(ref, 4 * a), 32, 1)
            for b in range(1, 4):
                node = tile(ref, 4 * a + b)
                first = jnp.where(group_of_lane == b, pltpu.roll(node, 32 * b, 1), first)
                moved = node if b == 3 else pltpu.roll(node, 32 * (b + 1), 1)
                last = jnp.where(group_of_lane == b, moved, last)
            emit(4, a, first)
            emit(5, a, last)

    def lift(ref, i, j):
        at = lambda f, a: ref[f * E : (f + 1) * E, a * 128 : (a + 1) * 128]
        low, high = at(4, i), at(5, i)
        low = pltpu.roll(low, (128 - 32 * j) % 128, 1) if j else low
        high = pltpu.roll(high, 96 - 32 * j, 1) if j < 3 else high
        value = jnp.where(group_of_lane == 0, low, jnp.where(group_of_lane == 3, high, 0.0))
        if i == 0:
            value = value + at(0, j)
        if i == 3:
            value = value + at(1, j)
        if j == 0:
            value = value + at(2, i)
        if j == 3:
            value = value + at(3, i)
        return value

    def keep_traces(layer):
        def emit(f, a, value):
            high, low = split(value)
            rows, cols = slice(f * E, (f + 1) * E), slice(a * 128, (a + 1) * 128)
            trace_h[rows, cols] = high
            trace_l[rows, cols] = low
            pair_h[layer, a, rows, 0:128] = high
            pair_l[layer, a, rows, 0:128] = low

        return emit

    def keep_gflux(f, a, value):
        high, low = split(STEP_SIZE * value)
        rows, cols = slice(f * E, (f + 1) * E), slice(a * 128, (a + 1) * 128)
        gflux_h[rows, cols] = high
        gflux_l[rows, cols] = low

    def volume_of(ref, layer, adjoint):
        for n in range(16):
            high, low = split(tile(ref, n))
            vol_xh[n * E : (n + 1) * E, :] = high
            vol_xl[n * E : (n + 1) * E, :] = low
        wh, wl = (vth, vtl) if adjoint else (vh, vl)
        vol_y[...] = three(dot, (vol_xh[...], vol_xl[...]), (wh[layer], wl[layer]))
        deriv = DERIV.T if adjoint else DERIV
        for i in range(4):
            for j in range(4):
                n = 4 * i + j
                value = vol_y[n * E : (n + 1) * E, 256:384]
                for o in range(4):
                    if abs(deriv[i, o]) > 1e-12:
                        at = 4 * o + j
                        value = value + float(deriv[i, o]) * vol_y[at * E : (at + 1) * E, 0:128]
                    if abs(deriv[j, o]) > 1e-12:
                        at = 4 * i + o
                        value = value + float(deriv[j, o]) * vol_y[at * E : (at + 1) * E, 128:256]
                volume[:, n * 128 : (n + 1) * 128] = value

    def flip_lanes(x, even):
        return jnp.where(even, pltpu.roll(x, 32, 1), pltpu.roll(x, 96, 1))

    def swap(x, by_group):
        odd, upper = by_group
        stage = [None] * 4
        for a in (0, 2):
            stage[a] = jnp.where(odd, pltpu.roll(x[a + 1], 32, 1), x[a])
            stage[a + 1] = jnp.where(odd, x[a + 1], pltpu.roll(x[a], 96, 1))
        out = [None] * 4
        for a in (0, 1):
            out[a] = jnp.where(upper, pltpu.roll(stage[a + 2], 64, 1), stage[a])
            out[a + 2] = jnp.where(upper, stage[a + 2], pltpu.roll(stage[a], 64, 1))
        return out

    def lane_masks():
        groups = iota((E, 128), 1) >> 5
        return (groups & 1) == 1, groups >= 2

    def row_masks(rows):
        return [masks[rows, m * 128 : (m + 1) * 128] > 0.5 for m in range(3)]

    def orient_rows(layer):
        def body(step, carry):
            rows = pl.ds(pl.multiple_of(step * E, E), E)
            odd, upper = lane_masks()
            up, across_, turned = row_masks(rows)
            x = [raw[rows, a * 128 : (a + 1) * 128] for a in range(4)]
            x = [jnp.where(up, x[3 - a], x[a]) for a in range(4)]
            x = [jnp.where(across_, flip_lanes(v, jnp.logical_not(odd)), v) for v in x]
            y = swap(x, (odd, upper))
            for a in range(4):
                high, low = split(jnp.where(turned, y[a], x[a]))
                pair_h[layer, a, rows, 128:256] = high
                pair_l[layer, a, rows, 128:256] = low
            return carry

        lax.fori_loop(0, 6, body, 0)

    def turn_back_rows():
        def body(step, carry):
            rows = pl.ds(pl.multiple_of(step * E, E), E)
            odd, upper = lane_masks()
            up, across_, turned = row_masks(rows)
            x = [gout[rows, a * 128 : (a + 1) * 128] for a in range(4)]
            y = swap(x, (odd, upper))
            x = [jnp.where(turned, y[a], x[a]) for a in range(4)]
            x = [jnp.where(across_, flip_lanes(v, jnp.logical_not(odd)), v) for v in x]
            for a in range(4):
                high, low = split(jnp.where(up, x[3 - a], x[a]))
                turn_h[rows, a * 128 : (a + 1) * 128] = high
                turn_l[rows, a * 128 : (a + 1) * 128] = low
            return carry

        lax.fori_loop(0, 6, body, 0)

    def hidden_of(layer, with_flux):
        def body(a, carry):
            x = (pair_h[layer, a], pair_l[layer, a])
            h = jnp.tanh(three(dot, x, (w1h[layer], w1l[layer])) + bias[layer, 0:1, :])
            hid[layer, a] = h
            if with_flux:
                flux[:, lanes(a)] = three(dot, split(h), (w2h[layer], w2l[layer]))
            return carry

        lax.fori_loop(0, 4, body, 0)

    def flux_back(layer):
        def body(a, carry):
            g = (gflux_h[:, lanes(a)], gflux_l[:, lanes(a)])
            h = hid[layer, a]
            pre = split(three(dot_nt, g, (w2h[layer], w2l[layer])) * (1.0 - h * h))
            gpre_h[a] = pre[0]
            gpre_l[a] = pre[1]
            both = three(dot_nt, pre, (w1h[layer], w1l[layer]))
            gin[:, lanes(a)] = both[:, 0:128]
            gout[:, lanes(a)] = both[:, 128:256]
            return carry

        lax.fori_loop(0, 4, body, 0)

    def weight_grads(layer):
        def body(a, carry):
            one, two, row = carry
            x = (pair_h[layer, a], pair_l[layer, a])
            pre = (gpre_h[a], gpre_l[a])
            g = (gflux_h[:, lanes(a)], gflux_l[:, lanes(a)])
            one = one + three(dot_tn, x, pre)
            two = two + three(dot_tn, split(hid[layer, a]), g)
            row = row + jnp.sum(pre[0].astype(F32) + pre[1].astype(F32), axis=0, keepdims=True)
            return one, two, row

        zeros = lambda *shape: jnp.zeros(shape, F32)
        one, two, row = lax.fori_loop(0, 4, body, (zeros(256, 256), zeros(256, 128), zeros(1, 256)))
        r, c = iota((256, 256), 0), iota((256, 256), 1)
        one = jnp.where(((r >> 5) & 3) == (c >> 6), one, 0.0)
        r, c = iota((256, 128), 0), iota((256, 128), 1)
        two = jnp.where((r >> 6) == (c >> 5), two, 0.0)
        r, c = iota((64, 256), 0), iota((64, 256), 1)
        pick_in = ones_where(r == ((c >> 7) * 32 + (c & 31)))
        pick_hid = ones_where(r == (c & 63))
        r, c = iota((256, 128), 0), iota((256, 128), 1)
        place_one = ones_where((r & 63) == c)
        place_bias = ones_where(c == 96)
        r, c = iota((128, 128), 0), iota((128, 128), 1)
        place_two = ones_where((r & 31) + 64 == c)
        value = dot_full(pick_in, dot_full(one, place_one))
        value = value + dot_full(pick_hid, dot_full(two, place_two))
        value = value + dot_full(pick_hid * row, place_bias)
        packed[layer * 64 : (layer + 1) * 64, :] = value

    alive = iota((E, 128), 0) < live_ref[0]
    for n in range(16):
        field[:, n * 128 : (n + 1) * 128] = jnp.where(alive, tile(state_ref, n), 0.0)
    traces(field, keep_traces(0))
    sent[0] = dot(sel[...], trace_h[...]) + dot(sel[...], trace_l[...])
    pl.semaphore_wait(barrier, len(partners))
    copies = exchange(0, 1)

    for f in range(6):
        rows = slice(f * E, (f + 1) * E)
        raw[rows, 0:FACES] = ones_where(6 * iota((E, FACES), 0) + f == iota((E, FACES), 1))
    order = raw[:, 0:FACES].astype(BF16)
    near = jnp.concatenate(
        [ones_where(6 * iota((E, FACES), 0) + f == src_ref[...], BF16) for f in range(6)], axis=0
    )
    far = ones_where(iota((SLOTS, FACES), 0) + FACES == src_ref[...], BF16)
    loc_t[...] = dot_nt(near, order).astype(BF16)
    loc[...] = dot_nt(order, near).astype(BF16)
    rem_t[...] = dot_nt(far, order).astype(BF16)
    rem[...] = dot_nt(order, far).astype(BF16)
    turn = orient_ref[...]
    flags = [(turn >> 1) & 1, (turn ^ (turn >> 1)) & 1, (turn ^ (turn >> 2)) & 1]
    for m in range(3):
        spread = jnp.broadcast_to(flags[m], (128, FACES)).astype(F32).astype(BF16)
        masks[:, m * 128 : (m + 1) * 128] = dot_nt(order, spread)

    for layer in range(2):
        r, c = iota((256, 64), 0), iota((256, 64), 1)
        rows_in = ones_where(c == ((r >> 7) * 32 + (r & 31)))
        rows_hid = ones_where(c == (r & 63))
        r, c = iota((64, 256), 0), iota((64, 256), 1)
        cols_hid = ones_where(r == (c & 63))
        r, c = iota((32, 128), 0), iota((32, 128), 1)
        cols_ch = ones_where(r == (c & 31))
        r, c = iota((128, 32), 0), iota((128, 32), 1)
        rows_ch = ones_where(c == (r & 31))
        r, c = iota((256, 256), 0), iota((256, 256), 1)
        big = dot_full(dot_full(rows_in, w1_ref[layer]), cols_hid)
        w1h[layer], w1l[layer] = split(jnp.where(((r >> 5) & 3) == (c >> 6), big, 0.0))
        r, c = iota((256, 128), 0), iota((256, 128), 1)
        big = dot_full(dot_full(rows_hid, w2_ref[layer]), cols_ch)
        w2h[layer], w2l[layer] = split(jnp.where((r >> 6) == (c >> 5), big, 0.0))
        r, c = iota((128, 128), 0), iota((128, 128), 1)
        same = (r >> 5) == (c >> 5)
        for axis in range(3):
            big = dot_full(dot_full(rows_ch, vol_ref[layer, axis]), cols_ch)
            big = jnp.where(same, big, 0.0) if axis < 2 else big * deriv_ref[...]
            cols = slice(axis * 128, (axis + 1) * 128)
            vh[layer, :, cols], vl[layer, :, cols] = split(big)
            vth[layer, :, cols], vtl[layer, :, cols] = split(big.T)
        bias[layer] = dot_full(jnp.broadcast_to(b1_ref[layer : layer + 1, :], (8, 64)), cols_hid)

    def gather_near():
        raw[...] = dot(loc[...], trace_h[...]) + dot(loc[...], trace_l[...])

    def gather_far(which):
        high, low = split(got[which])
        raw[...] += dot(rem[...], high) + dot(rem[...], low)

    gather_near()
    volume_of(field, 0, False)
    for copy in copies:
        copy.wait()
    gather_far(0)
    orient_rows(0)
    hidden_of(0, True)
    for n in range(16):
        cols = slice(n * 128, (n + 1) * 128)
        field[:, cols] += STEP_SIZE * (lift(flux, n // 4, n % 4) - volume[:, cols])

    traces(field, keep_traces(1))
    sent[1] = dot(sel[...], trace_h[...]) + dot(sel[...], trace_l[...])
    copies = exchange(1, 1)
    gather_near()
    traces(cot_ref, keep_gflux)
    volume_of(cot_ref, 1, True)
    for copy in copies:
        copy.wait()
    gather_far(1)
    orient_rows(1)
    hidden_of(1, False)

    def backward(layer, which, beside):
        flux_back(layer)
        turn_back_rows()
        sent[which] = dot(rem_t[...], turn_h[...]) + dot(rem_t[...], turn_l[...])
        copies = exchange(which, -1)
        gin[...] += dot(loc_t[...], turn_h[...]) + dot(loc_t[...], turn_l[...])
        beside()
        for copy in copies:
            copy.wait()
        high, low = split(got[which])
        gin[...] += dot(sel_t[...], high) + dot(sel_t[...], low)

    backward(1, 2, lambda: weight_grads(1))
    for n in range(16):
        cols = slice(n * 128, (n + 1) * 128)
        grad[:, cols] = tile(cot_ref, n) - STEP_SIZE * volume[:, cols] + lift(gin, n // 4, n % 4)
    traces(grad, keep_gflux)

    def reduce_grads():
        weight_grads(0)
        chunk = lambda j: pl.ds(pl.multiple_of(j * 8, 8), 8)
        stage = []
        for s in range(1, group):
            stage.append(
                pltpu.make_async_remote_copy(
                    src_ref=packed.at[chunk(lax.rem(mine + s, group))],
                    dst_ref=part.at[mine],
                    send_sem=ar_send.at[0, s],
                    recv_sem=ar_recv.at[0, s],
                    device_id=(in_group(s),),
                    device_id_type=MESH,
                )
            )
        for copy in stage:
            copy.start()
        part[mine] = packed[chunk(mine), :]
        volume_of(grad, 0, True)
        for copy in stage:
            copy.wait()
        value = part[0]
        for s in range(1, group):
            value = value + part[s]
        part_sum[rank] = value
        stage = []
        for s in range(1, others):
            stage.append(
                pltpu.make_async_remote_copy(
                    src_ref=part_sum.at[rank],
                    dst_ref=part_sum.at[rank],
                    send_sem=ar_send.at[1, s],
                    recv_sem=ar_recv.at[1, s],
                    device_id=(across(s),),
                    device_id_type=MESH,
                )
            )
        for copy in stage:
            copy.start()
        for copy in stage:
            copy.wait()
        value = part_sum[0]
        for s in range(1, others):
            value = value + part_sum[s]
        total[chunk(mine), :] = value
        stage = []
        for s in range(1, group):
            stage.append(
                pltpu.make_async_remote_copy(
                    src_ref=total.at[chunk(mine)],
                    dst_ref=total.at[chunk(mine)],
                    send_sem=ar_send.at[2, s],
                    recv_sem=ar_recv.at[2, s],
                    device_id=(in_group(s),),
                    device_id_type=MESH,
                )
            )
        for copy in stage:
            copy.start()
        for copy in stage:
            copy.wait()

    backward(0, 3, reduce_grads)
    for n in range(16):
        cols = slice(n * 128, (n + 1) * 128)
        value = grad[:, cols] - STEP_SIZE * volume[:, cols] + lift(gin, n // 4, n % 4)
        out_ref[:, cols] = jnp.where(alive, value, 0.0)
    factor = (2.0 * FACES * 8 * count) ** -0.5
    for layer in range(2):
        value = total[layer * 64 : (layer + 1) * 64, :] * factor
        out_w1[layer] = value[:, 0:64]
        out_w2[layer] = pltpu.roll(value, 64, 1)[:, 0:32]
        column = pltpu.roll(value, 32, 1)[:, 0:1]
        square = iota((64, 64), 0) == iota((64, 64), 1)
        out_b1[layer : layer + 1, :] = jnp.sum(jnp.where(square, column, 0.0), axis=0, keepdims=True)


def local(count, state, cotangent, elem_count, face_src, face_orient, send_face, vol_weight, w1, b1, w2):
    constant = np.zeros((128, 128), np.float32)
    for a in range(4):
        for k in range(4):
            constant[32 * k : 32 * k + 32, 32 * a : 32 * a + 32] = DERIV[a, k]
    vmem = pl.BlockSpec(memory_space=pltpu.VMEM)
    smem = pl.BlockSpec(memory_space=pltpu.SMEM)
    V = pltpu.VMEM
    scratch = [
        V((E, 2048), F32), V((E, 2048), F32), V((E, 2048), F32),
        V((16 * E, 384), F32), V((16 * E, 128), BF16), V((16 * E, 128), BF16),
        V((FACES, 512), BF16), V((FACES, 512), BF16), V((FACES, 512), F32),
        V((2, 4, FACES, 256), BF16), V((2, 4, FACES, 256), BF16), V((2, 4, FACES, 256), F32),
        V((FACES, 512), F32), V((FACES, 512), BF16), V((FACES, 512), BF16),
        V((4, FACES, 256), BF16), V((4, FACES, 256), BF16),
        V((FACES, 512), F32), V((FACES, 512), F32), V((FACES, 512), BF16), V((FACES, 512), BF16),
        V((SLOTS, FACES), BF16), V((FACES, SLOTS), BF16),
        V((FACES, FACES), BF16), V((FACES, SLOTS), BF16), V((FACES, FACES), BF16), V((SLOTS, FACES), BF16),
        V((FACES, 384), F32),
        V((2, 256, 256), BF16), V((2, 256, 256), BF16), V((2, 256, 128), BF16), V((2, 256, 128), BF16),
        V((2, 128, 384), BF16), V((2, 128, 384), BF16), V((2, 128, 384), BF16), V((2, 128, 384), BF16),
        V((2, 8, 256), F32),
        V((4, SLOTS, 512), F32), V((4, SLOTS, 512), F32),
        V((128, 128), F32), V((16, 8, 128), F32), V((count // 16, 8, 128), F32), V((128, 128), F32),
        pltpu.SemaphoreType.DMA((4, BLOCKS)), pltpu.SemaphoreType.DMA((4, BLOCKS)),
        pltpu.SemaphoreType.DMA((3, 16)), pltpu.SemaphoreType.DMA((3, 16)),
    ]
    return pl.pallas_call(
        functools.partial(kernel, count),
        out_shape=(
            jax.ShapeDtypeStruct(state.shape, F32),
            jax.ShapeDtypeStruct(w1.shape, F32),
            jax.ShapeDtypeStruct(b1.shape, F32),
            jax.ShapeDtypeStruct(w2.shape, F32),
        ),
        in_specs=[vmem, vmem, smem] + [vmem] * 8,
        out_specs=[vmem] * 4,
        scratch_shapes=scratch,
        compiler_params=pltpu.CompilerParams(
            collective_id=0, has_side_effects=True, vmem_limit_bytes=40 * 1024 * 1024
        ),
    )(
        state, cotangent, elem_count, face_src.reshape(1, -1), face_orient.reshape(1, -1),
        send_face.reshape(1, -1), vol_weight, w1, b1, w2, jnp.asarray(constant),
    )


def solution(mesh):
    rows, flat, whole = P("dom", None), P("dom"), P()
    return jax.shard_map(
        functools.partial(local, mesh.shape["dom"]),
        mesh=mesh,
        in_specs=(rows, rows, flat, flat, flat, flat, whole, whole, whole, whole),
        out_specs=(rows, whole, whole, whole),
        check_vma=False,
    )
```

```python
import functools
import types

import jax
import jax.numpy as jnp
import numpy as np
from jax import lax
from jax.experimental import pallas as pl
from jax.experimental.pallas import tpu as pltpu
from jax.sharding import PartitionSpec as P

MESH = pl.DeviceIdType.MESH
HIGHEST = lax.Precision.HIGHEST
F32 = jnp.float32
BF16 = jnp.bfloat16
I32 = jnp.int32
NEIGH = 4
BLOCKS = 2 * NEIGH
CAP = 32
SLOTS = BLOCKS * CAP
STEP_SIZE = 0.25
E = 48
FACES = 6 * E
OFFSETS = [level + 1 for level in range(NEIGH)] + [-(level + 1) for level in range(NEIGH)]


VMEM_LIMIT = 56 * 1024 * 1024


def deriv_matrix():
    points = np.array([-1.0, -np.sqrt(0.2), np.sqrt(0.2), 1.0])
    weights = np.array(
        [np.prod([points[r] - points[o] for o in range(4) if o != r]) for r in range(4)]
    )
    matrix = np.zeros((4, 4))
    for r in range(4):
        for c in range(4):
            if r != c:
                matrix[r, c] = weights[r] / weights[c] / (points[r] - points[c])
        matrix[r, r] = -np.sum(matrix[r])
    return matrix


DERIV = deriv_matrix()


def iota(shape, dim):
    return lax.broadcasted_iota(I32, shape, dim)


def dot(a, b):
    return jnp.dot(a, b, preferred_element_type=F32)


def dot_nt(a, b):
    return lax.dot_general(a, b, (((1,), (1,)), ((), ())), preferred_element_type=F32)


def dot_tn(a, b):
    return lax.dot_general(a, b, (((0,), (0,)), ((), ())), preferred_element_type=F32)


def dot_full(a, b):
    return jnp.dot(a, b, preferred_element_type=F32, precision=HIGHEST)


def split(x):
    high = x.astype(BF16)
    return high, (x - high.astype(F32)).astype(BF16)


def three(op, a, b):
    return op(a[0], b[0]) + op(a[1], b[0]) + op(a[0], b[1])


def lanes(a):
    return pl.ds(pl.multiple_of(a * 128, 128), 128)


def ones_where(match, dtype=F32):
    return jnp.where(match, 1.0, 0.0).astype(dtype)


MASKS = 4

INPUTS = ("state", "cot", "live", "src", "orient", "send", "vol", "w1", "b1", "w2t", "deriv")
OUTPUTS = ("out", "total")
SCRATCH = dict(
    src_v=((FACES,), I32), orient_v=((FACES,), I32), send_v=((1, SLOTS), I32), state_v=((E, 2048), F32), cot_v=((E, 2048), F32),
    vol_v=((2, 3, 32, 32), F32), w1_v=((2, 64, 64), F32), b1_v=((2, 64), F32), w2t_v=((2, 32, 64), F32), deriv_v=((128, 128), F32),
    out_v=((E, 2048), F32), field=((E, 2048), F32), grad=((E, 2048), F32), volume=((E, 2048), F32),
    vol_y=((16 * E, 384), F32), vol_x=((16 * E, 256), BF16),
    trace=((FACES, 1024), BF16), raw=((FACES, 512), F32),
    pair_nh=((2, FACES, 1024), BF16), pair_nl=((2, FACES, 1024), BF16), pair_fh=((2, SLOTS, 1024), BF16), pair_fl=((2, SLOTS, 1024), BF16),
    hid_nh=((2, FACES, 1024), BF16), hid_nl=((2, FACES, 1024), BF16), hid_fh=((2, SLOTS, 1024), BF16), hid_fl=((2, SLOTS, 1024), BF16),
    flux=((FACES, 512), F32), flux_fh=((SLOTS, 512), BF16), flux_fl=((SLOTS, 512), BF16),
    gflux=((FACES, 1024), BF16), gflux_n=((FACES, 1024), BF16), gflux_f=((SLOTS, 1024), BF16), ghid_f=((SLOTS, 1024), F32),
    gpre_nh=((FACES, 1024), BF16), gpre_nl=((FACES, 1024), BF16), gpre_fh=((SLOTS, 1024), BF16), gpre_fl=((SLOTS, 1024), BF16),
    gin=((FACES, 512), F32), gin_fh=((SLOTS, 512), BF16), gin_fl=((SLOTS, 512), BF16), gout=((FACES, 512), F32),
    turn=((FACES, 1024), BF16),
    sel=((SLOTS, FACES), BF16), sel_t=((FACES, SLOTS), BF16), loc=((FACES, FACES), BF16), loc_t=((FACES, FACES), BF16),
    rem=((FACES, SLOTS), BF16), rem_t=((SLOTS, FACES), BF16),
    masks_n=((FACES, MASKS * 128), F32), masks_f=((SLOTS, MASKS * 128), F32),
    w1h=((2, 256, 256), BF16), w1l=((2, 256, 256), BF16), w1th=((2, 256, 256), BF16), w1tl=((2, 256, 256), BF16),
    w2c=((2, 256, 256), BF16), w2ts=((2, 256, 256), BF16), w2tl=((2, 128, 256), BF16),
    vs=((2, 256, 384), BF16), vl=((2, 128, 384), BF16), vts=((2, 256, 384), BF16), vtl=((2, 128, 384), BF16), bias=((2, 8, 256), F32),
    sent=((4, SLOTS, 512), F32), got=((4, SLOTS, 512), F32),
    one=((256, 256), F32), two=((256, 128), F32), row=((8, 256), F32),
    packed=((2, 64, 128), F32), part=((2, 8, 8, 128), F32),
)


def kernel(count, names, *refs):
    s = types.SimpleNamespace(**dict(zip(names, refs, strict=True)))
    me = lax.axis_index("dom")
    group = 8
    others = count // group
    base = (me // group) * group
    mine = lax.rem(me, group)
    rank = me // group

    def neighbour(offset):
        return lax.rem(me + offset + count, count)

    def in_group(step):
        return base + lax.rem(mine + step, group)

    def across(step):
        return lax.rem(rank + step, others) * group + mine

    barrier = pltpu.get_barrier_semaphore()
    partners = [neighbour(o) for o in OFFSETS]
    partners += [in_group(step) for step in range(1, group)]
    partners += [across(step) for step in range(1, others)]
    for device in partners:
        pl.semaphore_signal(barrier, inc=1, device_id=(device,), device_id_type=MESH)

    pulls = {}
    for n, name in enumerate(("send", "state", "live", "src", "orient", "vol", "w1", "b1", "w2t", "deriv", "cot")):
        pulls[name] = pltpu.make_async_copy(getattr(s, name), getattr(s, name + "_v"), s.in_sem.at[n])
        pulls[name].start()

    def far_copy(which, pair, side, sign):
        rows = pl.ds(pl.multiple_of(64 * pair + CAP * side, CAP), CAP)
        offset = (pair + 1) * (sign if side == 0 else -sign)
        return pltpu.make_async_remote_copy(
            src_ref=s.sent.at[which, rows],
            dst_ref=s.got.at[which, rows],
            send_sem=s.send_sem.at[which, 2 * pair + side],
            recv_sem=s.recv_sem.at[which, 2 * pair + side],
            device_id=(neighbour(offset),),
            device_id_type=MESH,
        )

    def send_all(which, sign):
        for pair in (3, 2, 1, 0):
            for side in range(2):
                far_copy(which, pair, side, sign).start()

    def wait_all(which, sign):
        for pair in (3, 2, 1, 0):
            for side in range(2):
                far_copy(which, pair, side, sign).wait_recv()

    def wait_sent(which, sign):
        for pair in (3, 2, 1, 0):
            for side in range(2):
                far_copy(which, pair, side, sign).wait_send()

    def tile(ref, n):
        return ref[:, n * 128 : (n + 1) * 128]

    def wide(a):
        return slice(256 * a, 256 * a + 256)

    def high(a):
        return slice(256 * a, 256 * a + 128)

    def low(a):
        return slice(256 * a + 128, 256 * a + 256)

    def narrow(a):
        return slice(128 * a, 128 * a + 128)

    group_of_lane = iota((E, 128), 1) >> 5

    def traces(ref, emit):
        for a in range(4):
            emit(0, a, tile(ref, a))
            emit(1, a, tile(ref, 12 + a))
            emit(2, a, tile(ref, 4 * a))
            emit(3, a, tile(ref, 4 * a + 3))
            first = tile(ref, 4 * a)
            last = pltpu.roll(tile(ref, 4 * a), 32, 1)
            for b in range(1, 4):
                node = tile(ref, 4 * a + b)
                first = jnp.where(group_of_lane == b, pltpu.roll(node, 32 * b, 1), first)
                moved = node if b == 3 else pltpu.roll(node, 32 * (b + 1), 1)
                last = jnp.where(group_of_lane == b, moved, last)
            emit(4, a, first)
            emit(5, a, last)

    def lift(ref, i, j):
        at = lambda f, a: ref[f * E : (f + 1) * E, narrow(a)]
        first, last = at(4, i), at(5, i)
        first = pltpu.roll(first, (128 - 32 * j) % 128, 1) if j else first
        last = pltpu.roll(last, 96 - 32 * j, 1) if j < 3 else last
        value = jnp.where(group_of_lane == 0, first, jnp.where(group_of_lane == 3, last, 0.0))
        if i == 0:
            value = value + at(0, j)
        if i == 3:
            value = value + at(1, j)
        if j == 0:
            value = value + at(2, i)
        if j == 3:
            value = value + at(3, i)
        return value

    def keep_traces(layer):
        def emit(f, a, value):
            h, l = split(value)
            rows = slice(f * E, (f + 1) * E)
            s.trace[rows, narrow(a)] = h
            s.trace[rows, slice(512 + 128 * a, 640 + 128 * a)] = l
            s.pair_nh[layer, rows, high(a)] = h
            s.pair_nl[layer, rows, high(a)] = l

        return emit

    def keep_gflux(masked):
        def emit(f, a, value):
            h, l = split(STEP_SIZE * value)
            rows = slice(f * E, (f + 1) * E)
            s.gflux[rows, high(a)] = h
            s.gflux[rows, low(a)] = l
            if masked:
                here = s.masks_n[rows, 384:512].astype(BF16)
                s.gflux_n[rows, high(a)] = h * here
                s.gflux_n[rows, low(a)] = l * here

        return emit

    def gathered(matrix, ref):
        both = dot(matrix[...], ref[...])
        return both[:, 0:512] + both[:, 512:1024]

    def volume_of(ref, layer, adjoint):
        for n in range(16):
            h, l = split(tile(ref, n))
            s.vol_x[n * E : (n + 1) * E, 0:128] = h
            s.vol_x[n * E : (n + 1) * E, 128:256] = l
        stacked, rest = (s.vts, s.vtl) if adjoint else (s.vs, s.vl)
        s.vol_y[...] = dot(s.vol_x[...], stacked[layer]) + dot(s.vol_x[:, 0:128], rest[layer])
        deriv = DERIV.T if adjoint else DERIV
        for i in range(4):
            for j in range(4):
                n = 4 * i + j
                value = s.vol_y[n * E : (n + 1) * E, 256:384]
                for o in range(4):
                    if abs(deriv[i, o]) > 1e-12:
                        at = 4 * o + j
                        value = value + float(deriv[i, o]) * s.vol_y[at * E : (at + 1) * E, 0:128]
                    if abs(deriv[j, o]) > 1e-12:
                        at = 4 * i + o
                        value = value + float(deriv[j, o]) * s.vol_y[at * E : (at + 1) * E, 128:256]
                s.volume[:, narrow(n)] = value

    def flip_lanes(x, odd):
        return jnp.where(odd, pltpu.roll(x, 96, 1), pltpu.roll(x, 32, 1))

    def swap(x, odd, upper):
        stage = [None] * 4
        for a in (0, 2):
            stage[a] = jnp.where(odd, pltpu.roll(x[a + 1], 32, 1), x[a])
            stage[a + 1] = jnp.where(odd, x[a + 1], pltpu.roll(x[a], 96, 1))
        out = [None] * 4
        for a in (0, 1):
            out[a] = jnp.where(upper, pltpu.roll(stage[a + 2], 64, 1), stage[a])
            out[a + 2] = jnp.where(upper, stage[a + 2], pltpu.roll(stage[a], 64, 1))
        return out

    def lane_masks(count_):
        groups = iota((count_, 128), 1) >> 5
        return (groups & 1) == 1, groups >= 2

    def oriented(x, marks):
        odd, upper = lane_masks(x[0].shape[0])
        first, second, swapped = marks
        x = [jnp.where(first, x[3 - a], x[a]) for a in range(4)]
        x = [jnp.where(second, flip_lanes(v, odd), v) for v in x]
        y = swap(x, odd, upper)
        return [jnp.where(swapped, y[a], x[a]) for a in range(4)]

    def turned_back(x, marks):
        odd, upper = lane_masks(x[0].shape[0])
        first, second, swapped = marks
        y = swap(x, odd, upper)
        x = [jnp.where(swapped, y[a], x[a]) for a in range(4)]
        x = [jnp.where(second, flip_lanes(v, odd), v) for v in x]
        return [jnp.where(first, x[3 - a], x[a]) for a in range(4)]

    def marks_of(ref, rows):
        return [ref[rows, narrow(m)] > 0.5 for m in range(3)]

    def each_rows(body):
        body(slice(0, FACES))

    def orient_near(layer):
        def body(rows):
            x = oriented([s.raw[rows, narrow(a)] for a in range(4)], marks_of(s.masks_n, rows))
            for a in range(4):
                s.pair_nh[layer, rows, low(a)], s.pair_nl[layer, rows, low(a)] = split(x[a])

        each_rows(body)

    def turn_back_near():
        def body(rows):
            x = turned_back([s.gout[rows, narrow(a)] for a in range(4)], marks_of(s.masks_n, rows))
            for a in range(4):
                h, l = split(x[a])
                s.turn[rows, narrow(a)] = h
                s.turn[rows, slice(512 + 128 * a, 640 + 128 * a)] = l

        each_rows(body)

    def each_a(body):
        for a in range(4):
            body(wide(a), high(a), narrow(a))

    def hidden(xh, xl, layer):
        pre = dot(xh, s.w1h[layer]) + dot(xl, s.w1h[layer]) + dot(xh, s.w1l[layer])
        return jnp.tanh(pre + s.bias[layer, 0:1, :])

    def flux_of(h, l, layer):
        both = dot(h, s.w2c[layer])
        return both[:, 0:128] + both[:, 128:256] + dot(l, s.w2c[layer, :, 0:128])

    def hidden_grad(both, top, layer):
        return dot(both, s.w2ts[layer]) + dot(top, s.w2tl[layer])

    def pair_grad(h, l, layer):
        return dot(h, s.w1th[layer]) + dot(l, s.w1th[layer]) + dot(h, s.w1tl[layer])

    def hidden_near(layer):
        def body(w, h_, n):
            h, l = split(hidden(s.pair_nh[layer, :, w], s.pair_nl[layer, :, w], layer))
            s.hid_nh[layer, :, w] = h
            s.hid_nl[layer, :, w] = l
            if layer == 0:
                s.flux[:, n] = flux_of(h, l, layer) * s.masks_n[:, 384:512]

        each_a(body)

    def back_near(layer, gflux):
        def body(w, h_, n):
            h = s.hid_nh[layer, :, w].astype(F32) + s.hid_nl[layer, :, w].astype(F32)
            gp = hidden_grad(gflux[:, w], gflux[:, h_], layer) * (1.0 - h * h)
            gh, gl = split(gp)
            s.gpre_nh[:, w] = gh
            s.gpre_nl[:, w] = gl
            both = pair_grad(gh, gl, layer)
            s.gin[:, n] = both[:, 0:128]
            s.gout[:, n] = both[:, 128:256]

        each_a(body)

    def far_pairs(which, layer):
        def step(n, carry):
            pair = 3 - n
            rows = pl.ds(pl.multiple_of(64 * pair, 64), 64)
            for side in range(2):
                far_copy(which, pair, side, 1).wait_recv()
            for side in range(2):
                part_rows = pl.ds(pl.multiple_of(64 * pair + CAP * side, CAP), CAP)
                x = oriented([s.got[which, part_rows, narrow(a)] for a in range(4)], marks_of(s.masks_f, part_rows))
                for a in range(4):
                    s.pair_fh[layer, part_rows, low(a)], s.pair_fl[layer, part_rows, low(a)] = split(x[a])
            stack = lambda ref, cut: jnp.concatenate([ref[rows, cut(a)] for a in range(4)], axis=0)
            value = hidden(stack(s.pair_fh.at[layer], wide), stack(s.pair_fl.at[layer], wide), layer)
            h, l = split(value)
            part_of = lambda v, a: v[64 * a : 64 * a + 64]
            for a in range(4):
                s.hid_fh[layer, rows, wide(a)] = part_of(h, a)
                s.hid_fl[layer, rows, wide(a)] = part_of(l, a)
            if layer == 0:
                fh, fl = split(flux_of(h, l, layer))
                for a in range(4):
                    s.flux_fh[rows, narrow(a)] = part_of(fh, a)
                    s.flux_fl[rows, narrow(a)] = part_of(fl, a)
            else:
                gh, gl = split(stack(s.ghid_f, wide) * (1.0 - value * value))
                both = pair_grad(gh, gl, layer)
                ih, il = split(both[:, 0:128])
                for a in range(4):
                    s.gpre_fh[rows, wide(a)] = part_of(gh, a)
                    s.gpre_fl[rows, wide(a)] = part_of(gl, a)
                    s.gin_fh[rows, narrow(a)] = part_of(ih, a)
                    s.gin_fl[rows, narrow(a)] = part_of(il, a)
                for side in range(2):
                    part_rows = pl.ds(pl.multiple_of(64 * pair + CAP * side, CAP), CAP)
                    cut = lambda a: both[64 * a + CAP * side : 64 * a + CAP * side + CAP, 128:256]
                    x = turned_back([cut(a) for a in range(4)], marks_of(s.masks_f, part_rows))
                    for a in range(4):
                        s.sent[which + 1, part_rows, narrow(a)] = x[a]
                for side in range(2):
                    far_copy(which + 1, pair, side, -1).start()
            return carry

        lax.fori_loop(0, 4, step, 0)

    def far_inner(layer):
        both = dot(s.rem_t[...], s.trace[...]).astype(BF16)
        for a in range(4):
            s.pair_fh[layer, :, high(a)] = both[:, narrow(a)]
            s.pair_fl[layer, :, high(a)] = both[:, 512 + 128 * a : 640 + 128 * a]

    def weight_grads(parts):
        rows_of = lambda ref, cut: jnp.concatenate([ref[:, cut(a)] for a in range(4)], axis=0)
        xh, xl, gph, gpl, hh, hl, g = parts
        gh, gl, x = rows_of(gph, wide), rows_of(gpl, wide), rows_of(xh, wide)
        one = dot_tn(x, gh) + dot_tn(rows_of(xl, wide), gh) + dot_tn(x, gl)
        two = dot_tn(rows_of(hh, wide), rows_of(g, wide))
        top = dot_tn(rows_of(hl, wide), rows_of(g, high))
        two = two[:, 0:128] + two[:, 128:256] + top
        row = jnp.sum(gh.astype(F32) + gl.astype(F32), axis=0, keepdims=True)
        return one, two, row

    def pack_grads(layer, one, two, row):
        r, c = iota((256, 256), 0), iota((256, 256), 1)
        one = jnp.where(((r >> 5) & 3) == (c >> 6), one, 0.0)
        one = one[:, 0:128] + one[:, 128:256]
        one = one + pltpu.roll(one, 64, 1)
        halves = [sum(one[128 * half + 32 * b : 128 * half + 32 * b + 32] for b in range(4)) for half in range(2)]
        one = jnp.concatenate(halves, axis=0)
        r, c = iota((256, 128), 0), iota((256, 128), 1)
        two = jnp.where((r >> 6) == (c >> 5), two, 0.0)
        two = sum(two[64 * b : 64 * b + 64] for b in range(4))
        two = two + pltpu.roll(two, 64, 1)
        two = two + pltpu.roll(two, 32, 1)
        row = row[:, 0:128] + row[:, 128:256]
        row = row + pltpu.roll(row, 64, 1)
        r, c = iota((64, 128), 0), iota((64, 128), 1)
        column = jnp.sum(jnp.where(r == c, row, 0.0), axis=1, keepdims=True)
        value = jnp.where(c < 64, one, jnp.where(c < 96, two, jnp.where(c == 96, column, 0.0)))
        s.packed[layer] = value

    def piece(j):
        return pl.ds(pl.multiple_of(j * 8, 8), 8)

    def remote(src, dst, sems, device):
        return pltpu.make_async_remote_copy(
            src_ref=src, dst_ref=dst, send_sem=sems[0], recv_sem=sems[1], device_id=(device,), device_id_type=MESH
        )

    def sems(layer, stage, step):
        return s.ar_send.at[layer, stage, step], s.ar_recv.at[layer, stage, step]

    def scatter(layer):
        return [
            remote(s.packed.at[layer, piece(lax.rem(mine + t, group))], s.part.at[layer, mine], sems(layer, 0, t), in_group(t))
            for t in range(1, group)
        ]

    def spread(layer):
        here = s.part_sum.at[layer, rank]
        return [remote(here, here, sems(layer, 1, t), across(t)) for t in range(1, others)]

    def collect(layer):
        here = s.total_v.at[layer, piece(mine)]
        return [remote(here, here, sems(layer, 2, t), in_group(t)) for t in range(1, group)]

    def start(copies):
        for copy in copies:
            copy.start()

    def wait(copies):
        for copy in copies:
            copy.wait()

    def reduce_start(layer):
        start(scatter(layer))
        s.part[layer, mine] = s.packed[layer, piece(mine), :]

    def reduce_middle(layer):
        wait(scatter(layer))
        value = s.part[layer, 0]
        for t in range(1, group):
            value = value + s.part[layer, t]
        s.part_sum[layer, rank] = value
        start(spread(layer))

    def reduce_last(layer):
        wait(spread(layer))
        value = s.part_sum[layer, 0]
        for t in range(1, others):
            value = value + s.part_sum[layer, t]
        s.total_v[layer, piece(mine), :] = value
        start(collect(layer))

    with jax.named_scope("send_table"):
        order = (0, 4, 1, 5, 2, 6, 3, 7)
        pulls["send"].wait()
        row = s.send_v[...]
        row = jnp.concatenate([row[:, CAP * b : CAP * b + CAP] for b in order], axis=1)
        for f in range(6):
            s.sel_t[f * E : (f + 1) * E, :] = ones_where(6 * iota((E, SLOTS), 0) + f == row, BF16)
        eye = ones_where(iota((SLOTS, SLOTS), 0) == iota((SLOTS, SLOTS), 1), BF16)
        s.sel[...] = dot_nt(eye, s.sel_t[...]).astype(BF16)

    with jax.named_scope("field0"):
        pulls["state"].wait()
        pulls["live"].wait()
        alive = iota((E, 128), 0) < s.live_v[0]
        for n in range(16):
            s.field[:, narrow(n)] = jnp.where(alive, tile(s.state_v, n), 0.0)
        traces(s.field, keep_traces(0))
    with jax.named_scope("pack0"):
        s.sent[0] = gathered(s.sel, s.trace)
    with jax.named_scope("barrier"):
        pl.semaphore_wait(barrier, len(partners))
    send_all(0, 1)

    with jax.named_scope("tables"):
        for f in range(6):
            s.raw[f * E : (f + 1) * E, 0:FACES] = ones_where(6 * iota((E, FACES), 0) + f == iota((E, FACES), 1))
        by_kind = s.raw[:, 0:FACES].astype(BF16)
        pulls["src"].wait()
        source = s.src_v[...].reshape(1, FACES)
        near = jnp.concatenate([ones_where(6 * iota((E, FACES), 0) + f == source, BF16) for f in range(6)], axis=0)
        slot = iota((SLOTS, FACES), 0)
        slot = ((slot >> 5) & 1) * 128 + (slot >> 6) * CAP + (slot & 31)
        far = ones_where(slot + FACES == source, BF16)
        s.loc_t[...] = dot_nt(near, by_kind).astype(BF16)
        s.loc[...] = dot_nt(by_kind, near).astype(BF16)
        s.rem_t[...] = dot_nt(far, by_kind).astype(BF16)
        s.rem[...] = dot_nt(by_kind, far).astype(BF16)
        pulls["orient"].wait()
        turn = s.orient_v[...].reshape(1, FACES)
        flags = [(turn >> 1) & 1, (turn ^ (turn >> 1)) & 1, (turn ^ (turn >> 2)) & 1, jnp.where(source < FACES, 1, 0)]
        for m in range(MASKS):
            spread_out = jnp.broadcast_to(flags[m], (128, FACES)).astype(F32).astype(BF16)
            s.masks_n[:, narrow(m)] = dot_nt(by_kind, spread_out)
            s.masks_f[:, narrow(m)] = dot_nt(far, spread_out)

    def four(x):
        x = jnp.concatenate([x] * 4, axis=1)
        return jnp.concatenate([x] * 4, axis=0)

    def flux_weights(layer):
        r, c = iota((256, 256), 0), iota((256, 256), 1)
        w1 = s.w1_v[layer]
        big = jnp.concatenate([four(w1[0:32]), four(w1[32:64])], axis=0)
        big = jnp.where(((r >> 5) & 3) == (c >> 6), big, 0.0)
        s.w1h[layer], s.w1l[layer] = split(big)
        s.w1th[layer], s.w1tl[layer] = split(big.T)
        r, c = iota((128, 256), 0), iota((128, 256), 1)
        big = jnp.where((r >> 5) == (c >> 6), four(s.w2t_v[layer]), 0.0)
        h, l = split(big)
        s.w2ts[layer, 0:128] = h
        s.w2ts[layer, 128:256] = h
        s.w2tl[layer] = l
        h, l = split(big.T)
        s.w2c[layer, :, 0:128] = h
        s.w2c[layer, :, 128:256] = l
        bias = jnp.concatenate([s.b1_v[layer : layer + 1, :]] * 4, axis=1)
        s.bias[layer] = jnp.broadcast_to(bias, (8, 256))

    def volume_weights(layer):
        r, c = iota((128, 128), 0), iota((128, 128), 1)
        for axis in range(3):
            big = four(s.vol_v[layer, axis])
            big = jnp.where((r >> 5) == (c >> 5), big, 0.0) if axis < 2 else big * s.deriv_v[...]
            for value, stacked, rest in ((big, s.vs, s.vl), (big.T, s.vts, s.vtl)):
                h, l = split(value)
                stacked[layer, 0:128, narrow(axis)] = h
                stacked[layer, 128:256, narrow(axis)] = h
                rest[layer, :, narrow(axis)] = l

    with jax.named_scope("weights0"):
        for name in ("w1", "w2t", "b1", "vol", "deriv"):
            pulls[name].wait()
        flux_weights(0)
        volume_weights(0)
    with jax.named_scope("near0"):
        s.raw[...] = gathered(s.loc, s.trace)
        far_inner(0)
    with jax.named_scope("orient0"):
        orient_near(0)
    with jax.named_scope("hidden0"):
        hidden_near(0)
    with jax.named_scope("volume0"):
        volume_of(s.field, 0, False)
    with jax.named_scope("weights1"):
        flux_weights(1)
    with jax.named_scope("cotangent"):
        pulls["cot"].wait()
        traces(s.cot_v, keep_gflux(True))
    with jax.named_scope("cotangent_far"):
        s.gflux_f[...] = dot(s.rem_t[...], s.gflux[...]).astype(BF16)
        for a in range(4):
            s.ghid_f[:, wide(a)] = hidden_grad(s.gflux_f[:, wide(a)], s.gflux_f[:, high(a)], 1)
    with jax.named_scope("far0"):
        far_pairs(0, 0)
    with jax.named_scope("field1"):
        s.flux[...] += dot(s.rem[...], s.flux_fh[...]) + dot(s.rem[...], s.flux_fl[...])
        for n in range(16):
            s.field[:, narrow(n)] += STEP_SIZE * (lift(s.flux, n // 4, n % 4) - s.volume[:, narrow(n)])
        traces(s.field, keep_traces(1))
    with jax.named_scope("pack1"):
        s.sent[1] = gathered(s.sel, s.trace)
    send_all(1, 1)
    with jax.named_scope("near1"):
        s.raw[...] = gathered(s.loc, s.trace)
        far_inner(1)
    with jax.named_scope("orient1"):
        orient_near(1)
    with jax.named_scope("hidden1"):
        hidden_near(1)
    with jax.named_scope("back1"):
        back_near(1, s.gflux_n)
    with jax.named_scope("whole0"):
        for far, here in ((s.pair_fh, s.pair_nh), (s.pair_fl, s.pair_nl)):
            value = dot(s.rem[...], jnp.concatenate([far[0, :, low(a)] for a in range(4)], axis=1)).astype(BF16)
            for a in range(4):
                here[0, :, low(a)] += value[:, narrow(a)]
        for far, here in ((s.hid_fh, s.hid_nh), (s.hid_fl, s.hid_nl)):
            for a in range(4):
                own = s.masks_n[:, 384:512].astype(BF16)
                value = dot(s.rem[...], far[0, :, wide(a)]).astype(BF16)
                here[0, :, wide(a)] = here[0, :, wide(a)] * jnp.concatenate([own, own], axis=1) + value
    with jax.named_scope("weight_grads1_near"):
        parts = s.pair_nh.at[1], s.pair_nl.at[1], s.gpre_nh, s.gpre_nl, s.hid_nh.at[1], s.hid_nl.at[1], s.gflux_n
        s.one[...], s.two[...], row = weight_grads(parts)
        s.row[...] = jnp.broadcast_to(row, (8, 256))
    with jax.named_scope("far1"):
        far_pairs(1, 1)

    with jax.named_scope("turn1"):
        turn_back_near()
    with jax.named_scope("scatter1"):
        both = dot(s.loc_t[...], s.turn[...])
        value = both[:, 0:512] + both[:, 512:1024]
        s.gin[...] += value + dot(s.rem[...], s.gin_fh[...]) + dot(s.rem[...], s.gin_fl[...])
    with jax.named_scope("volume1"):
        volume_weights(1)
        volume_of(s.cot_v, 1, True)
    with jax.named_scope("weight_grads1"):
        parts = s.pair_fh.at[1], s.pair_fl.at[1], s.gpre_fh, s.gpre_fl, s.hid_fh.at[1], s.hid_fl.at[1], s.gflux_f
        one, two, row = weight_grads(parts)
        pack_grads(1, one + s.one[...], two + s.two[...], row + s.row[0:1, :])
        reduce_start(1)
    with jax.named_scope("wait2"):
        wait_all(2, -1)
    with jax.named_scope("grad1"):
        h, l = split(s.got[2])
        s.gin[...] += dot(s.sel_t[...], h) + dot(s.sel_t[...], l)
        for n in range(16):
            s.grad[:, narrow(n)] = tile(s.cot_v, n) - STEP_SIZE * s.volume[:, narrow(n)] + lift(s.gin, n // 4, n % 4)
        traces(s.grad, keep_gflux(False))
    with jax.named_scope("back0"):
        back_near(0, s.gflux)
    with jax.named_scope("weight_grads0"):
        parts = s.pair_nh.at[0], s.pair_nl.at[0], s.gpre_nh, s.gpre_nl, s.hid_nh.at[0], s.hid_nl.at[0], s.gflux
        pack_grads(0, *weight_grads(parts))
        reduce_start(0)
    with jax.named_scope("turn0"):
        turn_back_near()
    with jax.named_scope("pack3"):
        s.sent[3] = gathered(s.rem_t, s.turn)
    send_all(3, -1)
    with jax.named_scope("sum1a"):
        reduce_middle(1)
    with jax.named_scope("sum0a"):
        reduce_middle(0)
    with jax.named_scope("scatter0"):
        both = dot(s.loc_t[...], s.turn[...])
        s.gin[...] += both[:, 0:512] + both[:, 512:1024]
    with jax.named_scope("volume0b"):
        volume_of(s.grad, 0, True)
    with jax.named_scope("sum1b"):
        reduce_last(1)
    with jax.named_scope("sum0b"):
        reduce_last(0)
    with jax.named_scope("wait3"):
        wait_all(3, -1)
    with jax.named_scope("grad0"):
        h, l = split(s.got[3])
        s.gin[...] += dot(s.sel_t[...], h) + dot(s.sel_t[...], l)
        for n in range(16):
            value = s.grad[:, narrow(n)] - STEP_SIZE * s.volume[:, narrow(n)] + lift(s.gin, n // 4, n % 4)
            s.out_v[:, narrow(n)] = jnp.where(alive, value, 0.0)
        push = pltpu.make_async_copy(s.out_v, s.out, s.out_sem.at[0])
        push.start()
    with jax.named_scope("sumc"):
        wait(collect(1))
        wait(collect(0))
        push_total = pltpu.make_async_copy(s.total_v, s.total, s.out_sem.at[1])
        push_total.start()
    with jax.named_scope("sent"):
        wait_sent(0, 1)
        wait_sent(1, 1)
        wait_sent(2, -1)
        wait_sent(3, -1)
        push.wait()
        push_total.wait()


def finish(factor, total_ref, field_ref, out_ref, w1_ref, b1_ref, w2t_ref):
    out_ref[...] = field_ref[...]
    for layer in range(2):
        value = total_ref[layer] * factor
        w1_ref[layer] = value[:, 0:64]
        w2t_ref[layer] = value.T[64:96, :]
        b1_ref[layer : layer + 1, :] = value.T[96:97, :]


def local(count, state, cotangent, elem_count, face_src, face_orient, send_face, vol_weight, w1, b1, w2):
    constant = np.zeros((128, 128), np.float32)
    for a in range(4):
        for k in range(4):
            constant[32 * k : 32 * k + 32, 32 * a : 32 * a + 32] = DERIV[a, k]
    vmem = pl.BlockSpec(memory_space=pltpu.VMEM)
    smem = pl.BlockSpec(memory_space=pltpu.SMEM)
    hbm = pl.BlockSpec(memory_space=pl.ANY)
    names = [*INPUTS, *OUTPUTS, *SCRATCH]
    scratch = [pltpu.VMEM(shape, dtype) for shape, dtype in SCRATCH.values()]
    extra = dict(
        part_sum=pltpu.VMEM((2, count // 8, 8, 128), F32),
        total_v=pltpu.VMEM((2, 64, 128), F32),
        live_v=pltpu.SMEM((1,), I32),
        out_sem=pltpu.SemaphoreType.DMA((2,)),
        in_sem=pltpu.SemaphoreType.DMA((11,)),
        send_sem=pltpu.SemaphoreType.DMA((4, BLOCKS)),
        recv_sem=pltpu.SemaphoreType.DMA((4, BLOCKS)),
        ar_send=pltpu.SemaphoreType.DMA((2, 3, 16)),
        ar_recv=pltpu.SemaphoreType.DMA((2, 3, 16)),
    )
    names += list(extra)
    scratch += list(extra.values())
    field, total = pl.pallas_call(
        functools.partial(kernel, count, names),
        out_shape=(jax.ShapeDtypeStruct(state.shape, F32), jax.ShapeDtypeStruct((2, 64, 128), F32)),
        in_specs=[hbm, hbm, hbm, hbm, hbm, hbm] + [hbm] * 5,
        out_specs=[hbm] * 2,
        scratch_shapes=scratch,
        compiler_params=pltpu.CompilerParams(
            collective_id=0, has_side_effects=True, vmem_limit_bytes=VMEM_LIMIT
        ),
    )(
        state, cotangent, elem_count, face_src, face_orient,
        send_face.reshape(1, -1), vol_weight, w1, b1, jnp.swapaxes(w2, 1, 2), jnp.asarray(constant),
    )
    factor = (2.0 * FACES * 8 * count) ** -0.5
    grad, grad_w1, grad_b1, grad_w2t = pl.pallas_call(
        functools.partial(finish, factor),
        out_shape=(
            jax.ShapeDtypeStruct(state.shape, F32),
            jax.ShapeDtypeStruct(w1.shape, F32),
            jax.ShapeDtypeStruct(b1.shape, F32),
            jax.ShapeDtypeStruct((2, 32, 64), F32),
        ),
        in_specs=[vmem] * 2,
        out_specs=[vmem] * 4,
    )(total, field)
    return grad, grad_w1, grad_b1, jnp.swapaxes(grad_w2t, 1, 2)


def solution(mesh):
    rows, flat, whole = P("dom", None), P("dom"), P()
    return jax.shard_map(
        functools.partial(local, mesh.shape["dom"]),
        mesh=mesh,
        in_specs=(rows, rows, flat, flat, flat, flat, whole, whole, whole, whole),
        out_specs=(rows, whole, whole, whole),
        check_vma=False,
    )
```

```python
import functools
import types

import jax
import jax.numpy as jnp
import numpy as np
from jax import lax
from jax.experimental import pallas as pl
from jax.experimental.pallas import tpu as pltpu
from jax.sharding import PartitionSpec as P

MESH = pl.DeviceIdType.MESH
HIGHEST = lax.Precision.HIGHEST
F32 = jnp.float32
BF16 = jnp.bfloat16
I32 = jnp.int32
NEIGH = 4
BLOCKS = 2 * NEIGH
CAP = 32
SLOTS = BLOCKS * CAP
STEP_SIZE = 0.25
E = 48
FACES = 6 * E
OFFSETS = [level + 1 for level in range(NEIGH)] + [-(level + 1) for level in range(NEIGH)]


VMEM_LIMIT = 56 * 1024 * 1024


def deriv_matrix():
    points = np.array([-1.0, -np.sqrt(0.2), np.sqrt(0.2), 1.0])
    weights = np.array(
        [np.prod([points[r] - points[o] for o in range(4) if o != r]) for r in range(4)]
    )
    matrix = np.zeros((4, 4))
    for r in range(4):
        for c in range(4):
            if r != c:
                matrix[r, c] = weights[r] / weights[c] / (points[r] - points[c])
        matrix[r, r] = -np.sum(matrix[r])
    return matrix


DERIV = deriv_matrix()


def iota(shape, dim):
    return lax.broadcasted_iota(I32, shape, dim)


def dot(a, b):
    return jnp.dot(a, b, preferred_element_type=F32)


def dot_nt(a, b):
    return lax.dot_general(a, b, (((1,), (1,)), ((), ())), preferred_element_type=F32)


def dot_tn(a, b):
    return lax.dot_general(a, b, (((0,), (0,)), ((), ())), preferred_element_type=F32)


def dot_full(a, b):
    return jnp.dot(a, b, preferred_element_type=F32, precision=HIGHEST)


def split(x):
    high = x.astype(BF16)
    return high, (x - high.astype(F32)).astype(BF16)


def three(op, a, b):
    return op(a[0], b[0]) + op(a[1], b[0]) + op(a[0], b[1])


def lanes(a):
    return pl.ds(pl.multiple_of(a * 128, 128), 128)


def ones_where(match, dtype=F32):
    return jnp.where(match, 1.0, 0.0).astype(dtype)


MASKS = 4

INPUTS = ("state", "cot", "live", "src", "orient", "send", "vol", "w1", "b1", "w2t", "deriv")
OUTPUTS = ("out", "total")
SCRATCH = dict(
    src_v=((FACES,), I32), orient_v=((FACES,), I32), send_v=((1, SLOTS), I32), state_v=((E, 2048), F32), cot_v=((E, 2048), F32),
    vol_v=((2, 3, 32, 32), F32), w1_v=((2, 64, 64), F32), b1_v=((2, 64), F32), w2t_v=((2, 32, 64), F32), deriv_v=((128, 128), F32),
    out_v=((E, 2048), F32), field=((E, 2048), F32), grad=((E, 2048), F32), volume=((E, 2048), F32),
    vol_y=((16 * E, 384), F32), vol_x=((16 * E, 256), BF16),
    trace=((FACES, 1024), BF16), raw=((FACES, 512), F32),
    pair_nh=((2, FACES, 1024), BF16), pair_nl=((2, FACES, 1024), BF16), pair_fh=((2, SLOTS, 1024), BF16), pair_fl=((2, SLOTS, 1024), BF16),
    hid_nh=((2, FACES, 1024), BF16), hid_nl=((2, FACES, 1024), BF16), hid_fh=((2, SLOTS, 1024), BF16), hid_fl=((2, SLOTS, 1024), BF16),
    flux=((FACES, 512), F32), flux_fh=((SLOTS, 512), BF16), flux_fl=((SLOTS, 512), BF16),
    gflux=((FACES, 1024), BF16), gflux_n=((FACES, 1024), BF16), gflux_f=((SLOTS, 1024), BF16), ghid_f=((SLOTS, 1024), F32),
    gpre_nh=((FACES, 1024), BF16), gpre_nl=((FACES, 1024), BF16), gpre_fh=((SLOTS, 1024), BF16), gpre_fl=((SLOTS, 1024), BF16),
    gin=((FACES, 512), F32), gin_fh=((SLOTS, 512), BF16), gin_fl=((SLOTS, 512), BF16), gout=((FACES, 512), F32),
    turn=((FACES, 1024), BF16),
    sel=((SLOTS, FACES), BF16), sel_t=((FACES, SLOTS), BF16), loc=((FACES, FACES), BF16), loc_t=((FACES, FACES), BF16),
    rem=((FACES, SLOTS), BF16), rem_t=((SLOTS, FACES), BF16),
    masks_n=((FACES, MASKS * 128), F32), masks_f=((SLOTS, MASKS * 128), F32),
    w1h=((2, 256, 256), BF16), w1l=((2, 256, 256), BF16), w1th=((2, 256, 256), BF16), w1tl=((2, 256, 256), BF16),
    w2c=((2, 256, 256), BF16), w2ts=((2, 256, 256), BF16), w2tl=((2, 128, 256), BF16),
    vs=((2, 256, 384), BF16), vl=((2, 128, 384), BF16), vts=((2, 256, 384), BF16), vtl=((2, 128, 384), BF16), bias=((2, 8, 256), F32),
    sent=((4, SLOTS, 512), F32), got=((4, SLOTS, 512), F32),
    one=((256, 256), F32), two=((256, 128), F32), row=((8, 256), F32),
    packed=((2, 64, 128), F32), part=((2, 8, 8, 128), F32),
)


def kernel(count, names, *refs):
    s = types.SimpleNamespace(**dict(zip(names, refs, strict=True)))
    me = lax.axis_index("dom")
    group = 8
    others = count // group
    base = (me // group) * group
    mine = lax.rem(me, group)
    rank = me // group

    def neighbour(offset):
        return lax.rem(me + offset + count, count)

    def in_group(step):
        return base + lax.rem(mine + step, group)

    def across(step):
        return lax.rem(rank + step, others) * group + mine

    barrier = pltpu.get_barrier_semaphore()
    partners = [neighbour(o) for o in OFFSETS]
    partners += [in_group(step) for step in range(1, group)]
    partners += [across(step) for step in range(1, others)]
    for device in partners:
        pl.semaphore_signal(barrier, inc=1, device_id=(device,), device_id_type=MESH)

    pulls = {}
    for n, name in enumerate(("send", "state", "live", "src", "orient", "vol", "w1", "b1", "w2t", "deriv", "cot")):
        pulls[name] = pltpu.make_async_copy(getattr(s, name), getattr(s, name + "_v"), s.in_sem.at[n])
        pulls[name].start()

    def far_copy(which, pair, side, sign):
        rows = pl.ds(pl.multiple_of(64 * pair + CAP * side, CAP), CAP)
        offset = (pair + 1) * (sign if side == 0 else -sign)
        return pltpu.make_async_remote_copy(
            src_ref=s.sent.at[which, rows],
            dst_ref=s.got.at[which, rows],
            send_sem=s.send_sem.at[which],
            recv_sem=s.near_sem.at[which, pair] if which < 2 else s.back_sem.at[which - 2],
            device_id=(neighbour(offset),),
            device_id_type=MESH,
        )

    def send_all(which, sign):
        for pair in (3, 2, 1, 0):
            for side in range(2):
                far_copy(which, pair, side, sign).start()

    def all_of(which, pair=None):
        rows = pl.ds(0, SLOTS) if pair is None else pl.ds(pl.multiple_of(64 * pair, 64), 64)
        return pltpu.make_async_remote_copy(
            src_ref=s.sent.at[which, rows],
            dst_ref=s.got.at[which, rows],
            send_sem=s.send_sem.at[which],
            recv_sem=s.near_sem.at[which, pair] if which < 2 else s.back_sem.at[which - 2],
            device_id=(neighbour(1),),
            device_id_type=MESH,
        )

    def tile(ref, n):
        return ref[:, n * 128 : (n + 1) * 128]

    def wide(a):
        return slice(256 * a, 256 * a + 256)

    def high(a):
        return slice(256 * a, 256 * a + 128)

    def low(a):
        return slice(256 * a + 128, 256 * a + 256)

    def narrow(a):
        return slice(128 * a, 128 * a + 128)

    group_of_lane = iota((E, 128), 1) >> 5

    def traces(ref, emit):
        for a in range(4):
            emit(0, a, tile(ref, a))
            emit(1, a, tile(ref, 12 + a))
            emit(2, a, tile(ref, 4 * a))
            emit(3, a, tile(ref, 4 * a + 3))
            first = tile(ref, 4 * a)
            last = pltpu.roll(tile(ref, 4 * a), 32, 1)
            for b in range(1, 4):
                node = tile(ref, 4 * a + b)
                first = jnp.where(group_of_lane == b, pltpu.roll(node, 32 * b, 1), first)
                moved = node if b == 3 else pltpu.roll(node, 32 * (b + 1), 1)
                last = jnp.where(group_of_lane == b, moved, last)
            emit(4, a, first)
            emit(5, a, last)

    def lift(ref, i, j):
        at = lambda f, a: ref[f * E : (f + 1) * E, narrow(a)]
        first, last = at(4, i), at(5, i)
        first = pltpu.roll(first, (128 - 32 * j) % 128, 1) if j else first
        last = pltpu.roll(last, 96 - 32 * j, 1) if j < 3 else last
        value = jnp.where(group_of_lane == 0, first, jnp.where(group_of_lane == 3, last, 0.0))
        if i == 0:
            value = value + at(0, j)
        if i == 3:
            value = value + at(1, j)
        if j == 0:
            value = value + at(2, i)
        if j == 3:
            value = value + at(3, i)
        return value

    def keep_traces(layer):
        def emit(f, a, value):
            h, l = split(value)
            rows = slice(f * E, (f + 1) * E)
            s.trace[rows, narrow(a)] = h
            s.trace[rows, slice(512 + 128 * a, 640 + 128 * a)] = l
            s.pair_nh[layer, rows, high(a)] = h
            s.pair_nl[layer, rows, high(a)] = l

        return emit

    def keep_gflux(masked):
        def emit(f, a, value):
            h, l = split(STEP_SIZE * value)
            rows = slice(f * E, (f + 1) * E)
            s.gflux[rows, high(a)] = h
            s.gflux[rows, low(a)] = l
            if masked:
                here = s.masks_n[rows, 384:512].astype(BF16)
                s.gflux_n[rows, high(a)] = h * here
                s.gflux_n[rows, low(a)] = l * here

        return emit

    def gathered(matrix, ref):
        both = dot(matrix[...], ref[...])
        return both[:, 0:512] + both[:, 512:1024]

    def volume_of(ref, layer, adjoint):
        for n in range(16):
            h, l = split(tile(ref, n))
            s.vol_x[n * E : (n + 1) * E, 0:128] = h
            s.vol_x[n * E : (n + 1) * E, 128:256] = l
        stacked, rest = (s.vts, s.vtl) if adjoint else (s.vs, s.vl)
        s.vol_y[...] = dot(s.vol_x[...], stacked[layer]) + dot(s.vol_x[:, 0:128], rest[layer])
        deriv = DERIV.T if adjoint else DERIV
        for i in range(4):
            for j in range(4):
                n = 4 * i + j
                value = s.vol_y[n * E : (n + 1) * E, 256:384]
                for o in range(4):
                    if abs(deriv[i, o]) > 1e-12:
                        at = 4 * o + j
                        value = value + float(deriv[i, o]) * s.vol_y[at * E : (at + 1) * E, 0:128]
                    if abs(deriv[j, o]) > 1e-12:
                        at = 4 * i + o
                        value = value + float(deriv[j, o]) * s.vol_y[at * E : (at + 1) * E, 128:256]
                s.volume[:, narrow(n)] = value

    def flip_lanes(x, odd):
        return jnp.where(odd, pltpu.roll(x, 96, 1), pltpu.roll(x, 32, 1))

    def swap(x, odd, upper):
        stage = [None] * 4
        for a in (0, 2):
            stage[a] = jnp.where(odd, pltpu.roll(x[a + 1], 32, 1), x[a])
            stage[a + 1] = jnp.where(odd, x[a + 1], pltpu.roll(x[a], 96, 1))
        out = [None] * 4
        for a in (0, 1):
            out[a] = jnp.where(upper, pltpu.roll(stage[a + 2], 64, 1), stage[a])
            out[a + 2] = jnp.where(upper, stage[a + 2], pltpu.roll(stage[a], 64, 1))
        return out

    def lane_masks(count_):
        groups = iota((count_, 128), 1) >> 5
        return (groups & 1) == 1, groups >= 2

    def oriented(x, marks):
        odd, upper = lane_masks(x[0].shape[0])
        first, second, swapped = marks
        x = [jnp.where(first, x[3 - a], x[a]) for a in range(4)]
        x = [jnp.where(second, flip_lanes(v, odd), v) for v in x]
        y = swap(x, odd, upper)
        return [jnp.where(swapped, y[a], x[a]) for a in range(4)]

    def turned_back(x, marks):
        odd, upper = lane_masks(x[0].shape[0])
        first, second, swapped = marks
        y = swap(x, odd, upper)
        x = [jnp.where(swapped, y[a], x[a]) for a in range(4)]
        x = [jnp.where(second, flip_lanes(v, odd), v) for v in x]
        return [jnp.where(first, x[3 - a], x[a]) for a in range(4)]

    def marks_of(ref, rows):
        return [ref[rows, narrow(m)] > 0.5 for m in range(3)]

    def each_rows(body):
        body(slice(0, FACES))

    def orient_near(layer):
        def body(rows):
            x = oriented([s.raw[rows, narrow(a)] for a in range(4)], marks_of(s.masks_n, rows))
            for a in range(4):
                s.pair_nh[layer, rows, low(a)], s.pair_nl[layer, rows, low(a)] = split(x[a])

        each_rows(body)

    def turn_back_near():
        def body(rows):
            x = turned_back([s.gout[rows, narrow(a)] for a in range(4)], marks_of(s.masks_n, rows))
            for a in range(4):
                h, l = split(x[a])
                s.turn[rows, narrow(a)] = h
                s.turn[rows, slice(512 + 128 * a, 640 + 128 * a)] = l

        each_rows(body)

    def each_a(body):
        for a in range(4):
            body(wide(a), high(a), narrow(a))

    def hidden(xh, xl, layer):
        pre = dot(xh, s.w1h[layer]) + dot(xl, s.w1h[layer]) + dot(xh, s.w1l[layer])
        return jnp.tanh(pre + s.bias[layer, 0:1, :])

    def flux_of(h, l, layer):
        both = dot(h, s.w2c[layer])
        return both[:, 0:128] + both[:, 128:256] + dot(l, s.w2c[layer, :, 0:128])

    def hidden_grad(both, top, layer):
        return dot(both, s.w2ts[layer]) + dot(top, s.w2tl[layer])

    def pair_grad(h, l, layer):
        return dot(h, s.w1th[layer]) + dot(l, s.w1th[layer]) + dot(h, s.w1tl[layer])

    def hidden_near(layer):
        def body(w, h_, n):
            h, l = split(hidden(s.pair_nh[layer, :, w], s.pair_nl[layer, :, w], layer))
            s.hid_nh[layer, :, w] = h
            s.hid_nl[layer, :, w] = l
            if layer == 0:
                s.flux[:, n] = flux_of(h, l, layer) * s.masks_n[:, 384:512]

        each_a(body)

    def back_near(layer, gflux):
        def body(w, h_, n):
            h = s.hid_nh[layer, :, w].astype(F32) + s.hid_nl[layer, :, w].astype(F32)
            gp = hidden_grad(gflux[:, w], gflux[:, h_], layer) * (1.0 - h * h)
            gh, gl = split(gp)
            s.gpre_nh[:, w] = gh
            s.gpre_nl[:, w] = gl
            both = pair_grad(gh, gl, layer)
            s.gin[:, n] = both[:, 0:128]
            s.gout[:, n] = both[:, 128:256]

        each_a(body)

    def far_pairs(which, layer):
        def step(n, carry):
            pair = 3 - n
            rows = pl.ds(pl.multiple_of(64 * pair, 64), 64)
            all_of(which, pair).wait_recv()
            for side in range(2):
                part_rows = pl.ds(pl.multiple_of(64 * pair + CAP * side, CAP), CAP)
                x = oriented([s.got[which, part_rows, narrow(a)] for a in range(4)], marks_of(s.masks_f, part_rows))
                for a in range(4):
                    s.pair_fh[layer, part_rows, low(a)], s.pair_fl[layer, part_rows, low(a)] = split(x[a])
            stack = lambda ref, cut: jnp.concatenate([ref[rows, cut(a)] for a in range(4)], axis=0)
            value = hidden(stack(s.pair_fh.at[layer], wide), stack(s.pair_fl.at[layer], wide), layer)
            h, l = split(value)
            part_of = lambda v, a: v[64 * a : 64 * a + 64]
            for a in range(4):
                s.hid_fh[layer, rows, wide(a)] = part_of(h, a)
                s.hid_fl[layer, rows, wide(a)] = part_of(l, a)
            if layer == 0:
                fh, fl = split(flux_of(h, l, layer))
                for a in range(4):
                    s.flux_fh[rows, narrow(a)] = part_of(fh, a)
                    s.flux_fl[rows, narrow(a)] = part_of(fl, a)
            else:
                gh, gl = split(stack(s.ghid_f, wide) * (1.0 - value * value))
                both = pair_grad(gh, gl, layer)
                ih, il = split(both[:, 0:128])
                for a in range(4):
                    s.gpre_fh[rows, wide(a)] = part_of(gh, a)
                    s.gpre_fl[rows, wide(a)] = part_of(gl, a)
                    s.gin_fh[rows, narrow(a)] = part_of(ih, a)
                    s.gin_fl[rows, narrow(a)] = part_of(il, a)
                for side in range(2):
                    part_rows = pl.ds(pl.multiple_of(64 * pair + CAP * side, CAP), CAP)
                    cut = lambda a: both[64 * a + CAP * side : 64 * a + CAP * side + CAP, 128:256]
                    x = turned_back([cut(a) for a in range(4)], marks_of(s.masks_f, part_rows))
                    for a in range(4):
                        s.sent[which + 1, part_rows, narrow(a)] = x[a]
                for side in range(2):
                    far_copy(which + 1, pair, side, -1).start()
            return carry

        lax.fori_loop(0, 4, step, 0)

    def far_inner(layer):
        both = dot(s.rem_t[...], s.trace[...]).astype(BF16)
        for a in range(4):
            s.pair_fh[layer, :, high(a)] = both[:, narrow(a)]
            s.pair_fl[layer, :, high(a)] = both[:, 512 + 128 * a : 640 + 128 * a]

    def weight_grads(parts):
        rows_of = lambda ref, cut: jnp.concatenate([ref[:, cut(a)] for a in range(4)], axis=0)
        xh, xl, gph, gpl, hh, hl, g = parts
        gh, gl, x = rows_of(gph, wide), rows_of(gpl, wide), rows_of(xh, wide)
        one = dot_tn(x, gh) + dot_tn(rows_of(xl, wide), gh) + dot_tn(x, gl)
        two = dot_tn(rows_of(hh, wide), rows_of(g, wide))
        top = dot_tn(rows_of(hl, wide), rows_of(g, high))
        two = two[:, 0:128] + two[:, 128:256] + top
        row = jnp.sum(gh.astype(F32) + gl.astype(F32), axis=0, keepdims=True)
        return one, two, row

    def pack_grads(layer, one, two, row):
        r, c = iota((256, 256), 0), iota((256, 256), 1)
        one = jnp.where(((r >> 5) & 3) == (c >> 6), one, 0.0)
        one = one[:, 0:128] + one[:, 128:256]
        one = one + pltpu.roll(one, 64, 1)
        halves = [sum(one[128 * half + 32 * b : 128 * half + 32 * b + 32] for b in range(4)) for half in range(2)]
        one = jnp.concatenate(halves, axis=0)
        r, c = iota((256, 128), 0), iota((256, 128), 1)
        two = jnp.where((r >> 6) == (c >> 5), two, 0.0)
        two = sum(two[64 * b : 64 * b + 64] for b in range(4))
        two = two + pltpu.roll(two, 64, 1)
        two = two + pltpu.roll(two, 32, 1)
        row = row[:, 0:128] + row[:, 128:256]
        row = row + pltpu.roll(row, 64, 1)
        r, c = iota((64, 128), 0), iota((64, 128), 1)
        column = jnp.sum(jnp.where(r == c, row, 0.0), axis=1, keepdims=True)
        value = jnp.where(c < 64, one, jnp.where(c < 96, two, jnp.where(c == 96, column, 0.0)))
        s.packed[layer] = value

    def piece(j):
        return pl.ds(pl.multiple_of(j * 8, 8), 8)

    def remote(src, dst, sems, device):
        return pltpu.make_async_remote_copy(
            src_ref=src, dst_ref=dst, send_sem=sems[0], recv_sem=sems[1], device_id=(device,), device_id_type=MESH
        )

    def sems(layer, stage):
        return s.ar_send.at[layer, stage], s.ar_recv.at[layer, stage]

    def scatter(layer):
        return [
            remote(s.packed.at[layer, piece(lax.rem(mine + t, group))], s.part.at[layer, mine], sems(layer, 0), in_group(t))
            for t in range(1, group)
        ]

    def spread(layer):
        here = s.part_sum.at[layer, rank]
        return [remote(here, here, sems(layer, 1), across(t)) for t in range(1, others)]

    def collect(layer):
        here = s.total_v.at[layer, piece(mine)]
        return [remote(here, here, sems(layer, 2), in_group(t)) for t in range(1, group)]

    def stage_bytes(layer, stage):
        here = (
            s.part.at[layer, pl.ds(0, group - 1)],
            s.part_sum.at[layer, pl.ds(0, others - 1)],
            s.total_v.at[layer, pl.ds(0, 8 * (group - 1))],
        )[stage]
        return remote(here, here, sems(layer, stage), in_group(1))

    def start(copies):
        for copy in copies:
            copy.start()

    def reduce_start(layer):
        start(scatter(layer))
        s.part[layer, mine] = s.packed[layer, piece(mine), :]

    def reduce_middle(layer):
        stage_bytes(layer, 0).wait()
        value = s.part[layer, 0]
        for t in range(1, group):
            value = value + s.part[layer, t]
        s.part_sum[layer, rank] = value
        start(spread(layer))

    def reduce_last(layer):
        stage_bytes(layer, 1).wait()
        value = s.part_sum[layer, 0]
        for t in range(1, others):
            value = value + s.part_sum[layer, t]
        s.total_v[layer, piece(mine), :] = value
        start(collect(layer))

    with jax.named_scope("send_table"):
        order = (0, 4, 1, 5, 2, 6, 3, 7)
        pulls["send"].wait()
        row = s.send_v[...]
        row = jnp.concatenate([row[:, CAP * b : CAP * b + CAP] for b in order], axis=1)
        for f in range(6):
            s.sel_t[f * E : (f + 1) * E, :] = ones_where(6 * iota((E, SLOTS), 0) + f == row, BF16)
        eye = ones_where(iota((SLOTS, SLOTS), 0) == iota((SLOTS, SLOTS), 1), BF16)
        s.sel[...] = dot_nt(eye, s.sel_t[...]).astype(BF16)

    with jax.named_scope("field0"):
        pulls["state"].wait()
        pulls["live"].wait()
        alive = iota((E, 128), 0) < s.live_v[0]
        for n in range(16):
            s.field[:, narrow(n)] = jnp.where(alive, tile(s.state_v, n), 0.0)
        traces(s.field, keep_traces(0))
    with jax.named_scope("pack0"):
        s.sent[0] = gathered(s.sel, s.trace)
    with jax.named_scope("barrier"):
        pl.semaphore_wait(barrier, len(partners))
    send_all(0, 1)

    with jax.named_scope("tables"):
        for f in range(6):
            s.raw[f * E : (f + 1) * E, 0:FACES] = ones_where(6 * iota((E, FACES), 0) + f == iota((E, FACES), 1))
        by_kind = s.raw[:, 0:FACES].astype(BF16)
        pulls["src"].wait()
        source = s.src_v[...].reshape(1, FACES)
        near = jnp.concatenate([ones_where(6 * iota((E, FACES), 0) + f == source, BF16) for f in range(6)], axis=0)
        slot = iota((SLOTS, FACES), 0)
        slot = ((slot >> 5) & 1) * 128 + (slot >> 6) * CAP + (slot & 31)
        far = ones_where(slot + FACES == source, BF16)
        s.loc_t[...] = dot_nt(near, by_kind).astype(BF16)
        s.loc[...] = dot_nt(by_kind, near).astype(BF16)
        s.rem_t[...] = dot_nt(far, by_kind).astype(BF16)
        s.rem[...] = dot_nt(by_kind, far).astype(BF16)
        pulls["orient"].wait()
        turn = s.orient_v[...].reshape(1, FACES)
        flags = [(turn >> 1) & 1, (turn ^ (turn >> 1)) & 1, (turn ^ (turn >> 2)) & 1, jnp.where(source < FACES, 1, 0)]
        for m in range(MASKS):
            spread_out = jnp.broadcast_to(flags[m], (128, FACES)).astype(F32).astype(BF16)
            s.masks_n[:, narrow(m)] = dot_nt(by_kind, spread_out)
            s.masks_f[:, narrow(m)] = dot_nt(far, spread_out)

    def four(x):
        x = jnp.concatenate([x] * 4, axis=1)
        return jnp.concatenate([x] * 4, axis=0)

    def flux_weights(layer):
        r, c = iota((256, 256), 0), iota((256, 256), 1)
        w1 = s.w1_v[layer]
        big = jnp.concatenate([four(w1[0:32]), four(w1[32:64])], axis=0)
        big = jnp.where(((r >> 5) & 3) == (c >> 6), big, 0.0)
        s.w1h[layer], s.w1l[layer] = split(big)
        s.w1th[layer], s.w1tl[layer] = split(big.T)
        r, c = iota((128, 256), 0), iota((128, 256), 1)
        big = jnp.where((r >> 5) == (c >> 6), four(s.w2t_v[layer]), 0.0)
        h, l = split(big)
        s.w2ts[layer, 0:128] = h
        s.w2ts[layer, 128:256] = h
        s.w2tl[layer] = l
        h, l = split(big.T)
        s.w2c[layer, :, 0:128] = h
        s.w2c[layer, :, 128:256] = l
        bias = jnp.concatenate([s.b1_v[layer : layer + 1, :]] * 4, axis=1)
        s.bias[layer] = jnp.broadcast_to(bias, (8, 256))

    def volume_weights(layer):
        r, c = iota((128, 128), 0), iota((128, 128), 1)
        for axis in range(3):
            big = four(s.vol_v[layer, axis])
            big = jnp.where((r >> 5) == (c >> 5), big, 0.0) if axis < 2 else big * s.deriv_v[...]
            for value, stacked, rest in ((big, s.vs, s.vl), (big.T, s.vts, s.vtl)):
                h, l = split(value)
                stacked[layer, 0:128, narrow(axis)] = h
                stacked[layer, 128:256, narrow(axis)] = h
                rest[layer, :, narrow(axis)] = l

    with jax.named_scope("weights0"):
        for name in ("w1", "w2t", "b1", "vol", "deriv"):
            pulls[name].wait()
        flux_weights(0)
        volume_weights(0)
    with jax.named_scope("near0"):
        s.raw[...] = gathered(s.loc, s.trace)
        far_inner(0)
    with jax.named_scope("orient0"):
        orient_near(0)
    with jax.named_scope("hidden0"):
        hidden_near(0)
    with jax.named_scope("volume0"):
        volume_of(s.field, 0, False)
    with jax.named_scope("weights1"):
        flux_weights(1)
    with jax.named_scope("cotangent"):
        pulls["cot"].wait()
        traces(s.cot_v, keep_gflux(True))
    with jax.named_scope("far0"):
        far_pairs(0, 0)
    with jax.named_scope("field1"):
        s.flux[...] += dot(s.rem[...], s.flux_fh[...]) + dot(s.rem[...], s.flux_fl[...])
        for n in range(16):
            s.field[:, narrow(n)] += STEP_SIZE * (lift(s.flux, n // 4, n % 4) - s.volume[:, narrow(n)])
        traces(s.field, keep_traces(1))
    with jax.named_scope("pack1"):
        s.sent[1] = gathered(s.sel, s.trace)
    send_all(1, 1)
    with jax.named_scope("cotangent_far"):
        s.gflux_f[...] = dot(s.rem_t[...], s.gflux[...]).astype(BF16)
        for a in range(4):
            s.ghid_f[:, wide(a)] = hidden_grad(s.gflux_f[:, wide(a)], s.gflux_f[:, high(a)], 1)
    with jax.named_scope("near1"):
        s.raw[...] = gathered(s.loc, s.trace)
        far_inner(1)
    with jax.named_scope("orient1"):
        orient_near(1)
    with jax.named_scope("hidden1"):
        hidden_near(1)
    with jax.named_scope("back1"):
        back_near(1, s.gflux_n)
    with jax.named_scope("whole0"):
        for far, here in ((s.pair_fh, s.pair_nh), (s.pair_fl, s.pair_nl)):
            value = dot(s.rem[...], jnp.concatenate([far[0, :, low(a)] for a in range(4)], axis=1)).astype(BF16)
            for a in range(4):
                here[0, :, low(a)] += value[:, narrow(a)]
        for far, here in ((s.hid_fh, s.hid_nh), (s.hid_fl, s.hid_nl)):
            for a in range(4):
                own = s.masks_n[:, 384:512].astype(BF16)
                value = dot(s.rem[...], far[0, :, wide(a)]).astype(BF16)
                here[0, :, wide(a)] = here[0, :, wide(a)] * jnp.concatenate([own, own], axis=1) + value
    with jax.named_scope("weight_grads1_near"):
        parts = s.pair_nh.at[1], s.pair_nl.at[1], s.gpre_nh, s.gpre_nl, s.hid_nh.at[1], s.hid_nl.at[1], s.gflux_n
        s.one[...], s.two[...], row = weight_grads(parts)
        s.row[...] = jnp.broadcast_to(row, (8, 256))
    with jax.named_scope("far1"):
        far_pairs(1, 1)

    with jax.named_scope("turn1"):
        turn_back_near()
    with jax.named_scope("scatter1"):
        both = dot(s.loc_t[...], s.turn[...])
        value = both[:, 0:512] + both[:, 512:1024]
        s.gin[...] += value + dot(s.rem[...], s.gin_fh[...]) + dot(s.rem[...], s.gin_fl[...])
    with jax.named_scope("volume1"):
        volume_weights(1)
        volume_of(s.cot_v, 1, True)
    with jax.named_scope("weight_grads1"):
        parts = s.pair_fh.at[1], s.pair_fl.at[1], s.gpre_fh, s.gpre_fl, s.hid_fh.at[1], s.hid_fl.at[1], s.gflux_f
        one, two, row = weight_grads(parts)
        pack_grads(1, one + s.one[...], two + s.two[...], row + s.row[0:1, :])
        reduce_start(1)
    with jax.named_scope("wait2"):
        all_of(2).wait_recv()
    with jax.named_scope("grad1"):
        h, l = split(s.got[2])
        s.gin[...] += dot(s.sel_t[...], h) + dot(s.sel_t[...], l)
        for n in range(16):
            s.grad[:, narrow(n)] = tile(s.cot_v, n) - STEP_SIZE * s.volume[:, narrow(n)] + lift(s.gin, n // 4, n % 4)
        traces(s.grad, keep_gflux(False))
    with jax.named_scope("back0"):
        back_near(0, s.gflux)
    with jax.named_scope("sum1a"):
        reduce_middle(1)
    with jax.named_scope("weight_grads0"):
        parts = s.pair_nh.at[0], s.pair_nl.at[0], s.gpre_nh, s.gpre_nl, s.hid_nh.at[0], s.hid_nl.at[0], s.gflux
        pack_grads(0, *weight_grads(parts))
        reduce_start(0)
    with jax.named_scope("turn0"):
        turn_back_near()
    with jax.named_scope("pack3"):
        s.sent[3] = gathered(s.rem_t, s.turn)
    with jax.named_scope("sum0a"):
        reduce_middle(0)
    send_all(3, -1)
    with jax.named_scope("scatter0"):
        both = dot(s.loc_t[...], s.turn[...])
        s.gin[...] += both[:, 0:512] + both[:, 512:1024]
    with jax.named_scope("volume0b"):
        volume_of(s.grad, 0, True)
    with jax.named_scope("sum1b"):
        reduce_last(1)
    with jax.named_scope("sum0b"):
        reduce_last(0)
    with jax.named_scope("wait3"):
        all_of(3).wait_recv()
    with jax.named_scope("grad0"):
        h, l = split(s.got[3])
        s.gin[...] += dot(s.sel_t[...], h) + dot(s.sel_t[...], l)
        for n in range(16):
            value = s.grad[:, narrow(n)] - STEP_SIZE * s.volume[:, narrow(n)] + lift(s.gin, n // 4, n % 4)
            s.out_v[:, narrow(n)] = jnp.where(alive, value, 0.0)
        push = pltpu.make_async_copy(s.out_v, s.out, s.out_sem.at[0])
        push.start()
    with jax.named_scope("sumc"):
        stage_bytes(1, 2).wait()
        stage_bytes(0, 2).wait()
        push_total = pltpu.make_async_copy(s.total_v, s.total, s.out_sem.at[1])
        push_total.start()
    with jax.named_scope("sent"):
        for which in (0, 1):
            drain = pltpu.make_async_copy(s.sent.at[which], s.sent.at[which], s.send_sem.at[which])
            drain.wait()
        all_of(2).wait_send()
        all_of(3).wait_send()
        push.wait()
        push_total.wait()


def finish(factor, total_ref, field_ref, out_ref, w1_ref, b1_ref, w2t_ref):
    out_ref[...] = field_ref[...]
    for layer in range(2):
        value = total_ref[layer] * factor
        w1_ref[layer] = value[:, 0:64]
        w2t_ref[layer] = value.T[64:96, :]
        b1_ref[layer : layer + 1, :] = value.T[96:97, :]


def local(count, state, cotangent, elem_count, face_src, face_orient, send_face, vol_weight, w1, b1, w2):
    constant = np.zeros((128, 128), np.float32)
    for a in range(4):
        for k in range(4):
            constant[32 * k : 32 * k + 32, 32 * a : 32 * a + 32] = DERIV[a, k]
    vmem = pl.BlockSpec(memory_space=pltpu.VMEM)
    smem = pl.BlockSpec(memory_space=pltpu.SMEM)
    hbm = pl.BlockSpec(memory_space=pl.ANY)
    names = [*INPUTS, *OUTPUTS, *SCRATCH]
    scratch = [pltpu.VMEM(shape, dtype) for shape, dtype in SCRATCH.values()]
    extra = dict(
        part_sum=pltpu.VMEM((2, count // 8, 8, 128), F32),
        total_v=pltpu.VMEM((2, 64, 128), F32),
        live_v=pltpu.SMEM((1,), I32),
        out_sem=pltpu.SemaphoreType.DMA((2,)),
        in_sem=pltpu.SemaphoreType.DMA((11,)),
        send_sem=pltpu.SemaphoreType.DMA((4,)),
        near_sem=pltpu.SemaphoreType.DMA((2, NEIGH)),
        back_sem=pltpu.SemaphoreType.DMA((2,)),
        ar_send=pltpu.SemaphoreType.DMA((2, 3)),
        ar_recv=pltpu.SemaphoreType.DMA((2, 3)),
    )
    names += list(extra)
    scratch += list(extra.values())
    field, total = pl.pallas_call(
        functools.partial(kernel, count, names),
        out_shape=(jax.ShapeDtypeStruct(state.shape, F32), jax.ShapeDtypeStruct((2, 64, 128), F32)),
        in_specs=[hbm, hbm, hbm, hbm, hbm, hbm] + [hbm] * 5,
        out_specs=[hbm] * 2,
        scratch_shapes=scratch,
        compiler_params=pltpu.CompilerParams(
            collective_id=0, has_side_effects=True, vmem_limit_bytes=VMEM_LIMIT
        ),
    )(
        state, cotangent, elem_count, face_src, face_orient,
        send_face.reshape(1, -1), vol_weight, w1, b1, jnp.swapaxes(w2, 1, 2), jnp.asarray(constant),
    )
    factor = (2.0 * FACES * 8 * count) ** -0.5
    grad, grad_w1, grad_b1, grad_w2t = pl.pallas_call(
        functools.partial(finish, factor),
        out_shape=(
            jax.ShapeDtypeStruct(state.shape, F32),
            jax.ShapeDtypeStruct(w1.shape, F32),
            jax.ShapeDtypeStruct(b1.shape, F32),
            jax.ShapeDtypeStruct((2, 32, 64), F32),
        ),
        in_specs=[vmem] * 2,
        out_specs=[vmem] * 4,
    )(total, field)
    return grad, grad_w1, grad_b1, jnp.swapaxes(grad_w2t, 1, 2)


def solution(mesh):
    rows, flat, whole = P("dom", None), P("dom"), P()
    return jax.shard_map(
        functools.partial(local, mesh.shape["dom"]),
        mesh=mesh,
        in_specs=(rows, rows, flat, flat, flat, flat, whole, whole, whole, whole),
        out_specs=(rows, whole, whole, whole),
        check_vma=False,
    )
```

```python
import functools
import types

import jax
import jax.numpy as jnp
import numpy as np
from jax import lax
from jax.experimental import pallas as pl
from jax.experimental.pallas import tpu as pltpu
from jax.sharding import PartitionSpec as P

MESH = pl.DeviceIdType.MESH
HIGHEST = lax.Precision.HIGHEST
F32 = jnp.float32
BF16 = jnp.bfloat16
I32 = jnp.int32
NEIGH = 4
BLOCKS = 2 * NEIGH
CAP = 32
SLOTS = BLOCKS * CAP
STEP_SIZE = 0.25
E = 48
FACES = 6 * E
OFFSETS = [level + 1 for level in range(NEIGH)] + [-(level + 1) for level in range(NEIGH)]


VMEM_LIMIT = 56 * 1024 * 1024


def deriv_matrix():
    points = np.array([-1.0, -np.sqrt(0.2), np.sqrt(0.2), 1.0])
    weights = np.array(
        [np.prod([points[r] - points[o] for o in range(4) if o != r]) for r in range(4)]
    )
    matrix = np.zeros((4, 4))
    for r in range(4):
        for c in range(4):
            if r != c:
                matrix[r, c] = weights[r] / weights[c] / (points[r] - points[c])
        matrix[r, r] = -np.sum(matrix[r])
    return matrix


DERIV = deriv_matrix()


def iota(shape, dim):
    return lax.broadcasted_iota(I32, shape, dim)


def dot(a, b):
    return jnp.dot(a, b, preferred_element_type=F32)


def dot_nt(a, b):
    return lax.dot_general(a, b, (((1,), (1,)), ((), ())), preferred_element_type=F32)


def dot_tn(a, b):
    return lax.dot_general(a, b, (((0,), (0,)), ((), ())), preferred_element_type=F32)


def dot_full(a, b):
    return jnp.dot(a, b, preferred_element_type=F32, precision=HIGHEST)


def split(x):
    high = x.astype(BF16)
    return high, (x - high.astype(F32)).astype(BF16)


def three(op, a, b):
    return op(a[0], b[0]) + op(a[1], b[0]) + op(a[0], b[1])


def lanes(a):
    return pl.ds(pl.multiple_of(a * 128, 128), 128)


def ones_where(match, dtype=F32):
    return jnp.where(match, 1.0, 0.0).astype(dtype)


MASKS = 4

INPUTS = ("state", "cot", "live", "src", "orient", "send", "vol", "w1", "b1", "w2t", "deriv")
OUTPUTS = ("out", "total")
SCRATCH = dict(
    src_v=((FACES,), I32), orient_v=((FACES,), I32), send_v=((1, SLOTS), I32), state_v=((E, 2048), F32), cot_v=((E, 2048), F32),
    vol_v=((2, 3, 32, 32), F32), w1_v=((2, 64, 64), F32), b1_v=((2, 64), F32), w2t_v=((2, 32, 64), F32), deriv_v=((128, 128), F32),
    out_v=((E, 2048), F32), field=((E, 2048), F32), grad=((E, 2048), F32), volume=((E, 2048), F32),
    vol_y=((16 * E, 384), F32), vol_x=((16 * E, 256), BF16),
    trace=((FACES, 1024), BF16), raw=((FACES, 512), F32),
    pair_nh=((2, FACES, 1024), BF16), pair_nl=((2, FACES, 1024), BF16), pair_fh=((2, SLOTS, 1024), BF16), pair_fl=((2, SLOTS, 1024), BF16),
    hid_nh=((2, FACES, 1024), BF16), hid_nl=((2, FACES, 1024), BF16), hid_fh=((2, SLOTS, 1024), BF16), hid_fl=((2, SLOTS, 1024), BF16),
    flux=((FACES, 512), F32), flux_fh=((SLOTS, 512), BF16), flux_fl=((SLOTS, 512), BF16),
    gflux=((FACES, 1024), BF16), gflux_n=((FACES, 1024), BF16), gflux_f=((SLOTS, 1024), BF16), ghid_f=((SLOTS, 1024), F32),
    gpre_nh=((FACES, 1024), BF16), gpre_nl=((FACES, 1024), BF16), gpre_fh=((SLOTS, 1024), BF16), gpre_fl=((SLOTS, 1024), BF16),
    gin=((FACES, 512), F32), gin_fh=((SLOTS, 512), BF16), gin_fl=((SLOTS, 512), BF16), gout=((FACES, 512), F32),
    turn=((FACES, 1024), BF16),
    sel=((SLOTS, FACES), BF16), sel_t=((FACES, SLOTS), BF16), loc=((FACES, FACES), BF16), loc_t=((FACES, FACES), BF16),
    rem=((FACES, SLOTS), BF16), rem_t=((SLOTS, FACES), BF16),
    masks_n=((FACES, MASKS * 128), F32), masks_f=((SLOTS, MASKS * 128), F32),
    w1h=((2, 256, 256), BF16), w1l=((2, 256, 256), BF16), w1th=((2, 256, 256), BF16), w1tl=((2, 256, 256), BF16),
    w2c=((2, 256, 256), BF16), w2ts=((2, 256, 256), BF16), w2tl=((2, 128, 256), BF16),
    vs=((2, 256, 384), BF16), vl=((2, 128, 384), BF16), vts=((2, 256, 384), BF16), vtl=((2, 128, 384), BF16), bias=((2, 8, 256), F32),
    sent=((4, SLOTS, 512), F32), got=((4, SLOTS, 512), F32),
    one=((256, 256), F32), two=((256, 128), F32), row=((8, 256), F32),
    packed=((2, 64, 128), F32), part=((2, 8, 8, 128), F32),
)


def kernel(count, names, *refs):
    s = types.SimpleNamespace(**dict(zip(names, refs, strict=True)))
    me = lax.axis_index("dom")
    group = 8
    others = count // group
    base = (me // group) * group
    mine = lax.rem(me, group)
    rank = me // group

    def neighbour(offset):
        return lax.rem(me + offset + count, count)

    def in_group(step):
        return base + lax.rem(mine + step, group)

    def across(step):
        return lax.rem(rank + step, others) * group + mine

    barrier = pltpu.get_barrier_semaphore()
    partners = [neighbour(o) for o in OFFSETS]
    partners += [in_group(step) for step in range(1, group)]
    partners += [across(step) for step in range(1, others)]
    pulls = {}
    for n, name in enumerate(("send", "state", "live", "src", "orient", "vol", "w1", "b1", "w2t", "deriv", "cot")):
        pulls[name] = pltpu.make_async_copy(getattr(s, name), getattr(s, name + "_v"), s.in_sem.at[n])
        pulls[name].start()
    for device in partners:
        pl.semaphore_signal(barrier, inc=1, device_id=(device,), device_id_type=MESH)

    def far_copy(which, pair, side, sign):
        rows = pl.ds(pl.multiple_of(64 * pair + CAP * side, CAP), CAP)
        offset = (pair + 1) * (sign if side == 0 else -sign)
        return pltpu.make_async_remote_copy(
            src_ref=s.sent.at[which, rows],
            dst_ref=s.got.at[which, rows],
            send_sem=s.send_sem.at[which],
            recv_sem=s.near_sem.at[which, pair] if which < 2 else s.back_sem.at[which - 2],
            device_id=(neighbour(offset),),
            device_id_type=MESH,
        )

    def send_all(which, sign, pairs=(3, 2, 1, 0)):
        for pair in pairs:
            for side in range(2):
                far_copy(which, pair, side, sign).start()

    def all_of(which, pair=None):
        rows = pl.ds(0, SLOTS) if pair is None else pl.ds(pl.multiple_of(64 * pair, 64), 64)
        return pltpu.make_async_remote_copy(
            src_ref=s.sent.at[which, rows],
            dst_ref=s.got.at[which, rows],
            send_sem=s.send_sem.at[which],
            recv_sem=s.near_sem.at[which, pair] if which < 2 else s.back_sem.at[which - 2],
            device_id=(neighbour(1),),
            device_id_type=MESH,
        )

    def tile(ref, n):
        return ref[:, n * 128 : (n + 1) * 128]

    def wide(a):
        return slice(256 * a, 256 * a + 256)

    def high(a):
        return slice(256 * a, 256 * a + 128)

    def low(a):
        return slice(256 * a + 128, 256 * a + 256)

    def narrow(a):
        return slice(128 * a, 128 * a + 128)

    group_of_lane = iota((E, 128), 1) >> 5

    def traces(ref, emit):
        for a in range(4):
            emit(0, a, tile(ref, a))
            emit(1, a, tile(ref, 12 + a))
            emit(2, a, tile(ref, 4 * a))
            emit(3, a, tile(ref, 4 * a + 3))
            first = tile(ref, 4 * a)
            last = pltpu.roll(tile(ref, 4 * a), 32, 1)
            for b in range(1, 4):
                node = tile(ref, 4 * a + b)
                first = jnp.where(group_of_lane == b, pltpu.roll(node, 32 * b, 1), first)
                moved = node if b == 3 else pltpu.roll(node, 32 * (b + 1), 1)
                last = jnp.where(group_of_lane == b, moved, last)
            emit(4, a, first)
            emit(5, a, last)

    def lift(ref, i, j):
        at = lambda f, a: ref[f * E : (f + 1) * E, narrow(a)]
        first, last = at(4, i), at(5, i)
        first = pltpu.roll(first, (128 - 32 * j) % 128, 1) if j else first
        last = pltpu.roll(last, 96 - 32 * j, 1) if j < 3 else last
        value = jnp.where(group_of_lane == 0, first, jnp.where(group_of_lane == 3, last, 0.0))
        if i == 0:
            value = value + at(0, j)
        if i == 3:
            value = value + at(1, j)
        if j == 0:
            value = value + at(2, i)
        if j == 3:
            value = value + at(3, i)
        return value

    def keep_traces(layer):
        def emit(f, a, value):
            h, l = split(value)
            rows = slice(f * E, (f + 1) * E)
            s.trace[rows, narrow(a)] = h
            s.trace[rows, slice(512 + 128 * a, 640 + 128 * a)] = l
            s.pair_nh[layer, rows, high(a)] = h
            s.pair_nl[layer, rows, high(a)] = l

        return emit

    def keep_gflux(masked):
        def emit(f, a, value):
            h, l = split(STEP_SIZE * value)
            rows = slice(f * E, (f + 1) * E)
            s.gflux[rows, high(a)] = h
            s.gflux[rows, low(a)] = l
            if masked:
                here = s.masks_n[rows, 384:512].astype(BF16)
                s.gflux_n[rows, high(a)] = h * here
                s.gflux_n[rows, low(a)] = l * here

        return emit

    def gathered(matrix, ref):
        both = dot(matrix[...], ref[...])
        return both[:, 0:512] + both[:, 512:1024]

    def volume_of(ref, layer, adjoint):
        for n in range(16):
            h, l = split(tile(ref, n))
            s.vol_x[n * E : (n + 1) * E, 0:128] = h
            s.vol_x[n * E : (n + 1) * E, 128:256] = l
        stacked, rest = (s.vts, s.vtl) if adjoint else (s.vs, s.vl)
        s.vol_y[...] = dot(s.vol_x[...], stacked[layer]) + dot(s.vol_x[:, 0:128], rest[layer])
        deriv = DERIV.T if adjoint else DERIV
        for i in range(4):
            for j in range(4):
                n = 4 * i + j
                value = s.vol_y[n * E : (n + 1) * E, 256:384]
                for o in range(4):
                    if abs(deriv[i, o]) > 1e-12:
                        at = 4 * o + j
                        value = value + float(deriv[i, o]) * s.vol_y[at * E : (at + 1) * E, 0:128]
                    if abs(deriv[j, o]) > 1e-12:
                        at = 4 * i + o
                        value = value + float(deriv[j, o]) * s.vol_y[at * E : (at + 1) * E, 128:256]
                s.volume[:, narrow(n)] = value

    def flip_lanes(x, odd):
        return jnp.where(odd, pltpu.roll(x, 96, 1), pltpu.roll(x, 32, 1))

    def swap(x, odd, upper):
        stage = [None] * 4
        for a in (0, 2):
            stage[a] = jnp.where(odd, pltpu.roll(x[a + 1], 32, 1), x[a])
            stage[a + 1] = jnp.where(odd, x[a + 1], pltpu.roll(x[a], 96, 1))
        out = [None] * 4
        for a in (0, 1):
            out[a] = jnp.where(upper, pltpu.roll(stage[a + 2], 64, 1), stage[a])
            out[a + 2] = jnp.where(upper, stage[a + 2], pltpu.roll(stage[a], 64, 1))
        return out

    def lane_masks(count_):
        groups = iota((count_, 128), 1) >> 5
        return (groups & 1) == 1, groups >= 2

    def oriented(x, marks):
        odd, upper = lane_masks(x[0].shape[0])
        first, second, swapped = marks
        x = [jnp.where(first, x[3 - a], x[a]) for a in range(4)]
        x = [jnp.where(second, flip_lanes(v, odd), v) for v in x]
        y = swap(x, odd, upper)
        return [jnp.where(swapped, y[a], x[a]) for a in range(4)]

    def turned_back(x, marks):
        odd, upper = lane_masks(x[0].shape[0])
        first, second, swapped = marks
        y = swap(x, odd, upper)
        x = [jnp.where(swapped, y[a], x[a]) for a in range(4)]
        x = [jnp.where(second, flip_lanes(v, odd), v) for v in x]
        return [jnp.where(first, x[3 - a], x[a]) for a in range(4)]

    def marks_of(ref, rows):
        return [ref[rows, narrow(m)] > 0.5 for m in range(3)]

    def each_rows(body):
        body(slice(0, FACES))

    def orient_near(layer):
        def body(rows):
            x = oriented([s.raw[rows, narrow(a)] for a in range(4)], marks_of(s.masks_n, rows))
            for a in range(4):
                s.pair_nh[layer, rows, low(a)], s.pair_nl[layer, rows, low(a)] = split(x[a])

        each_rows(body)

    def turn_back_near():
        def body(rows):
            x = turned_back([s.gout[rows, narrow(a)] for a in range(4)], marks_of(s.masks_n, rows))
            for a in range(4):
                h, l = split(x[a])
                s.turn[rows, narrow(a)] = h
                s.turn[rows, slice(512 + 128 * a, 640 + 128 * a)] = l

        each_rows(body)

    def each_a(body):
        for a in range(4):
            body(wide(a), high(a), narrow(a))

    def hidden(xh, xl, layer):
        pre = dot(xh, s.w1h[layer]) + dot(xl, s.w1h[layer]) + dot(xh, s.w1l[layer])
        return jnp.tanh(pre + s.bias[layer, 0:1, :])

    def flux_of(h, l, layer):
        both = dot(h, s.w2c[layer])
        return both[:, 0:128] + both[:, 128:256] + dot(l, s.w2c[layer, :, 0:128])

    def hidden_grad(both, top, layer):
        return dot(both, s.w2ts[layer]) + dot(top, s.w2tl[layer])

    def pair_grad(h, l, layer):
        return dot(h, s.w1th[layer]) + dot(l, s.w1th[layer]) + dot(h, s.w1tl[layer])

    def hidden_near(layer):
        def body(w, h_, n):
            h, l = split(hidden(s.pair_nh[layer, :, w], s.pair_nl[layer, :, w], layer))
            s.hid_nh[layer, :, w] = h
            s.hid_nl[layer, :, w] = l
            if layer == 0:
                s.flux[:, n] = flux_of(h, l, layer) * s.masks_n[:, 384:512]

        each_a(body)

    def back_near(layer, gflux):
        def body(w, h_, n):
            h = s.hid_nh[layer, :, w].astype(F32) + s.hid_nl[layer, :, w].astype(F32)
            gp = hidden_grad(gflux[:, w], gflux[:, h_], layer) * (1.0 - h * h)
            gh, gl = split(gp)
            s.gpre_nh[:, w] = gh
            s.gpre_nl[:, w] = gl
            both = pair_grad(gh, gl, layer)
            s.gin[:, n] = both[:, 0:128]
            s.gout[:, n] = both[:, 128:256]

        each_a(body)

    def far_pairs(which, layer):
        def step(n, carry):
            pair = 3 - n
            rows = pl.ds(pl.multiple_of(64 * pair, 64), 64)
            all_of(which, pair).wait_recv()
            for side in range(2):
                part_rows = pl.ds(pl.multiple_of(64 * pair + CAP * side, CAP), CAP)
                x = oriented([s.got[which, part_rows, narrow(a)] for a in range(4)], marks_of(s.masks_f, part_rows))
                for a in range(4):
                    s.pair_fh[layer, part_rows, low(a)], s.pair_fl[layer, part_rows, low(a)] = split(x[a])
            stack = lambda ref, cut: jnp.concatenate([ref[rows, cut(a)] for a in range(4)], axis=0)
            value = hidden(stack(s.pair_fh.at[layer], wide), stack(s.pair_fl.at[layer], wide), layer)
            h, l = split(value)
            part_of = lambda v, a: v[64 * a : 64 * a + 64]
            for a in range(4):
                s.hid_fh[layer, rows, wide(a)] = part_of(h, a)
                s.hid_fl[layer, rows, wide(a)] = part_of(l, a)
            if layer == 0:
                fh, fl = split(flux_of(h, l, layer))
                for a in range(4):
                    s.flux_fh[rows, narrow(a)] = part_of(fh, a)
                    s.flux_fl[rows, narrow(a)] = part_of(fl, a)
            else:
                gh, gl = split(stack(s.ghid_f, wide) * (1.0 - value * value))
                both = pair_grad(gh, gl, layer)
                ih, il = split(both[:, 0:128])
                for a in range(4):
                    s.gpre_fh[rows, wide(a)] = part_of(gh, a)
                    s.gpre_fl[rows, wide(a)] = part_of(gl, a)
                    s.gin_fh[rows, narrow(a)] = part_of(ih, a)
                    s.gin_fl[rows, narrow(a)] = part_of(il, a)
                for side in range(2):
                    part_rows = pl.ds(pl.multiple_of(64 * pair + CAP * side, CAP), CAP)
                    cut = lambda a: both[64 * a + CAP * side : 64 * a + CAP * side + CAP, 128:256]
                    x = turned_back([cut(a) for a in range(4)], marks_of(s.masks_f, part_rows))
                    for a in range(4):
                        s.sent[which + 1, part_rows, narrow(a)] = x[a]
                for side in range(2):
                    far_copy(which + 1, pair, side, -1).start()
            return carry

        lax.fori_loop(0, 4, step, 0)

    def far_inner(layer):
        both = dot(s.rem_t[...], s.trace[...]).astype(BF16)
        for a in range(4):
            s.pair_fh[layer, :, high(a)] = both[:, narrow(a)]
            s.pair_fl[layer, :, high(a)] = both[:, 512 + 128 * a : 640 + 128 * a]

    def weight_grads(parts):
        rows_of = lambda ref, cut: jnp.concatenate([ref[:, cut(a)] for a in range(4)], axis=0)
        xh, xl, gph, gpl, hh, hl, g = parts
        gh, gl, x = rows_of(gph, wide), rows_of(gpl, wide), rows_of(xh, wide)
        one = dot_tn(x, gh) + dot_tn(rows_of(xl, wide), gh) + dot_tn(x, gl)
        two = dot_tn(rows_of(hh, wide), rows_of(g, wide))
        top = dot_tn(rows_of(hl, wide), rows_of(g, high))
        two = two[:, 0:128] + two[:, 128:256] + top
        row = jnp.sum(gh.astype(F32) + gl.astype(F32), axis=0, keepdims=True)
        return one, two, row

    def pack_grads(layer, one, two, row):
        r, c = iota((256, 256), 0), iota((256, 256), 1)
        one = jnp.where(((r >> 5) & 3) == (c >> 6), one, 0.0)
        one = one[:, 0:128] + one[:, 128:256]
        one = one + pltpu.roll(one, 64, 1)
        halves = [sum(one[128 * half + 32 * b : 128 * half + 32 * b + 32] for b in range(4)) for half in range(2)]
        one = jnp.concatenate(halves, axis=0)
        r, c = iota((256, 128), 0), iota((256, 128), 1)
        two = jnp.where((r >> 6) == (c >> 5), two, 0.0)
        two = sum(two[64 * b : 64 * b + 64] for b in range(4))
        two = two + pltpu.roll(two, 64, 1)
        two = two + pltpu.roll(two, 32, 1)
        row = row[:, 0:128] + row[:, 128:256]
        row = row + pltpu.roll(row, 64, 1)
        r, c = iota((64, 128), 0), iota((64, 128), 1)
        column = jnp.sum(jnp.where(r == c, row, 0.0), axis=1, keepdims=True)
        value = jnp.where(c < 64, one, jnp.where(c < 96, two, jnp.where(c == 96, column, 0.0)))
        s.packed[layer] = value

    def piece(j):
        return pl.ds(pl.multiple_of(j * 8, 8), 8)

    def remote(src, dst, sems, device):
        return pltpu.make_async_remote_copy(
            src_ref=src, dst_ref=dst, send_sem=sems[0], recv_sem=sems[1], device_id=(device,), device_id_type=MESH
        )

    def sems(layer, stage):
        return s.ar_send.at[layer, stage], s.ar_recv.at[layer, stage]

    def scatter(layer):
        return [
            remote(s.packed.at[layer, piece(lax.rem(mine + t, group))], s.part.at[layer, mine], sems(layer, 0), in_group(t))
            for t in range(1, group)
        ]

    def spread(layer):
        here = s.part_sum.at[layer, rank]
        return [remote(here, here, sems(layer, 1), across(t)) for t in range(1, others)]

    def collect(layer):
        here = s.total_v.at[layer, piece(mine)]
        return [remote(here, here, sems(layer, 2), in_group(t)) for t in range(1, group)]

    def stage_bytes(layer, stage):
        here = (
            s.part.at[layer, pl.ds(0, group - 1)],
            s.part_sum.at[layer, pl.ds(0, others - 1)],
            s.total_v.at[layer, pl.ds(0, 8 * (group - 1))],
        )[stage]
        return remote(here, here, sems(layer, stage), in_group(1))

    def start(copies):
        for copy in copies:
            copy.start()

    def reduce_start(layer):
        start(scatter(layer))
        s.part[layer, mine] = s.packed[layer, piece(mine), :]

    def reduce_middle(layer):
        stage_bytes(layer, 0).wait()
        value = s.part[layer, 0]
        for t in range(1, group):
            value = value + s.part[layer, t]
        s.part_sum[layer, rank] = value
        start(spread(layer))

    def reduce_last(layer):
        stage_bytes(layer, 1).wait()
        value = s.part_sum[layer, 0]
        for t in range(1, others):
            value = value + s.part_sum[layer, t]
        s.total_v[layer, piece(mine), :] = value
        start(collect(layer))

    with jax.named_scope("send_table"):
        order = (0, 4, 1, 5, 2, 6, 3, 7)
        pulls["send"].wait()
        row = s.send_v[...]
        row = jnp.concatenate([row[:, CAP * b : CAP * b + CAP] for b in order], axis=1)
        for f in range(6):
            s.sel_t[f * E : (f + 1) * E, :] = ones_where(6 * iota((E, SLOTS), 0) + f == row, BF16)
        eye = ones_where(iota((SLOTS, SLOTS), 0) == iota((SLOTS, SLOTS), 1), BF16)
        s.sel[...] = dot_nt(eye, s.sel_t[...]).astype(BF16)

    with jax.named_scope("field0"):
        pulls["state"].wait()
        pulls["live"].wait()
        alive = iota((E, 128), 0) < s.live_v[0]
        for n in range(16):
            s.field[:, narrow(n)] = jnp.where(alive, tile(s.state_v, n), 0.0)
        traces(s.field, keep_traces(0))
    with jax.named_scope("pack0"):
        s.sent[0] = gathered(s.sel, s.trace)
    with jax.named_scope("barrier"):
        pl.semaphore_wait(barrier, len(partners))
    send_all(0, 1)

    with jax.named_scope("tables"):
        for f in range(6):
            s.raw[f * E : (f + 1) * E, 0:FACES] = ones_where(6 * iota((E, FACES), 0) + f == iota((E, FACES), 1))
        by_kind = s.raw[:, 0:FACES].astype(BF16)
        pulls["src"].wait()
        source = s.src_v[...].reshape(1, FACES)
        near = jnp.concatenate([ones_where(6 * iota((E, FACES), 0) + f == source, BF16) for f in range(6)], axis=0)
        slot = iota((SLOTS, FACES), 0)
        slot = ((slot >> 5) & 1) * 128 + (slot >> 6) * CAP + (slot & 31)
        far = ones_where(slot + FACES == source, BF16)
        s.loc_t[...] = dot_nt(near, by_kind).astype(BF16)
        s.loc[...] = dot_nt(by_kind, near).astype(BF16)
        s.rem_t[...] = dot_nt(far, by_kind).astype(BF16)
        s.rem[...] = dot_nt(by_kind, far).astype(BF16)
        pulls["orient"].wait()
        turn = s.orient_v[...].reshape(1, FACES)
        flags = [(turn >> 1) & 1, (turn ^ (turn >> 1)) & 1, (turn ^ (turn >> 2)) & 1, jnp.where(source < FACES, 1, 0)]
        for m in range(MASKS):
            spread_out = jnp.broadcast_to(flags[m], (128, FACES)).astype(F32).astype(BF16)
            s.masks_n[:, narrow(m)] = dot_nt(by_kind, spread_out)
            s.masks_f[:, narrow(m)] = dot_nt(far, spread_out)

    def four(x):
        x = jnp.concatenate([x] * 4, axis=1)
        return jnp.concatenate([x] * 4, axis=0)

    def flux_weights(layer):
        r, c = iota((256, 256), 0), iota((256, 256), 1)
        w1 = s.w1_v[layer]
        big = jnp.concatenate([four(w1[0:32]), four(w1[32:64])], axis=0)
        big = jnp.where(((r >> 5) & 3) == (c >> 6), big, 0.0)
        s.w1h[layer], s.w1l[layer] = split(big)
        s.w1th[layer], s.w1tl[layer] = split(big.T)
        r, c = iota((128, 256), 0), iota((128, 256), 1)
        big = jnp.where((r >> 5) == (c >> 6), four(s.w2t_v[layer]), 0.0)
        h, l = split(big)
        s.w2ts[layer, 0:128] = h
        s.w2ts[layer, 128:256] = h
        s.w2tl[layer] = l
        h, l = split(big.T)
        s.w2c[layer, :, 0:128] = h
        s.w2c[layer, :, 128:256] = l
        bias = jnp.concatenate([s.b1_v[layer : layer + 1, :]] * 4, axis=1)
        s.bias[layer] = jnp.broadcast_to(bias, (8, 256))

    def volume_weights(layer):
        r, c = iota((128, 128), 0), iota((128, 128), 1)
        for axis in range(3):
            big = four(s.vol_v[layer, axis])
            big = jnp.where((r >> 5) == (c >> 5), big, 0.0) if axis < 2 else big * s.deriv_v[...]
            for value, stacked, rest in ((big, s.vs, s.vl), (big.T, s.vts, s.vtl)):
                h, l = split(value)
                stacked[layer, 0:128, narrow(axis)] = h
                stacked[layer, 128:256, narrow(axis)] = h
                rest[layer, :, narrow(axis)] = l

    with jax.named_scope("weights0"):
        for name in ("w1", "w2t", "b1", "vol", "deriv"):
            pulls[name].wait()
        flux_weights(0)
        volume_weights(0)
    with jax.named_scope("near0"):
        s.raw[...] = gathered(s.loc, s.trace)
        far_inner(0)
    with jax.named_scope("orient0"):
        orient_near(0)
    with jax.named_scope("hidden0"):
        hidden_near(0)
    with jax.named_scope("volume0"):
        volume_of(s.field, 0, False)
    with jax.named_scope("weights1"):
        flux_weights(1)
    with jax.named_scope("cotangent"):
        pulls["cot"].wait()
        traces(s.cot_v, keep_gflux(True))
    with jax.named_scope("far0"):
        far_pairs(0, 0)
    with jax.named_scope("field1"):
        s.flux[...] += dot(s.rem[...], s.flux_fh[...]) + dot(s.rem[...], s.flux_fl[...])
        for n in range(16):
            s.field[:, narrow(n)] += STEP_SIZE * (lift(s.flux, n // 4, n % 4) - s.volume[:, narrow(n)])
        traces(s.field, keep_traces(1))
    with jax.named_scope("pack1"):
        s.sent[1] = gathered(s.sel, s.trace)
    send_all(1, 1)
    with jax.named_scope("cotangent_far"):
        s.gflux_f[...] = dot(s.rem_t[...], s.gflux[...]).astype(BF16)
        for a in range(4):
            s.ghid_f[:, wide(a)] = hidden_grad(s.gflux_f[:, wide(a)], s.gflux_f[:, high(a)], 1)
    with jax.named_scope("near1"):
        s.raw[...] = gathered(s.loc, s.trace)
        far_inner(1)
    with jax.named_scope("orient1"):
        orient_near(1)
    with jax.named_scope("hidden1"):
        hidden_near(1)
    with jax.named_scope("back1"):
        back_near(1, s.gflux_n)
    with jax.named_scope("whole0"):
        for far, here in ((s.pair_fh, s.pair_nh), (s.pair_fl, s.pair_nl)):
            value = dot(s.rem[...], jnp.concatenate([far[0, :, low(a)] for a in range(4)], axis=1)).astype(BF16)
            for a in range(4):
                here[0, :, low(a)] += value[:, narrow(a)]
        for far, here in ((s.hid_fh, s.hid_nh), (s.hid_fl, s.hid_nl)):
            for a in range(4):
                own = s.masks_n[:, 384:512].astype(BF16)
                value = dot(s.rem[...], far[0, :, wide(a)]).astype(BF16)
                here[0, :, wide(a)] = here[0, :, wide(a)] * jnp.concatenate([own, own], axis=1) + value
    with jax.named_scope("weight_grads1_near"):
        parts = s.pair_nh.at[1], s.pair_nl.at[1], s.gpre_nh, s.gpre_nl, s.hid_nh.at[1], s.hid_nl.at[1], s.gflux_n
        s.one[...], s.two[...], row = weight_grads(parts)
        s.row[...] = jnp.broadcast_to(row, (8, 256))
    with jax.named_scope("far1"):
        far_pairs(1, 1)

    with jax.named_scope("turn1"):
        turn_back_near()
    with jax.named_scope("scatter1"):
        both = dot(s.loc_t[...], s.turn[...])
        value = both[:, 0:512] + both[:, 512:1024]
        s.gin[...] += value + dot(s.rem[...], s.gin_fh[...]) + dot(s.rem[...], s.gin_fl[...])
    with jax.named_scope("volume1"):
        volume_weights(1)
        volume_of(s.cot_v, 1, True)
    with jax.named_scope("weight_grads1"):
        parts = s.pair_fh.at[1], s.pair_fl.at[1], s.gpre_fh, s.gpre_fl, s.hid_fh.at[1], s.hid_fl.at[1], s.gflux_f
        one, two, row = weight_grads(parts)
        pack_grads(1, one + s.one[...], two + s.two[...], row + s.row[0:1, :])
        reduce_start(1)
    with jax.named_scope("wait2"):
        all_of(2).wait_recv()
    with jax.named_scope("grad1"):
        h, l = split(s.got[2])
        s.gin[...] += dot(s.sel_t[...], h) + dot(s.sel_t[...], l)
        for n in range(16):
            s.grad[:, narrow(n)] = tile(s.cot_v, n) - STEP_SIZE * s.volume[:, narrow(n)] + lift(s.gin, n // 4, n % 4)
        traces(s.grad, keep_gflux(False))
    with jax.named_scope("back0"):
        back_near(0, s.gflux)
    with jax.named_scope("weight_grads0"):
        parts = s.pair_nh.at[0], s.pair_nl.at[0], s.gpre_nh, s.gpre_nl, s.hid_nh.at[0], s.hid_nl.at[0], s.gflux
        pack_grads(0, *weight_grads(parts))
        reduce_start(0)
    with jax.named_scope("sum1a"):
        reduce_middle(1)
    with jax.named_scope("turn0"):
        turn_back_near()
    with jax.named_scope("pack3"):
        s.sent[3] = gathered(s.rem_t, s.turn)
    send_all(3, -1, (3,))
    with jax.named_scope("sum0a"):
        reduce_middle(0)
    send_all(3, -1, (2, 1, 0))
    with jax.named_scope("scatter0"):
        both = dot(s.loc_t[...], s.turn[...])
        s.gin[...] += both[:, 0:512] + both[:, 512:1024]
    with jax.named_scope("volume0b"):
        volume_of(s.grad, 0, True)
    with jax.named_scope("sum1b"):
        reduce_last(1)
    with jax.named_scope("sum0b"):
        reduce_last(0)
    with jax.named_scope("wait3"):
        all_of(3).wait_recv()
    with jax.named_scope("grad0"):
        h, l = split(s.got[3])
        s.gin[...] += dot(s.sel_t[...], h) + dot(s.sel_t[...], l)
        for n in range(16):
            value = s.grad[:, narrow(n)] - STEP_SIZE * s.volume[:, narrow(n)] + lift(s.gin, n // 4, n % 4)
            s.out_v[:, narrow(n)] = jnp.where(alive, value, 0.0)
        push = pltpu.make_async_copy(s.out_v, s.out, s.out_sem.at[0])
        push.start()
    with jax.named_scope("sumc"):
        stage_bytes(1, 2).wait()
        stage_bytes(0, 2).wait()
        push_total = pltpu.make_async_copy(s.total_v, s.total, s.out_sem.at[1])
        push_total.start()
    with jax.named_scope("sent"):
        for which in (0, 1):
            drain = pltpu.make_async_copy(s.sent.at[which], s.sent.at[which], s.send_sem.at[which])
            drain.wait()
        all_of(2).wait_send()
        all_of(3).wait_send()
        push.wait()
        push_total.wait()


def finish(factor, total_ref, field_ref, out_ref, w1_ref, b1_ref, w2t_ref):
    out_ref[...] = field_ref[...]
    for layer in range(2):
        value = total_ref[layer] * factor
        w1_ref[layer] = value[:, 0:64]
        w2t_ref[layer] = value.T[64:96, :]
        b1_ref[layer : layer + 1, :] = value.T[96:97, :]


def local(count, state, cotangent, elem_count, face_src, face_orient, send_face, vol_weight, w1, b1, w2):
    constant = np.zeros((128, 128), np.float32)
    for a in range(4):
        for k in range(4):
            constant[32 * k : 32 * k + 32, 32 * a : 32 * a + 32] = DERIV[a, k]
    vmem = pl.BlockSpec(memory_space=pltpu.VMEM)
    smem = pl.BlockSpec(memory_space=pltpu.SMEM)
    hbm = pl.BlockSpec(memory_space=pl.ANY)
    names = [*INPUTS, *OUTPUTS, *SCRATCH]
    scratch = [pltpu.VMEM(shape, dtype) for shape, dtype in SCRATCH.values()]
    extra = dict(
        part_sum=pltpu.VMEM((2, count // 8, 8, 128), F32),
        total_v=pltpu.VMEM((2, 64, 128), F32),
        live_v=pltpu.SMEM((1,), I32),
        out_sem=pltpu.SemaphoreType.DMA((2,)),
        in_sem=pltpu.SemaphoreType.DMA((11,)),
        send_sem=pltpu.SemaphoreType.DMA((4,)),
        near_sem=pltpu.SemaphoreType.DMA((2, NEIGH)),
        back_sem=pltpu.SemaphoreType.DMA((2,)),
        ar_send=pltpu.SemaphoreType.DMA((2, 3)),
        ar_recv=pltpu.SemaphoreType.DMA((2, 3)),
    )
    names += list(extra)
    scratch += list(extra.values())
    field, total = pl.pallas_call(
        functools.partial(kernel, count, names),
        out_shape=(jax.ShapeDtypeStruct(state.shape, F32), jax.ShapeDtypeStruct((2, 64, 128), F32)),
        in_specs=[hbm, hbm, hbm, hbm, hbm, hbm] + [hbm] * 5,
        out_specs=[hbm] * 2,
        scratch_shapes=scratch,
        compiler_params=pltpu.CompilerParams(
            collective_id=0, has_side_effects=True, vmem_limit_bytes=VMEM_LIMIT
        ),
    )(
        state, cotangent, elem_count, face_src, face_orient,
        send_face.reshape(1, -1), vol_weight, w1, b1, jnp.swapaxes(w2, 1, 2), jnp.asarray(constant),
    )
    factor = (2.0 * FACES * 8 * count) ** -0.5
    grad, grad_w1, grad_b1, grad_w2t = pl.pallas_call(
        functools.partial(finish, factor),
        out_shape=(
            jax.ShapeDtypeStruct(state.shape, F32),
            jax.ShapeDtypeStruct(w1.shape, F32),
            jax.ShapeDtypeStruct(b1.shape, F32),
            jax.ShapeDtypeStruct((2, 32, 64), F32),
        ),
        in_specs=[vmem] * 2,
        out_specs=[vmem] * 4,
    )(total, field)
    return grad, grad_w1, grad_b1, jnp.swapaxes(grad_w2t, 1, 2)


def solution(mesh):
    rows, flat, whole = P("dom", None), P("dom"), P()
    return jax.shard_map(
        functools.partial(local, mesh.shape["dom"]),
        mesh=mesh,
        in_specs=(rows, rows, flat, flat, flat, flat, whole, whole, whole, whole),
        out_specs=(rows, whole, whole, whole),
        check_vma=False,
    )
```

```python
import functools
import types

import jax
import jax.numpy as jnp
import numpy as np
from jax import lax
from jax.experimental import pallas as pl
from jax.experimental.pallas import tpu as pltpu
from jax.sharding import PartitionSpec as P

MESH = pl.DeviceIdType.MESH
HIGHEST = lax.Precision.HIGHEST
F32 = jnp.float32
BF16 = jnp.bfloat16
I32 = jnp.int32
NEIGH = 4
BLOCKS = 2 * NEIGH
CAP = 32
SLOTS = BLOCKS * CAP
STEP_SIZE = 0.25
E = 48
FACES = 6 * E
OFFSETS = [level + 1 for level in range(NEIGH)] + [-(level + 1) for level in range(NEIGH)]


VMEM_LIMIT = 56 * 1024 * 1024


def deriv_matrix():
    points = np.array([-1.0, -np.sqrt(0.2), np.sqrt(0.2), 1.0])
    weights = np.array(
        [np.prod([points[r] - points[o] for o in range(4) if o != r]) for r in range(4)]
    )
    matrix = np.zeros((4, 4))
    for r in range(4):
        for c in range(4):
            if r != c:
                matrix[r, c] = weights[r] / weights[c] / (points[r] - points[c])
        matrix[r, r] = -np.sum(matrix[r])
    return matrix


DERIV = deriv_matrix()


def iota(shape, dim):
    return lax.broadcasted_iota(I32, shape, dim)


def dot(a, b):
    return jnp.dot(a, b, preferred_element_type=F32)


def dot_nt(a, b):
    return lax.dot_general(a, b, (((1,), (1,)), ((), ())), preferred_element_type=F32)


def dot_tn(a, b):
    return lax.dot_general(a, b, (((0,), (0,)), ((), ())), preferred_element_type=F32)


def dot_full(a, b):
    return jnp.dot(a, b, preferred_element_type=F32, precision=HIGHEST)


def split(x):
    high = x.astype(BF16)
    return high, (x - high.astype(F32)).astype(BF16)


def three(op, a, b):
    return op(a[0], b[0]) + op(a[1], b[0]) + op(a[0], b[1])


def lanes(a):
    return pl.ds(pl.multiple_of(a * 128, 128), 128)


def ones_where(match, dtype=F32):
    return jnp.where(match, 1.0, 0.0).astype(dtype)


MASKS = 4

INPUTS = ("state", "cot", "live", "src", "orient", "send", "vol", "w1", "b1", "w2t", "deriv")
OUTPUTS = ("out", "total")
SCRATCH = dict(
    src_v=((FACES,), I32), orient_v=((FACES,), I32), send_v=((1, SLOTS), I32), state_v=((E, 2048), F32), cot_v=((E, 2048), F32),
    vol_v=((2, 3, 32, 32), F32), w1_v=((2, 64, 64), F32), b1_v=((2, 64), F32), w2t_v=((2, 32, 64), F32), deriv_v=((128, 128), F32),
    out_v=((E, 2048), F32), field=((E, 2048), F32), grad=((E, 2048), F32), volume=((E, 2048), F32),
    vol_y=((16 * E, 384), F32), vol_x=((16 * E, 256), BF16),
    trace=((FACES, 1024), BF16), raw=((FACES, 512), F32),
    pair_nh=((2, FACES, 1024), BF16), pair_nl=((2, FACES, 1024), BF16), pair_fh=((2, SLOTS, 1024), BF16), pair_fl=((2, SLOTS, 1024), BF16),
    hid_nh=((2, FACES, 1024), BF16), hid_nl=((2, FACES, 1024), BF16), hid_fh=((2, SLOTS, 1024), BF16), hid_fl=((2, SLOTS, 1024), BF16),
    flux=((FACES, 512), F32), flux_fh=((SLOTS, 512), BF16), flux_fl=((SLOTS, 512), BF16),
    gflux=((FACES, 1024), BF16), gflux_n=((FACES, 1024), BF16), gflux_f=((SLOTS, 1024), BF16), ghid_f=((SLOTS, 1024), F32),
    gpre_nh=((FACES, 1024), BF16), gpre_nl=((FACES, 1024), BF16), gpre_fh=((SLOTS, 1024), BF16), gpre_fl=((SLOTS, 1024), BF16),
    gin=((FACES, 512), F32), gin_fh=((SLOTS, 512), BF16), gin_fl=((SLOTS, 512), BF16), gout=((FACES, 512), F32),
    turn=((FACES, 1024), BF16),
    sel=((SLOTS, FACES), BF16), sel_t=((FACES, SLOTS), BF16), loc=((FACES, FACES), BF16), loc_t=((FACES, FACES), BF16),
    rem=((FACES, SLOTS), BF16), rem_t=((SLOTS, FACES), BF16),
    masks_n=((FACES, MASKS * 128), F32), masks_f=((SLOTS, MASKS * 128), F32),
    w1h=((2, 256, 256), BF16), w1l=((2, 256, 256), BF16), w1th=((2, 256, 256), BF16), w1tl=((2, 256, 256), BF16),
    w2c=((2, 256, 256), BF16), w2ts=((2, 256, 256), BF16), w2tl=((2, 128, 256), BF16),
    vs=((2, 256, 384), BF16), vl=((2, 128, 384), BF16), vts=((2, 256, 384), BF16), vtl=((2, 128, 384), BF16), bias=((2, 8, 256), F32),
    sent=((4, SLOTS, 512), F32), got=((4, SLOTS, 512), F32),
    slope=((FACES, 1024), F32),
    one=((256, 256), F32), two=((256, 128), F32), row=((8, 256), F32),
    packed=((2, 64, 128), F32), part=((2, 8, 8, 128), F32),
)


def kernel(count, names, *refs):
    s = types.SimpleNamespace(**dict(zip(names, refs, strict=True)))
    me = lax.axis_index("dom")
    group = 8
    others = count // group
    base = (me // group) * group
    mine = lax.rem(me, group)
    rank = me // group

    def neighbour(offset):
        return lax.rem(me + offset + count, count)

    def in_group(step):
        return base + lax.rem(mine + step, group)

    def across(step):
        return lax.rem(rank + step, others) * group + mine

    barrier = pltpu.get_barrier_semaphore()
    partners = [neighbour(o) for o in OFFSETS]
    partners += [in_group(step) for step in range(1, group)]
    partners += [across(step) for step in range(1, others)]
    pulls = {}
    for n, name in enumerate(("send", "state", "live", "src", "orient", "vol", "w1", "b1", "w2t", "deriv", "cot")):
        pulls[name] = pltpu.make_async_copy(getattr(s, name), getattr(s, name + "_v"), s.in_sem.at[n])
        pulls[name].start()
    for device in partners:
        pl.semaphore_signal(barrier, inc=1, device_id=(device,), device_id_type=MESH)

    def far_copy(which, pair, side, sign):
        rows = pl.ds(64 * pair + CAP * side, CAP)
        offset = (pair + 1) * (sign if side == 0 else -sign)
        return pltpu.make_async_remote_copy(
            src_ref=s.sent.at[which, rows],
            dst_ref=s.got.at[which, rows],
            send_sem=s.send_sem.at[which],
            recv_sem=s.near_sem.at[which, pair] if which < 2 else s.back_sem.at[which - 2],
            device_id=(neighbour(offset),),
            device_id_type=MESH,
        )

    def send_all(which, sign, pairs=(3, 2, 1, 0)):
        for pair in pairs:
            for side in range(2):
                far_copy(which, pair, side, sign).start()

    def all_of(which, pair=None):
        rows = pl.ds(0, SLOTS) if pair is None else pl.ds(64 * pair, 64)
        return pltpu.make_async_remote_copy(
            src_ref=s.sent.at[which, rows],
            dst_ref=s.got.at[which, rows],
            send_sem=s.send_sem.at[which],
            recv_sem=s.near_sem.at[which, pair] if which < 2 else s.back_sem.at[which - 2],
            device_id=(neighbour(1),),
            device_id_type=MESH,
        )

    def tile(ref, n):
        return ref[:, n * 128 : (n + 1) * 128]

    def wide(a):
        return slice(256 * a, 256 * a + 256)

    def high(a):
        return slice(256 * a, 256 * a + 128)

    def low(a):
        return slice(256 * a + 128, 256 * a + 256)

    def narrow(a):
        return slice(128 * a, 128 * a + 128)

    group_of_lane = iota((E, 128), 1) >> 5

    def traces(ref, emit):
        for a in range(4):
            emit(0, a, tile(ref, a))
            emit(1, a, tile(ref, 12 + a))
            emit(2, a, tile(ref, 4 * a))
            emit(3, a, tile(ref, 4 * a + 3))
            first = tile(ref, 4 * a)
            last = pltpu.roll(tile(ref, 4 * a), 32, 1)
            for b in range(1, 4):
                node = tile(ref, 4 * a + b)
                first = jnp.where(group_of_lane == b, pltpu.roll(node, 32 * b, 1), first)
                moved = node if b == 3 else pltpu.roll(node, 32 * (b + 1), 1)
                last = jnp.where(group_of_lane == b, moved, last)
            emit(4, a, first)
            emit(5, a, last)

    def lift(ref, i, j):
        at = lambda f, a: ref[f * E : (f + 1) * E, narrow(a)]
        first, last = at(4, i), at(5, i)
        first = pltpu.roll(first, (128 - 32 * j) % 128, 1) if j else first
        last = pltpu.roll(last, 96 - 32 * j, 1) if j < 3 else last
        value = jnp.where(group_of_lane == 0, first, jnp.where(group_of_lane == 3, last, 0.0))
        if i == 0:
            value = value + at(0, j)
        if i == 3:
            value = value + at(1, j)
        if j == 0:
            value = value + at(2, i)
        if j == 3:
            value = value + at(3, i)
        return value

    def keep_traces(layer):
        def emit(f, a, value):
            h, l = split(value)
            rows = slice(f * E, (f + 1) * E)
            s.trace[rows, narrow(a)] = h
            s.trace[rows, slice(512 + 128 * a, 640 + 128 * a)] = l
            s.pair_nh[layer, rows, high(a)] = h
            s.pair_nl[layer, rows, high(a)] = l

        return emit

    def keep_gflux(masked):
        def emit(f, a, value):
            h, l = split(STEP_SIZE * value)
            rows = slice(f * E, (f + 1) * E)
            s.gflux[rows, high(a)] = h
            s.gflux[rows, low(a)] = l
            if masked:
                here = s.masks_n[rows, 384:512].astype(BF16)
                s.gflux_n[rows, high(a)] = h * here
                s.gflux_n[rows, low(a)] = l * here

        return emit

    def gathered(matrix, ref):
        both = dot(matrix[...], ref[...])
        return both[:, 0:512] + both[:, 512:1024]

    def volume_of(ref, layer, adjoint):
        for n in range(16):
            h, l = split(tile(ref, n))
            s.vol_x[n * E : (n + 1) * E, 0:128] = h
            s.vol_x[n * E : (n + 1) * E, 128:256] = l
        stacked, rest = (s.vts, s.vtl) if adjoint else (s.vs, s.vl)
        s.vol_y[...] = dot(s.vol_x[...], stacked[layer]) + dot(s.vol_x[:, 0:128], rest[layer])
        deriv = DERIV.T if adjoint else DERIV
        for i in range(4):
            for j in range(4):
                n = 4 * i + j
                value = s.vol_y[n * E : (n + 1) * E, 256:384]
                for o in range(4):
                    if abs(deriv[i, o]) > 1e-12:
                        at = 4 * o + j
                        value = value + float(deriv[i, o]) * s.vol_y[at * E : (at + 1) * E, 0:128]
                    if abs(deriv[j, o]) > 1e-12:
                        at = 4 * i + o
                        value = value + float(deriv[j, o]) * s.vol_y[at * E : (at + 1) * E, 128:256]
                s.volume[:, narrow(n)] = value

    def flip_lanes(x, odd):
        return jnp.where(odd, pltpu.roll(x, 96, 1), pltpu.roll(x, 32, 1))

    def swap(x, odd, upper):
        stage = [None] * 4
        for a in (0, 2):
            stage[a] = jnp.where(odd, pltpu.roll(x[a + 1], 32, 1), x[a])
            stage[a + 1] = jnp.where(odd, x[a + 1], pltpu.roll(x[a], 96, 1))
        out = [None] * 4
        for a in (0, 1):
            out[a] = jnp.where(upper, pltpu.roll(stage[a + 2], 64, 1), stage[a])
            out[a + 2] = jnp.where(upper, stage[a + 2], pltpu.roll(stage[a], 64, 1))
        return out

    def lane_masks(count_):
        groups = iota((count_, 128), 1) >> 5
        return (groups & 1) == 1, groups >= 2

    def oriented(x, marks):
        odd, upper = lane_masks(x[0].shape[0])
        first, second, swapped = marks
        x = [jnp.where(first, x[3 - a], x[a]) for a in range(4)]
        x = [jnp.where(second, flip_lanes(v, odd), v) for v in x]
        y = swap(x, odd, upper)
        return [jnp.where(swapped, y[a], x[a]) for a in range(4)]

    def turned_back(x, marks):
        odd, upper = lane_masks(x[0].shape[0])
        first, second, swapped = marks
        y = swap(x, odd, upper)
        x = [jnp.where(swapped, y[a], x[a]) for a in range(4)]
        x = [jnp.where(second, flip_lanes(v, odd), v) for v in x]
        return [jnp.where(first, x[3 - a], x[a]) for a in range(4)]

    def marks_of(ref, rows):
        return [ref[rows, narrow(m)] > 0.5 for m in range(3)]

    def each_rows(body):
        body(slice(0, FACES))

    def orient_near(layer):
        def body(rows):
            x = oriented([s.raw[rows, narrow(a)] for a in range(4)], marks_of(s.masks_n, rows))
            for a in range(4):
                s.pair_nh[layer, rows, low(a)], s.pair_nl[layer, rows, low(a)] = split(x[a])

        each_rows(body)

    def turn_back_near():
        def body(rows):
            x = turned_back([s.gout[rows, narrow(a)] for a in range(4)], marks_of(s.masks_n, rows))
            for a in range(4):
                h, l = split(x[a])
                s.turn[rows, narrow(a)] = h
                s.turn[rows, slice(512 + 128 * a, 640 + 128 * a)] = l

        each_rows(body)

    def each_a(body):
        for a in range(4):
            body(wide(a), high(a), narrow(a))

    def hidden(xh, xl, layer):
        pre = dot(xh, s.w1h[layer]) + dot(xl, s.w1h[layer]) + dot(xh, s.w1l[layer])
        return jnp.tanh(pre + s.bias[layer, 0:1, :])

    def flux_of(h, l, layer):
        both = dot(h, s.w2c[layer])
        return both[:, 0:128] + both[:, 128:256] + dot(l, s.w2c[layer, :, 0:128])

    def hidden_grad(both, top, layer):
        return dot(both, s.w2ts[layer]) + dot(top, s.w2tl[layer])

    def pair_grad(h, l, layer):
        return dot(h, s.w1th[layer]) + dot(l, s.w1th[layer]) + dot(h, s.w1tl[layer])

    def hidden_near(layer):
        def body(w, h_, n):
            value = hidden(s.pair_nh[layer, :, w], s.pair_nl[layer, :, w], layer)
            h, l = split(value)
            if layer == 1:
                s.slope[:, w] = 1.0 - value * value
            s.hid_nh[layer, :, w] = h
            s.hid_nl[layer, :, w] = l
            if layer == 0:
                s.flux[:, n] = flux_of(h, l, layer) * s.masks_n[:, 384:512]

        each_a(body)

    def back_near(layer, gflux):
        def body(w, h_, n):
            gp = hidden_grad(gflux[:, w], gflux[:, h_], layer) * s.slope[:, w]
            s.gpre_nh[:, w], s.gpre_nl[:, w] = split(gp)

        each_a(body)

    def back_pair(layer):
        def body(w, h_, n):
            both = pair_grad(s.gpre_nh[:, w], s.gpre_nl[:, w], layer)
            s.gin[:, n] = both[:, 0:128]
            s.gout[:, n] = both[:, 128:256]

        each_a(body)

    def far_pairs(which, layer):
        def step(pair):
            rows = pl.ds(64 * pair, 64)
            all_of(which, pair).wait_recv()
            for side in range(2):
                part_rows = pl.ds(64 * pair + CAP * side, CAP)
                x = oriented([s.got[which, part_rows, narrow(a)] for a in range(4)], marks_of(s.masks_f, part_rows))
                for a in range(4):
                    s.pair_fh[layer, part_rows, low(a)], s.pair_fl[layer, part_rows, low(a)] = split(x[a])
            stack = lambda ref, cut: jnp.concatenate([ref[rows, cut(a)] for a in range(4)], axis=0)
            value = hidden(stack(s.pair_fh.at[layer], wide), stack(s.pair_fl.at[layer], wide), layer)
            h, l = split(value)
            part_of = lambda v, a: v[64 * a : 64 * a + 64]
            for a in range(4):
                s.hid_fh[layer, rows, wide(a)] = part_of(h, a)
                s.hid_fl[layer, rows, wide(a)] = part_of(l, a)
            if layer == 0:
                fh, fl = split(flux_of(h, l, layer))
                for a in range(4):
                    s.flux_fh[rows, narrow(a)] = part_of(fh, a)
                    s.flux_fl[rows, narrow(a)] = part_of(fl, a)
            else:
                gh, gl = split(stack(s.ghid_f, wide) * (1.0 - value * value))
                both = pair_grad(gh, gl, layer)
                ih, il = split(both[:, 0:128])
                for a in range(4):
                    s.gpre_fh[rows, wide(a)] = part_of(gh, a)
                    s.gpre_fl[rows, wide(a)] = part_of(gl, a)
                    s.gin_fh[rows, narrow(a)] = part_of(ih, a)
                    s.gin_fl[rows, narrow(a)] = part_of(il, a)
                for side in range(2):
                    part_rows = pl.ds(64 * pair + CAP * side, CAP)
                    cut = lambda a: both[64 * a + CAP * side : 64 * a + CAP * side + CAP, 128:256]
                    x = turned_back([cut(a) for a in range(4)], marks_of(s.masks_f, part_rows))
                    for a in range(4):
                        s.sent[which + 1, part_rows, narrow(a)] = x[a]
                for side in range(2):
                    far_copy(which + 1, pair, side, -1).start()

        for pair in (3, 2, 1, 0):
            step(pair)

    def far_inner(layer):
        both = dot(s.rem_t[...], s.trace[...]).astype(BF16)
        for a in range(4):
            s.pair_fh[layer, :, high(a)] = both[:, narrow(a)]
            s.pair_fl[layer, :, high(a)] = both[:, 512 + 128 * a : 640 + 128 * a]

    def weight_grads(parts):
        rows_of = lambda ref, cut: jnp.concatenate([ref[:, cut(a)] for a in range(4)], axis=0)
        xh, xl, gph, gpl, hh, hl, g = parts
        gh, gl, x = rows_of(gph, wide), rows_of(gpl, wide), rows_of(xh, wide)
        one = dot_tn(x, gh) + dot_tn(rows_of(xl, wide), gh) + dot_tn(x, gl)
        two = dot_tn(rows_of(hh, wide), rows_of(g, wide))
        top = dot_tn(rows_of(hl, wide), rows_of(g, high))
        two = two[:, 0:128] + two[:, 128:256] + top
        row = jnp.sum(gh.astype(F32) + gl.astype(F32), axis=0, keepdims=True)
        return one, two, row

    def pack_grads(layer, one, two, row):
        r, c = iota((256, 256), 0), iota((256, 256), 1)
        one = jnp.where(((r >> 5) & 3) == (c >> 6), one, 0.0)
        one = one[:, 0:128] + one[:, 128:256]
        one = one + pltpu.roll(one, 64, 1)
        halves = [sum(one[128 * half + 32 * b : 128 * half + 32 * b + 32] for b in range(4)) for half in range(2)]
        one = jnp.concatenate(halves, axis=0)
        r, c = iota((256, 128), 0), iota((256, 128), 1)
        two = jnp.where((r >> 6) == (c >> 5), two, 0.0)
        two = sum(two[64 * b : 64 * b + 64] for b in range(4))
        two = two + pltpu.roll(two, 64, 1)
        two = two + pltpu.roll(two, 32, 1)
        row = row[:, 0:128] + row[:, 128:256]
        row = row + pltpu.roll(row, 64, 1)
        r, c = iota((64, 128), 0), iota((64, 128), 1)
        column = jnp.sum(jnp.where(r == c, row, 0.0), axis=1, keepdims=True)
        value = jnp.where(c < 64, one, jnp.where(c < 96, two, jnp.where(c == 96, column, 0.0)))
        s.packed[layer] = value

    def piece(j):
        return pl.ds(pl.multiple_of(j * 8, 8), 8)

    def remote(src, dst, sems, device):
        return pltpu.make_async_remote_copy(
            src_ref=src, dst_ref=dst, send_sem=sems[0], recv_sem=sems[1], device_id=(device,), device_id_type=MESH
        )

    def sems(layer, stage):
        return s.ar_send.at[layer, stage], s.ar_recv.at[layer, stage]

    def scatter(layer):
        return [
            remote(s.packed.at[layer, piece(lax.rem(mine + t, group))], s.part.at[layer, mine], sems(layer, 0), in_group(t))
            for t in range(1, group)
        ]

    def spread(layer):
        here = s.part_sum.at[layer, rank]
        return [remote(here, here, sems(layer, 1), across(t)) for t in range(1, others)]

    def collect(layer):
        here, there = s.total_v.at[layer, piece(mine)], s.total.at[layer, piece(mine)]
        return [remote(here, there, sems(layer, 2), in_group(t)) for t in range(1, group)]

    def stage_bytes(layer, stage):
        here = (
            s.part.at[layer, pl.ds(0, group - 1)],
            s.part_sum.at[layer, pl.ds(0, others - 1)],
            s.total.at[layer, pl.ds(0, 8 * (group - 1))],
        )[stage]
        return remote(here, here, sems(layer, stage), in_group(1))

    def start(copies):
        for copy in copies:
            copy.start()

    def reduce_start(layer):
        start(scatter(layer))
        s.part[layer, mine] = s.packed[layer, piece(mine), :]

    def reduce_middle(layer):
        stage_bytes(layer, 0).wait()
        value = s.part[layer, 0]
        for t in range(1, group):
            value = value + s.part[layer, t]
        s.part_sum[layer, rank] = value
        start(spread(layer))

    def push_piece(layer):
        return pltpu.make_async_copy(
            s.total_v.at[layer, piece(mine)], s.total.at[layer, piece(mine)], s.out_sem.at[1 + layer]
        )

    def reduce_last(layer):
        stage_bytes(layer, 1).wait()
        value = s.part_sum[layer, 0]
        for t in range(1, others):
            value = value + s.part_sum[layer, t]
        s.total_v[layer, piece(mine), :] = value
        start(collect(layer))
        push_piece(layer).start()

    with jax.named_scope("send_table"):
        order = (0, 4, 1, 5, 2, 6, 3, 7)
        pulls["send"].wait()
        row = s.send_v[...]
        row = jnp.concatenate([row[:, CAP * b : CAP * b + CAP] for b in order], axis=1)
        for f in range(6):
            s.sel_t[f * E : (f + 1) * E, :] = ones_where(6 * iota((E, SLOTS), 0) + f == row, BF16)
        eye = ones_where(iota((SLOTS, SLOTS), 0) == iota((SLOTS, SLOTS), 1), BF16)
        s.sel[...] = dot_nt(eye, s.sel_t[...]).astype(BF16)

    with jax.named_scope("field0"):
        pulls["state"].wait()
        pulls["live"].wait()
        alive = iota((E, 128), 0) < s.live_v[0]
        for n in range(16):
            s.field[:, narrow(n)] = jnp.where(alive, tile(s.state_v, n), 0.0)
        traces(s.field, keep_traces(0))
    far_half, close_half = slice(128, 256), slice(0, 128)
    with jax.named_scope("pack0"):
        s.sent[0, far_half] = gathered(s.sel.at[far_half], s.trace)
    with jax.named_scope("barrier"):
        pl.semaphore_wait(barrier, len(partners))
    send_all(0, 1, (3, 2))
    with jax.named_scope("pack0b"):
        s.sent[0, close_half] = gathered(s.sel.at[close_half], s.trace)
    send_all(0, 1, (1, 0))

    with jax.named_scope("tables"):
        for f in range(6):
            s.raw[f * E : (f + 1) * E, 0:FACES] = ones_where(6 * iota((E, FACES), 0) + f == iota((E, FACES), 1))
        by_kind = s.raw[:, 0:FACES].astype(BF16)
        pulls["src"].wait()
        source = s.src_v[...].reshape(1, FACES)
        near = jnp.concatenate([ones_where(6 * iota((E, FACES), 0) + f == source, BF16) for f in range(6)], axis=0)
        slot = iota((SLOTS, FACES), 0)
        slot = ((slot >> 5) & 1) * 128 + (slot >> 6) * CAP + (slot & 31)
        far = ones_where(slot + FACES == source, BF16)
        s.loc_t[...] = dot_nt(near, by_kind).astype(BF16)
        s.loc[...] = dot_nt(by_kind, near).astype(BF16)
        s.rem_t[...] = dot_nt(far, by_kind).astype(BF16)
        s.rem[...] = dot_nt(by_kind, far).astype(BF16)
        pulls["orient"].wait()
        turn = s.orient_v[...].reshape(1, FACES)
        flags = [(turn >> 1) & 1, (turn ^ (turn >> 1)) & 1, (turn ^ (turn >> 2)) & 1, jnp.where(source < FACES, 1, 0)]
        for m in range(MASKS):
            spread_out = jnp.broadcast_to(flags[m], (128, FACES)).astype(F32).astype(BF16)
            s.masks_n[:, narrow(m)] = dot_nt(by_kind, spread_out)
            s.masks_f[:, narrow(m)] = dot_nt(far, spread_out)

    def four(x):
        x = jnp.concatenate([x] * 4, axis=1)
        return jnp.concatenate([x] * 4, axis=0)

    def flux_weights(layer):
        r, c = iota((256, 256), 0), iota((256, 256), 1)
        w1 = s.w1_v[layer]
        big = jnp.concatenate([four(w1[0:32]), four(w1[32:64])], axis=0)
        big = jnp.where(((r >> 5) & 3) == (c >> 6), big, 0.0)
        s.w1h[layer], s.w1l[layer] = split(big)
        s.w1th[layer], s.w1tl[layer] = split(big.T)
        r, c = iota((128, 256), 0), iota((128, 256), 1)
        big = jnp.where((r >> 5) == (c >> 6), four(s.w2t_v[layer]), 0.0)
        h, l = split(big)
        s.w2ts[layer, 0:128] = h
        s.w2ts[layer, 128:256] = h
        s.w2tl[layer] = l
        h, l = split(big.T)
        s.w2c[layer, :, 0:128] = h
        s.w2c[layer, :, 128:256] = l
        bias = jnp.concatenate([s.b1_v[layer : layer + 1, :]] * 4, axis=1)
        s.bias[layer] = jnp.broadcast_to(bias, (8, 256))

    def volume_weights(layer):
        r, c = iota((128, 128), 0), iota((128, 128), 1)
        for axis in range(3):
            big = four(s.vol_v[layer, axis])
            big = jnp.where((r >> 5) == (c >> 5), big, 0.0) if axis < 2 else big * s.deriv_v[...]
            for value, stacked, rest in ((big, s.vs, s.vl), (big.T, s.vts, s.vtl)):
                h, l = split(value)
                stacked[layer, 0:128, narrow(axis)] = h
                stacked[layer, 128:256, narrow(axis)] = h
                rest[layer, :, narrow(axis)] = l

    with jax.named_scope("weights0"):
        for name in ("w1", "w2t", "b1", "vol", "deriv"):
            pulls[name].wait()
        flux_weights(0)
        volume_weights(0)
    with jax.named_scope("near0"):
        s.raw[...] = gathered(s.loc, s.trace)
        far_inner(0)
    with jax.named_scope("orient0"):
        orient_near(0)
    with jax.named_scope("hidden0"):
        hidden_near(0)
    with jax.named_scope("volume0"):
        volume_of(s.field, 0, False)
    with jax.named_scope("weights1"):
        flux_weights(1)
    with jax.named_scope("cotangent"):
        pulls["cot"].wait()
        traces(s.cot_v, keep_gflux(True))
    with jax.named_scope("far0"):
        far_pairs(0, 0)
    with jax.named_scope("field1"):
        s.flux[...] += dot(s.rem[...], s.flux_fh[...]) + dot(s.rem[...], s.flux_fl[...])
        for n in range(16):
            s.field[:, narrow(n)] += STEP_SIZE * (lift(s.flux, n // 4, n % 4) - s.volume[:, narrow(n)])
        traces(s.field, keep_traces(1))
    with jax.named_scope("pack1"):
        s.sent[1, far_half] = gathered(s.sel.at[far_half], s.trace)
    send_all(1, 1, (3, 2))
    with jax.named_scope("pack1b"):
        s.sent[1, close_half] = gathered(s.sel.at[close_half], s.trace)
    send_all(1, 1, (1, 0))
    with jax.named_scope("cotangent_far"):
        s.gflux_f[...] = dot(s.rem_t[...], s.gflux[...]).astype(BF16)
        for a in range(4):
            s.ghid_f[:, wide(a)] = hidden_grad(s.gflux_f[:, wide(a)], s.gflux_f[:, high(a)], 1)
    with jax.named_scope("near1"):
        s.raw[...] = gathered(s.loc, s.trace)
        far_inner(1)
    with jax.named_scope("orient1"):
        orient_near(1)
    with jax.named_scope("hidden1"):
        hidden_near(1)
    with jax.named_scope("back1"):
        back_near(1, s.gflux_n)
        back_pair(1)
    with jax.named_scope("whole0"):
        for far, here in ((s.pair_fh, s.pair_nh), (s.pair_fl, s.pair_nl)):
            value = dot(s.rem[...], jnp.concatenate([far[0, :, low(a)] for a in range(4)], axis=1)).astype(BF16)
            for a in range(4):
                here[0, :, low(a)] += value[:, narrow(a)]
        for far, here in ((s.hid_fh, s.hid_nh), (s.hid_fl, s.hid_nl)):
            for a in range(4):
                own = s.masks_n[:, 384:512].astype(BF16)
                value = dot(s.rem[...], far[0, :, wide(a)]).astype(BF16)
                here[0, :, wide(a)] = here[0, :, wide(a)] * jnp.concatenate([own, own], axis=1) + value
    with jax.named_scope("weight_grads1_near"):
        parts = s.pair_nh.at[1], s.pair_nl.at[1], s.gpre_nh, s.gpre_nl, s.hid_nh.at[1], s.hid_nl.at[1], s.gflux_n
        s.one[...], s.two[...], row = weight_grads(parts)
        s.row[...] = jnp.broadcast_to(row, (8, 256))
    with jax.named_scope("far1"):
        far_pairs(1, 1)

    with jax.named_scope("turn1"):
        turn_back_near()
    with jax.named_scope("scatter1"):
        both = dot(s.loc_t[...], s.turn[...])
        value = both[:, 0:512] + both[:, 512:1024]
        s.gin[...] += value + dot(s.rem[...], s.gin_fh[...]) + dot(s.rem[...], s.gin_fl[...])
    with jax.named_scope("volume1"):
        volume_weights(1)
        volume_of(s.cot_v, 1, True)
    with jax.named_scope("weight_grads1"):
        parts = s.pair_fh.at[1], s.pair_fl.at[1], s.gpre_fh, s.gpre_fl, s.hid_fh.at[1], s.hid_fl.at[1], s.gflux_f
        one, two, row = weight_grads(parts)
        pack_grads(1, one + s.one[...], two + s.two[...], row + s.row[0:1, :])
        reduce_start(1)
    with jax.named_scope("slope0"):
        for a in range(4):
            h = s.hid_nh[0, :, wide(a)].astype(F32) + s.hid_nl[0, :, wide(a)].astype(F32)
            s.slope[:, wide(a)] = 1.0 - h * h
    with jax.named_scope("wait2"):
        all_of(2).wait_recv()
    with jax.named_scope("grad1"):
        h, l = split(s.got[2])
        s.gin[...] += dot(s.sel_t[...], h) + dot(s.sel_t[...], l)
        for n in range(16):
            s.grad[:, narrow(n)] = tile(s.cot_v, n) - STEP_SIZE * s.volume[:, narrow(n)] + lift(s.gin, n // 4, n % 4)
        traces(s.grad, keep_gflux(False))
    with jax.named_scope("back0"):
        back_near(0, s.gflux)
    with jax.named_scope("weight_grads0"):
        parts = s.pair_nh.at[0], s.pair_nl.at[0], s.gpre_nh, s.gpre_nl, s.hid_nh.at[0], s.hid_nl.at[0], s.gflux
        pack_grads(0, *weight_grads(parts))
        reduce_start(0)
    with jax.named_scope("sum1a"):
        reduce_middle(1)
    with jax.named_scope("back0_pair"):
        back_pair(0)
    with jax.named_scope("turn0"):
        turn_back_near()
    with jax.named_scope("pack3"):
        s.sent[3, far_half] = gathered(s.rem_t.at[far_half], s.turn)
    send_all(3, -1, (3,))
    with jax.named_scope("pack3b"):
        s.sent[3, close_half] = gathered(s.rem_t.at[close_half], s.turn)
    with jax.named_scope("sum0a"):
        reduce_middle(0)
    send_all(3, -1, (2, 1, 0))
    with jax.named_scope("scatter0"):
        both = dot(s.loc_t[...], s.turn[...])
        s.gin[...] += both[:, 0:512] + both[:, 512:1024]
    with jax.named_scope("volume0b"):
        volume_of(s.grad, 0, True)
    with jax.named_scope("sum1b"):
        reduce_last(1)
    with jax.named_scope("sum0b"):
        reduce_last(0)
    with jax.named_scope("wait3"):
        all_of(3).wait_recv()
    with jax.named_scope("grad0"):
        h, l = split(s.got[3])
        s.gin[...] += dot(s.sel_t[...], h) + dot(s.sel_t[...], l)
        for n in range(16):
            value = s.grad[:, narrow(n)] - STEP_SIZE * s.volume[:, narrow(n)] + lift(s.gin, n // 4, n % 4)
            s.out_v[:, narrow(n)] = jnp.where(alive, value, 0.0)
        push = pltpu.make_async_copy(s.out_v, s.out, s.out_sem.at[0])
        push.start()
    with jax.named_scope("sumc"):
        stage_bytes(1, 2).wait()
        stage_bytes(0, 2).wait()
    with jax.named_scope("sent"):
        for which in (0, 1):
            drain = pltpu.make_async_copy(s.sent.at[which], s.sent.at[which], s.send_sem.at[which])
            drain.wait()
        all_of(2).wait_send()
        all_of(3).wait_send()
        push.wait()
        push_piece(1).wait()
        push_piece(0).wait()


def finish(factor, total_ref, field_ref, out_ref, w1_ref, b1_ref, w2t_ref):
    out_ref[...] = field_ref[...]
    for layer in range(2):
        value = total_ref[layer] * factor
        w1_ref[layer] = value[:, 0:64]
        w2t_ref[layer] = value.T[64:96, :]
        b1_ref[layer : layer + 1, :] = value.T[96:97, :]


def local(count, state, cotangent, elem_count, face_src, face_orient, send_face, vol_weight, w1, b1, w2):
    constant = np.zeros((128, 128), np.float32)
    for a in range(4):
        for k in range(4):
            constant[32 * k : 32 * k + 32, 32 * a : 32 * a + 32] = DERIV[a, k]
    vmem = pl.BlockSpec(memory_space=pltpu.VMEM)
    smem = pl.BlockSpec(memory_space=pltpu.SMEM)
    hbm = pl.BlockSpec(memory_space=pl.ANY)
    names = [*INPUTS, *OUTPUTS, *SCRATCH]
    scratch = [pltpu.VMEM(shape, dtype) for shape, dtype in SCRATCH.values()]
    extra = dict(
        part_sum=pltpu.VMEM((2, count // 8, 8, 128), F32),
        total_v=pltpu.VMEM((2, 64, 128), F32),
        live_v=pltpu.SMEM((1,), I32),
        out_sem=pltpu.SemaphoreType.DMA((3,)),
        in_sem=pltpu.SemaphoreType.DMA((11,)),
        send_sem=pltpu.SemaphoreType.DMA((4,)),
        near_sem=pltpu.SemaphoreType.DMA((2, NEIGH)),
        back_sem=pltpu.SemaphoreType.DMA((2,)),
        ar_send=pltpu.SemaphoreType.DMA((2, 3)),
        ar_recv=pltpu.SemaphoreType.DMA((2, 3)),
    )
    names += list(extra)
    scratch += list(extra.values())
    field, total = pl.pallas_call(
        functools.partial(kernel, count, names),
        out_shape=(jax.ShapeDtypeStruct(state.shape, F32), jax.ShapeDtypeStruct((2, 64, 128), F32)),
        in_specs=[hbm, hbm, hbm, hbm, hbm, hbm] + [hbm] * 5,
        out_specs=[hbm] * 2,
        scratch_shapes=scratch,
        compiler_params=pltpu.CompilerParams(
            collective_id=0, has_side_effects=True, vmem_limit_bytes=VMEM_LIMIT
        ),
    )(
        state, cotangent, elem_count, face_src, face_orient,
        send_face.reshape(1, -1), vol_weight, w1, b1, jnp.swapaxes(w2, 1, 2), jnp.asarray(constant),
    )
    factor = (2.0 * FACES * 8 * count) ** -0.5
    grad, grad_w1, grad_b1, grad_w2t = pl.pallas_call(
        functools.partial(finish, factor),
        out_shape=(
            jax.ShapeDtypeStruct(state.shape, F32),
            jax.ShapeDtypeStruct(w1.shape, F32),
            jax.ShapeDtypeStruct(b1.shape, F32),
            jax.ShapeDtypeStruct((2, 32, 64), F32),
        ),
        in_specs=[vmem] * 2,
        out_specs=[vmem] * 4,
    )(total, field)
    return grad, grad_w1, grad_b1, jnp.swapaxes(grad_w2t, 1, 2)


def solution(mesh):
    rows, flat, whole = P("dom", None), P("dom"), P()
    return jax.shard_map(
        functools.partial(local, mesh.shape["dom"]),
        mesh=mesh,
        in_specs=(rows, rows, flat, flat, flat, flat, whole, whole, whole, whole),
        out_specs=(rows, whole, whole, whole),
        check_vma=False,
    )
```

```python
import functools
import types

import jax
import jax.numpy as jnp
import numpy as np
from jax import lax
from jax.experimental import pallas as pl
from jax.experimental.pallas import tpu as pltpu
from jax.sharding import PartitionSpec as P

MESH = pl.DeviceIdType.MESH
HIGHEST = lax.Precision.HIGHEST
F32 = jnp.float32
BF16 = jnp.bfloat16
I32 = jnp.int32
NEIGH = 4
BLOCKS = 2 * NEIGH
CAP = 32
SLOTS = BLOCKS * CAP
STEP_SIZE = 0.25
E = 48
FACES = 6 * E
OFFSETS = [level + 1 for level in range(NEIGH)] + [-(level + 1) for level in range(NEIGH)]


VMEM_LIMIT = 56 * 1024 * 1024


def deriv_matrix():
    points = np.array([-1.0, -np.sqrt(0.2), np.sqrt(0.2), 1.0])
    weights = np.array(
        [np.prod([points[r] - points[o] for o in range(4) if o != r]) for r in range(4)]
    )
    matrix = np.zeros((4, 4))
    for r in range(4):
        for c in range(4):
            if r != c:
                matrix[r, c] = weights[r] / weights[c] / (points[r] - points[c])
        matrix[r, r] = -np.sum(matrix[r])
    return matrix


DERIV = deriv_matrix()


def iota(shape, dim):
    return lax.broadcasted_iota(I32, shape, dim)


def dot(a, b):
    return jnp.dot(a, b, preferred_element_type=F32)


def dot_nt(a, b):
    return lax.dot_general(a, b, (((1,), (1,)), ((), ())), preferred_element_type=F32)


def dot_tn(a, b):
    return lax.dot_general(a, b, (((0,), (0,)), ((), ())), preferred_element_type=F32)


def dot_full(a, b):
    return jnp.dot(a, b, preferred_element_type=F32, precision=HIGHEST)


def split(x):
    high = x.astype(BF16)
    return high, (x - high.astype(F32)).astype(BF16)


def three(op, a, b):
    return op(a[0], b[0]) + op(a[1], b[0]) + op(a[0], b[1])


def lanes(a):
    return pl.ds(pl.multiple_of(a * 128, 128), 128)


def ones_where(match, dtype=F32):
    return jnp.where(match, 1.0, 0.0).astype(dtype)


MASKS = 4

INPUTS = ("state", "cot", "live", "src", "orient", "send", "vol", "w1", "b1", "w2t", "deriv")
OUTPUTS = ("out", "total")
SCRATCH = dict(
    src_v=((FACES,), I32), orient_v=((FACES,), I32), send_v=((1, SLOTS), I32), state_v=((E, 2048), F32), cot_v=((E, 2048), F32),
    vol_v=((2, 3, 32, 32), F32), w1_v=((2, 64, 64), F32), b1_v=((2, 64), F32), w2t_v=((2, 32, 64), F32), deriv_v=((128, 128), F32),
    out_v=((E, 2048), F32), field=((E, 2048), F32), grad=((E, 2048), F32), volume=((E, 2048), F32),
    vol_y=((16 * E, 384), F32), vol_x=((16 * E, 256), BF16),
    trace=((FACES, 1024), BF16), raw=((FACES, 512), F32),
    pair_nh=((2, FACES, 1024), BF16), pair_nl=((2, FACES, 1024), BF16), pair_fh=((2, SLOTS, 1024), BF16), pair_fl=((2, SLOTS, 1024), BF16),
    hid_nh=((2, FACES, 1024), BF16), hid_nl=((2, FACES, 1024), BF16), hid_fh=((2, SLOTS, 1024), BF16), hid_fl=((2, SLOTS, 1024), BF16),
    flux=((FACES, 512), F32), flux_fh=((SLOTS, 512), BF16), flux_fl=((SLOTS, 512), BF16),
    gflux=((FACES, 1024), BF16), gflux_n=((FACES, 1024), BF16), gflux_f=((SLOTS, 1024), BF16), ghid_f=((SLOTS, 1024), F32),
    gpre_nh=((FACES, 1024), BF16), gpre_nl=((FACES, 1024), BF16), gpre_fh=((SLOTS, 1024), BF16), gpre_fl=((SLOTS, 1024), BF16),
    gin=((FACES, 512), F32), gin_fh=((SLOTS, 512), BF16), gin_fl=((SLOTS, 512), BF16), gout=((FACES, 512), F32),
    turn=((FACES, 1024), BF16),
    sel=((SLOTS, FACES), BF16), sel_t=((FACES, SLOTS), BF16), loc=((FACES, FACES), BF16), loc_t=((FACES, FACES), BF16),
    rem=((FACES, SLOTS), BF16), rem_t=((SLOTS, FACES), BF16),
    masks_n=((FACES, MASKS * 128), F32), masks_f=((SLOTS, MASKS * 128), F32),
    w1h=((2, 256, 256), BF16), w1l=((2, 256, 256), BF16), w1th=((2, 256, 256), BF16), w1tl=((2, 256, 256), BF16),
    w2c=((2, 256, 256), BF16), w2ts=((2, 256, 256), BF16), w2tl=((2, 128, 256), BF16),
    vs=((2, 256, 384), BF16), vl=((2, 128, 384), BF16), vts=((2, 256, 384), BF16), vtl=((2, 128, 384), BF16), bias=((2, 8, 256), F32),
    sent=((4, SLOTS, 512), F32), got=((4, SLOTS, 512), F32),
    slope=((FACES, 1024), F32),
    one=((256, 256), F32), two=((256, 128), F32), row=((8, 256), F32),
    packed=((2, 64, 128), F32), part=((2, 8, 8, 128), F32),
)


def kernel(count, names, *refs):
    s = types.SimpleNamespace(**dict(zip(names, refs, strict=True)))
    me = lax.axis_index("dom")
    group = 8
    others = count // group
    base = (me // group) * group
    mine = lax.rem(me, group)
    rank = me // group

    def neighbour(offset):
        return lax.rem(me + offset + count, count)

    def in_group(step):
        return base + lax.rem(mine + step, group)

    def across(step):
        return lax.rem(rank + step, others) * group + mine

    barrier = pltpu.get_barrier_semaphore()
    partners = [neighbour(o) for o in OFFSETS]
    partners += [in_group(step) for step in range(1, group)]
    partners += [across(step) for step in range(1, others)]
    pulls = {}
    for n, name in enumerate(("send", "state", "live", "src", "orient", "vol", "w1", "b1", "w2t", "deriv", "cot")):
        pulls[name] = pltpu.make_async_copy(getattr(s, name), getattr(s, name + "_v"), s.in_sem.at[n])
        pulls[name].start()
    for device in partners:
        pl.semaphore_signal(barrier, inc=1, device_id=(device,), device_id_type=MESH)

    def far_copy(which, pair, side, sign):
        rows = pl.ds(64 * pair + CAP * side, CAP)
        offset = (pair + 1) * (sign if side == 0 else -sign)
        return pltpu.make_async_remote_copy(
            src_ref=s.sent.at[which, rows],
            dst_ref=s.got.at[which, rows],
            send_sem=s.send_sem.at[which],
            recv_sem=s.near_sem.at[which, pair] if which < 2 else s.back_sem.at[which - 2],
            device_id=(neighbour(offset),),
            device_id_type=MESH,
        )

    def send_all(which, sign, pairs=(3, 2, 1, 0)):
        for pair in pairs:
            for side in range(2):
                far_copy(which, pair, side, sign).start()

    def all_of(which, pair=None):
        rows = pl.ds(0, SLOTS) if pair is None else pl.ds(64 * pair, 64)
        return pltpu.make_async_remote_copy(
            src_ref=s.sent.at[which, rows],
            dst_ref=s.got.at[which, rows],
            send_sem=s.send_sem.at[which],
            recv_sem=s.near_sem.at[which, pair] if which < 2 else s.back_sem.at[which - 2],
            device_id=(neighbour(1),),
            device_id_type=MESH,
        )

    def tile(ref, n):
        return ref[:, n * 128 : (n + 1) * 128]

    def wide(a):
        return slice(256 * a, 256 * a + 256)

    def high(a):
        return slice(256 * a, 256 * a + 128)

    def low(a):
        return slice(256 * a + 128, 256 * a + 256)

    def narrow(a):
        return slice(128 * a, 128 * a + 128)

    group_of_lane = iota((E, 128), 1) >> 5

    def traces(ref, emit):
        for a in range(4):
            emit(0, a, tile(ref, a))
            emit(1, a, tile(ref, 12 + a))
            emit(2, a, tile(ref, 4 * a))
            emit(3, a, tile(ref, 4 * a + 3))
            first = tile(ref, 4 * a)
            last = pltpu.roll(tile(ref, 4 * a), 32, 1)
            for b in range(1, 4):
                node = tile(ref, 4 * a + b)
                first = jnp.where(group_of_lane == b, pltpu.roll(node, 32 * b, 1), first)
                moved = node if b == 3 else pltpu.roll(node, 32 * (b + 1), 1)
                last = jnp.where(group_of_lane == b, moved, last)
            emit(4, a, first)
            emit(5, a, last)

    def lift(ref, i, j):
        at = lambda f, a: ref[f * E : (f + 1) * E, narrow(a)]
        first, last = at(4, i), at(5, i)
        first = pltpu.roll(first, (128 - 32 * j) % 128, 1) if j else first
        last = pltpu.roll(last, 96 - 32 * j, 1) if j < 3 else last
        value = jnp.where(group_of_lane == 0, first, jnp.where(group_of_lane == 3, last, 0.0))
        if i == 0:
            value = value + at(0, j)
        if i == 3:
            value = value + at(1, j)
        if j == 0:
            value = value + at(2, i)
        if j == 3:
            value = value + at(3, i)
        return value

    def keep_traces(layer):
        def emit(f, a, value):
            h, l = split(value)
            rows = slice(f * E, (f + 1) * E)
            s.trace[rows, narrow(a)] = h
            s.trace[rows, slice(512 + 128 * a, 640 + 128 * a)] = l
            s.pair_nh[layer, rows, high(a)] = h
            s.pair_nl[layer, rows, high(a)] = l

        return emit

    def keep_gflux(masked):
        def emit(f, a, value):
            h, l = split(STEP_SIZE * value)
            rows = slice(f * E, (f + 1) * E)
            s.gflux[rows, high(a)] = h
            s.gflux[rows, low(a)] = l
            if masked:
                here = s.masks_n[rows, 384:512].astype(BF16)
                s.gflux_n[rows, high(a)] = h * here
                s.gflux_n[rows, low(a)] = l * here

        return emit

    def gathered(matrix, ref):
        both = dot(matrix[...], ref[...])
        return both[:, 0:512] + both[:, 512:1024]

    def volume_of(ref, layer, adjoint):
        for n in range(16):
            h, l = split(tile(ref, n))
            s.vol_x[n * E : (n + 1) * E, 0:128] = h
            s.vol_x[n * E : (n + 1) * E, 128:256] = l
        stacked, rest = (s.vts, s.vtl) if adjoint else (s.vs, s.vl)
        s.vol_y[...] = dot(s.vol_x[...], stacked[layer]) + dot(s.vol_x[:, 0:128], rest[layer])
        deriv = DERIV.T if adjoint else DERIV
        for i in range(4):
            for j in range(4):
                n = 4 * i + j
                value = s.vol_y[n * E : (n + 1) * E, 256:384]
                for o in range(4):
                    if abs(deriv[i, o]) > 1e-12:
                        at = 4 * o + j
                        value = value + float(deriv[i, o]) * s.vol_y[at * E : (at + 1) * E, 0:128]
                    if abs(deriv[j, o]) > 1e-12:
                        at = 4 * i + o
                        value = value + float(deriv[j, o]) * s.vol_y[at * E : (at + 1) * E, 128:256]
                s.volume[:, narrow(n)] = value

    def flip_lanes(x, odd):
        return jnp.where(odd, pltpu.roll(x, 96, 1), pltpu.roll(x, 32, 1))

    def swap(x, odd, upper):
        stage = [None] * 4
        for a in (0, 2):
            stage[a] = jnp.where(odd, pltpu.roll(x[a + 1], 32, 1), x[a])
            stage[a + 1] = jnp.where(odd, x[a + 1], pltpu.roll(x[a], 96, 1))
        out = [None] * 4
        for a in (0, 1):
            out[a] = jnp.where(upper, pltpu.roll(stage[a + 2], 64, 1), stage[a])
            out[a + 2] = jnp.where(upper, stage[a + 2], pltpu.roll(stage[a], 64, 1))
        return out

    def lane_masks(count_):
        groups = iota((count_, 128), 1) >> 5
        return (groups & 1) == 1, groups >= 2

    def oriented(x, marks):
        odd, upper = lane_masks(x[0].shape[0])
        first, second, swapped = marks
        x = [jnp.where(first, x[3 - a], x[a]) for a in range(4)]
        x = [jnp.where(second, flip_lanes(v, odd), v) for v in x]
        y = swap(x, odd, upper)
        return [jnp.where(swapped, y[a], x[a]) for a in range(4)]

    def turned_back(x, marks):
        odd, upper = lane_masks(x[0].shape[0])
        first, second, swapped = marks
        y = swap(x, odd, upper)
        x = [jnp.where(swapped, y[a], x[a]) for a in range(4)]
        x = [jnp.where(second, flip_lanes(v, odd), v) for v in x]
        return [jnp.where(first, x[3 - a], x[a]) for a in range(4)]

    def marks_of(ref, rows):
        return [ref[rows, narrow(m)] > 0.5 for m in range(3)]

    def each_rows(body):
        body(slice(0, FACES))

    def orient_near(layer):
        def body(rows):
            x = oriented([s.raw[rows, narrow(a)] for a in range(4)], marks_of(s.masks_n, rows))
            for a in range(4):
                s.pair_nh[layer, rows, low(a)], s.pair_nl[layer, rows, low(a)] = split(x[a])

        each_rows(body)

    def turn_back_near():
        def body(rows):
            x = turned_back([s.gout[rows, narrow(a)] for a in range(4)], marks_of(s.masks_n, rows))
            for a in range(4):
                h, l = split(x[a])
                s.turn[rows, narrow(a)] = h
                s.turn[rows, slice(512 + 128 * a, 640 + 128 * a)] = l

        each_rows(body)

    def each_a(body):
        for a in range(4):
            body(wide(a), high(a), narrow(a))

    def hidden(xh, xl, layer):
        pre = dot(xh, s.w1h[layer]) + dot(xl, s.w1h[layer]) + dot(xh, s.w1l[layer])
        return jnp.tanh(pre + s.bias[layer, 0:1, :])

    def flux_of(h, l, layer):
        both = dot(h, s.w2c[layer])
        return both[:, 0:128] + both[:, 128:256] + dot(l, s.w2c[layer, :, 0:128])

    def hidden_grad(both, top, layer):
        return dot(both, s.w2ts[layer]) + dot(top, s.w2tl[layer])

    def pair_grad(h, l, layer):
        return dot(h, s.w1th[layer]) + dot(l, s.w1th[layer]) + dot(h, s.w1tl[layer])

    def hidden_near(layer):
        def body(w, h_, n):
            value = hidden(s.pair_nh[layer, :, w], s.pair_nl[layer, :, w], layer)
            h, l = split(value)
            if layer == 1:
                s.slope[:, w] = 1.0 - value * value
            s.hid_nh[layer, :, w] = h
            s.hid_nl[layer, :, w] = l
            if layer == 0:
                s.flux[:, n] = flux_of(h, l, layer) * s.masks_n[:, 384:512]

        each_a(body)

    def back_near(layer, gflux):
        def body(w, h_, n):
            gp = hidden_grad(gflux[:, w], gflux[:, h_], layer) * s.slope[:, w]
            s.gpre_nh[:, w], s.gpre_nl[:, w] = split(gp)

        each_a(body)

    def back_pair(layer):
        def body(w, h_, n):
            both = pair_grad(s.gpre_nh[:, w], s.gpre_nl[:, w], layer)
            s.gin[:, n] = both[:, 0:128]
            s.gout[:, n] = both[:, 128:256]

        each_a(body)

    def far_pairs(which, layer):
        def step(pair):
            rows = pl.ds(64 * pair, 64)
            all_of(which, pair).wait_recv()
            for side in range(2):
                part_rows = pl.ds(64 * pair + CAP * side, CAP)
                x = oriented([s.got[which, part_rows, narrow(a)] for a in range(4)], marks_of(s.masks_f, part_rows))
                for a in range(4):
                    s.pair_fh[layer, part_rows, low(a)], s.pair_fl[layer, part_rows, low(a)] = split(x[a])
            stack = lambda ref, cut: jnp.concatenate([ref[rows, cut(a)] for a in range(4)], axis=0)
            value = hidden(stack(s.pair_fh.at[layer], wide), stack(s.pair_fl.at[layer], wide), layer)
            h, l = split(value)
            part_of = lambda v, a: v[64 * a : 64 * a + 64]
            for a in range(4):
                s.hid_fh[layer, rows, wide(a)] = part_of(h, a)
                s.hid_fl[layer, rows, wide(a)] = part_of(l, a)
            if layer == 0:
                fh, fl = split(flux_of(h, l, layer))
                for a in range(4):
                    s.flux_fh[rows, narrow(a)] = part_of(fh, a)
                    s.flux_fl[rows, narrow(a)] = part_of(fl, a)
            else:
                gh, gl = split(stack(s.ghid_f, wide) * (1.0 - value * value))
                both = pair_grad(gh, gl, layer)
                ih, il = split(both[:, 0:128])
                for a in range(4):
                    s.gpre_fh[rows, wide(a)] = part_of(gh, a)
                    s.gpre_fl[rows, wide(a)] = part_of(gl, a)
                    s.gin_fh[rows, narrow(a)] = part_of(ih, a)
                    s.gin_fl[rows, narrow(a)] = part_of(il, a)
                for side in range(2):
                    part_rows = pl.ds(64 * pair + CAP * side, CAP)
                    cut = lambda a: both[64 * a + CAP * side : 64 * a + CAP * side + CAP, 128:256]
                    x = turned_back([cut(a) for a in range(4)], marks_of(s.masks_f, part_rows))
                    for a in range(4):
                        s.sent[which + 1, part_rows, narrow(a)] = x[a]
                for side in range(2):
                    far_copy(which + 1, pair, side, -1).start()

        for pair in (3, 2, 1, 0):
            step(pair)

    def far_inner(layer):
        both = dot(s.rem_t[...], s.trace[...]).astype(BF16)
        for a in range(4):
            s.pair_fh[layer, :, high(a)] = both[:, narrow(a)]
            s.pair_fl[layer, :, high(a)] = both[:, 512 + 128 * a : 640 + 128 * a]

    def weight_grads(parts):
        rows_of = lambda ref, cut: jnp.concatenate([ref[:, cut(a)] for a in range(4)], axis=0)
        xh, xl, gph, gpl, hh, hl, g = parts
        gh, gl, x = rows_of(gph, wide), rows_of(gpl, wide), rows_of(xh, wide)
        one = dot_tn(x, gh) + dot_tn(rows_of(xl, wide), gh) + dot_tn(x, gl)
        two = dot_tn(rows_of(hh, wide), rows_of(g, wide))
        top = dot_tn(rows_of(hl, wide), rows_of(g, high))
        two = two[:, 0:128] + two[:, 128:256] + top
        row = jnp.sum(gh.astype(F32) + gl.astype(F32), axis=0, keepdims=True)
        return one, two, row

    def pack_grads(layer, one, two, row):
        r, c = iota((256, 256), 0), iota((256, 256), 1)
        one = jnp.where(((r >> 5) & 3) == (c >> 6), one, 0.0)
        one = one[:, 0:128] + one[:, 128:256]
        one = one + pltpu.roll(one, 64, 1)
        halves = [sum(one[128 * half + 32 * b : 128 * half + 32 * b + 32] for b in range(4)) for half in range(2)]
        one = jnp.concatenate(halves, axis=0)
        r, c = iota((256, 128), 0), iota((256, 128), 1)
        two = jnp.where((r >> 6) == (c >> 5), two, 0.0)
        two = sum(two[64 * b : 64 * b + 64] for b in range(4))
        two = two + pltpu.roll(two, 64, 1)
        two = two + pltpu.roll(two, 32, 1)
        row = row[:, 0:128] + row[:, 128:256]
        row = row + pltpu.roll(row, 64, 1)
        r, c = iota((64, 128), 0), iota((64, 128), 1)
        column = jnp.sum(jnp.where(r == c, row, 0.0), axis=1, keepdims=True)
        value = jnp.where(c < 64, one, jnp.where(c < 96, two, jnp.where(c == 96, column, 0.0)))
        s.packed[layer] = value

    def piece(j):
        return pl.ds(pl.multiple_of(j * 8, 8), 8)

    def remote(src, dst, sems, device):
        return pltpu.make_async_remote_copy(
            src_ref=src, dst_ref=dst, send_sem=sems[0], recv_sem=sems[1], device_id=(device,), device_id_type=MESH
        )

    def sems(layer, stage):
        return s.ar_send.at[layer, stage], s.ar_recv.at[layer, stage]

    def scatter(layer):
        return [
            remote(s.packed.at[layer, piece(lax.rem(mine + t, group))], s.part.at[layer, mine], sems(layer, 0), in_group(t))
            for t in range(1, group)
        ]

    def spread(layer):
        here = s.part_sum.at[layer, rank]
        return [remote(here, here, sems(layer, 1), across(t)) for t in range(1, others)]

    def collect(layer):
        here, there = s.total_v.at[layer, piece(mine)], s.total.at[layer, piece(mine)]
        return [remote(here, there, sems(layer, 2), in_group(t)) for t in range(1, group)]

    def stage_bytes(layer, stage):
        here = (
            s.part.at[layer, pl.ds(0, group - 1)],
            s.part_sum.at[layer, pl.ds(0, others - 1)],
            s.total.at[layer, pl.ds(0, 8 * (group - 1))],
        )[stage]
        return remote(here, here, sems(layer, stage), in_group(1))

    def start(copies):
        for copy in copies:
            copy.start()

    def reduce_start(layer):
        start(scatter(layer))
        s.part[layer, mine] = s.packed[layer, piece(mine), :]

    def reduce_middle(layer):
        stage_bytes(layer, 0).wait()
        value = s.part[layer, 0]
        for t in range(1, group):
            value = value + s.part[layer, t]
        s.part_sum[layer, rank] = value
        start(spread(layer))

    def push_piece(layer):
        return pltpu.make_async_copy(
            s.total_v.at[layer, piece(mine)], s.total.at[layer, piece(mine)], s.out_sem.at[1 + layer]
        )

    def reduce_last(layer):
        stage_bytes(layer, 1).wait()
        value = s.part_sum[layer, 0]
        for t in range(1, others):
            value = value + s.part_sum[layer, t]
        s.total_v[layer, piece(mine), :] = value
        start(collect(layer))
        push_piece(layer).start()

    with jax.named_scope("send_table"):
        order = (0, 4, 1, 5, 2, 6, 3, 7)
        pulls["send"].wait()
        row = s.send_v[...]
        row = jnp.concatenate([row[:, CAP * b : CAP * b + CAP] for b in order], axis=1)
        for f in range(6):
            s.sel_t[f * E : (f + 1) * E, :] = ones_where(6 * iota((E, SLOTS), 0) + f == row, BF16)
        eye = ones_where(iota((SLOTS, SLOTS), 0) == iota((SLOTS, SLOTS), 1), BF16)
        s.sel[...] = dot_nt(eye, s.sel_t[...]).astype(BF16)

    with jax.named_scope("field0"):
        pulls["state"].wait()
        pulls["live"].wait()
        alive = iota((E, 128), 0) < s.live_v[0]
        for n in range(16):
            s.field[:, narrow(n)] = jnp.where(alive, tile(s.state_v, n), 0.0)
        traces(s.field, keep_traces(0))
    far_half, close_half = slice(128, 256), slice(0, 128)
    with jax.named_scope("pack0"):
        s.sent[0, far_half] = gathered(s.sel.at[far_half], s.trace)
    with jax.named_scope("barrier"):
        pl.semaphore_wait(barrier, len(partners))
    send_all(0, 1, (3, 2))
    with jax.named_scope("pack0b"):
        s.sent[0, close_half] = gathered(s.sel.at[close_half], s.trace)
    send_all(0, 1, (1, 0))

    with jax.named_scope("tables"):
        for f in range(6):
            s.raw[f * E : (f + 1) * E, 0:FACES] = ones_where(6 * iota((E, FACES), 0) + f == iota((E, FACES), 1))
        by_kind = s.raw[:, 0:FACES].astype(BF16)
        pulls["src"].wait()
        source = s.src_v[...].reshape(1, FACES)
        near = jnp.concatenate([ones_where(6 * iota((E, FACES), 0) + f == source, BF16) for f in range(6)], axis=0)
        slot = iota((SLOTS, FACES), 0)
        slot = ((slot >> 5) & 1) * 128 + (slot >> 6) * CAP + (slot & 31)
        far = ones_where(slot + FACES == source, BF16)
        s.loc_t[...] = dot_nt(near, by_kind).astype(BF16)
        s.loc[...] = dot_nt(by_kind, near).astype(BF16)
        s.rem_t[...] = dot_nt(far, by_kind).astype(BF16)
        s.rem[...] = dot_nt(by_kind, far).astype(BF16)
        pulls["orient"].wait()
        turn = s.orient_v[...].reshape(1, FACES)
        flags = [(turn >> 1) & 1, (turn ^ (turn >> 1)) & 1, (turn ^ (turn >> 2)) & 1, jnp.where(source < FACES, 1, 0)]
        for m in range(MASKS):
            spread_out = jnp.broadcast_to(flags[m], (128, FACES)).astype(F32).astype(BF16)
            s.masks_n[:, narrow(m)] = dot_nt(by_kind, spread_out)
            s.masks_f[:, narrow(m)] = dot_nt(far, spread_out)

    def four(x):
        x = jnp.concatenate([x] * 4, axis=1)
        return jnp.concatenate([x] * 4, axis=0)

    def flux_weights(layer):
        r, c = iota((256, 256), 0), iota((256, 256), 1)
        w1 = s.w1_v[layer]
        big = jnp.concatenate([four(w1[0:32]), four(w1[32:64])], axis=0)
        big = jnp.where(((r >> 5) & 3) == (c >> 6), big, 0.0)
        s.w1h[layer], s.w1l[layer] = split(big)
        s.w1th[layer], s.w1tl[layer] = split(big.T)
        r, c = iota((128, 256), 0), iota((128, 256), 1)
        big = jnp.where((r >> 5) == (c >> 6), four(s.w2t_v[layer]), 0.0)
        h, l = split(big)
        s.w2ts[layer, 0:128] = h
        s.w2ts[layer, 128:256] = h
        s.w2tl[layer] = l
        h, l = split(big.T)
        s.w2c[layer, :, 0:128] = h
        s.w2c[layer, :, 128:256] = l
        bias = jnp.concatenate([s.b1_v[layer : layer + 1, :]] * 4, axis=1)
        s.bias[layer] = jnp.broadcast_to(bias, (8, 256))

    def volume_weights(layer):
        r, c = iota((128, 128), 0), iota((128, 128), 1)
        for axis in range(3):
            big = four(s.vol_v[layer, axis])
            big = jnp.where((r >> 5) == (c >> 5), big, 0.0) if axis < 2 else big * s.deriv_v[...]
            for value, stacked, rest in ((big, s.vs, s.vl), (big.T, s.vts, s.vtl)):
                h, l = split(value)
                stacked[layer, 0:128, narrow(axis)] = h
                stacked[layer, 128:256, narrow(axis)] = h
                rest[layer, :, narrow(axis)] = l

    with jax.named_scope("weights0"):
        for name in ("w1", "w2t", "b1", "vol", "deriv"):
            pulls[name].wait()
        flux_weights(0)
        volume_weights(0)
    with jax.named_scope("near0"):
        s.raw[...] = gathered(s.loc, s.trace)
        far_inner(0)
    with jax.named_scope("orient0"):
        orient_near(0)
    with jax.named_scope("hidden0"):
        hidden_near(0)
    with jax.named_scope("volume0"):
        volume_of(s.field, 0, False)
    with jax.named_scope("weights1"):
        flux_weights(1)
    with jax.named_scope("cotangent"):
        pulls["cot"].wait()
        traces(s.cot_v, keep_gflux(True))
    with jax.named_scope("far0"):
        far_pairs(0, 0)
    with jax.named_scope("field1"):
        s.flux[...] += dot(s.rem[...], s.flux_fh[...]) + dot(s.rem[...], s.flux_fl[...])
        for n in range(16):
            s.field[:, narrow(n)] += STEP_SIZE * (lift(s.flux, n // 4, n % 4) - s.volume[:, narrow(n)])
        traces(s.field, keep_traces(1))
    with jax.named_scope("pack1"):
        s.sent[1, far_half] = gathered(s.sel.at[far_half], s.trace)
    send_all(1, 1, (3, 2))
    with jax.named_scope("pack1b"):
        s.sent[1, close_half] = gathered(s.sel.at[close_half], s.trace)
    send_all(1, 1, (1, 0))
    with jax.named_scope("cotangent_far"):
        s.gflux_f[...] = dot(s.rem_t[...], s.gflux[...]).astype(BF16)
        for a in range(4):
            s.ghid_f[:, wide(a)] = hidden_grad(s.gflux_f[:, wide(a)], s.gflux_f[:, high(a)], 1)
    with jax.named_scope("near1"):
        s.raw[...] = gathered(s.loc, s.trace)
        far_inner(1)
    with jax.named_scope("orient1"):
        orient_near(1)
    with jax.named_scope("hidden1"):
        hidden_near(1)
    with jax.named_scope("back1"):
        back_near(1, s.gflux_n)
        back_pair(1)
    with jax.named_scope("whole0"):
        for far, here in ((s.pair_fh, s.pair_nh), (s.pair_fl, s.pair_nl)):
            value = dot(s.rem[...], jnp.concatenate([far[0, :, low(a)] for a in range(4)], axis=1)).astype(BF16)
            for a in range(4):
                here[0, :, low(a)] += value[:, narrow(a)]
        for far, here in ((s.hid_fh, s.hid_nh), (s.hid_fl, s.hid_nl)):
            for a in range(4):
                own = s.masks_n[:, 384:512].astype(BF16)
                value = dot(s.rem[...], far[0, :, wide(a)]).astype(BF16)
                here[0, :, wide(a)] = here[0, :, wide(a)] * jnp.concatenate([own, own], axis=1) + value
    with jax.named_scope("weight_grads1_near"):
        parts = s.pair_nh.at[1], s.pair_nl.at[1], s.gpre_nh, s.gpre_nl, s.hid_nh.at[1], s.hid_nl.at[1], s.gflux_n
        s.one[...], s.two[...], row = weight_grads(parts)
        s.row[...] = jnp.broadcast_to(row, (8, 256))
    with jax.named_scope("far1"):
        far_pairs(1, 1)

    with jax.named_scope("turn1"):
        turn_back_near()
    with jax.named_scope("scatter1"):
        both = dot(s.loc_t[...], s.turn[...])
        value = both[:, 0:512] + both[:, 512:1024]
        s.gin[...] += value + dot(s.rem[...], s.gin_fh[...]) + dot(s.rem[...], s.gin_fl[...])
    with jax.named_scope("volume1"):
        volume_weights(1)
        volume_of(s.cot_v, 1, True)
    with jax.named_scope("weight_grads1"):
        parts = s.pair_fh.at[1], s.pair_fl.at[1], s.gpre_fh, s.gpre_fl, s.hid_fh.at[1], s.hid_fl.at[1], s.gflux_f
        one, two, row = weight_grads(parts)
        pack_grads(1, one + s.one[...], two + s.two[...], row + s.row[0:1, :])
        reduce_start(1)
    with jax.named_scope("slope0"):
        for a in range(4):
            h = s.hid_nh[0, :, wide(a)].astype(F32) + s.hid_nl[0, :, wide(a)].astype(F32)
            s.slope[:, wide(a)] = 1.0 - h * h
    with jax.named_scope("wait2"):
        all_of(2).wait_recv()
    with jax.named_scope("grad1"):
        h, l = split(s.got[2])
        s.gin[...] += dot(s.sel_t[...], h) + dot(s.sel_t[...], l)
        for n in range(16):
            s.grad[:, narrow(n)] = tile(s.cot_v, n) - STEP_SIZE * s.volume[:, narrow(n)] + lift(s.gin, n // 4, n % 4)
        traces(s.grad, keep_gflux(False))
    with jax.named_scope("back0"):
        back_near(0, s.gflux)
    with jax.named_scope("weight_grads0"):
        parts = s.pair_nh.at[0], s.pair_nl.at[0], s.gpre_nh, s.gpre_nl, s.hid_nh.at[0], s.hid_nl.at[0], s.gflux
        pack_grads(0, *weight_grads(parts))
        reduce_start(0)
    with jax.named_scope("sum1a"):
        reduce_middle(1)
    with jax.named_scope("back0_pair"):
        back_pair(0)
    with jax.named_scope("pack3"):
        h, l = split(s.gout[...])
        s.turn[:, 0:512] = h
        s.turn[:, 512:1024] = l
        value = gathered(s.rem_t.at[far_half], s.turn)
        x = turned_back([value[:, narrow(a)] for a in range(4)], marks_of(s.masks_f, far_half))
        for a in range(4):
            s.sent[3, far_half, narrow(a)] = x[a]
    send_all(3, -1, (3,))
    with jax.named_scope("turn0"):
        turn_back_near()
    with jax.named_scope("pack3b"):
        s.sent[3, close_half] = gathered(s.rem_t.at[close_half], s.turn)
    with jax.named_scope("sum0a"):
        reduce_middle(0)
    send_all(3, -1, (2, 1, 0))
    with jax.named_scope("scatter0"):
        both = dot(s.loc_t[...], s.turn[...])
        s.gin[...] += both[:, 0:512] + both[:, 512:1024]
    with jax.named_scope("volume0b"):
        volume_of(s.grad, 0, True)
    with jax.named_scope("sum1b"):
        reduce_last(1)
    with jax.named_scope("sum0b"):
        reduce_last(0)
    with jax.named_scope("wait3"):
        all_of(3).wait_recv()
    with jax.named_scope("grad0"):
        h, l = split(s.got[3])
        s.gin[...] += dot(s.sel_t[...], h) + dot(s.sel_t[...], l)
        for n in range(16):
            value = s.grad[:, narrow(n)] - STEP_SIZE * s.volume[:, narrow(n)] + lift(s.gin, n // 4, n % 4)
            s.out_v[:, narrow(n)] = jnp.where(alive, value, 0.0)
        push = pltpu.make_async_copy(s.out_v, s.out, s.out_sem.at[0])
        push.start()
    with jax.named_scope("sumc"):
        stage_bytes(1, 2).wait()
        stage_bytes(0, 2).wait()
    with jax.named_scope("sent"):
        for which in (0, 1):
            drain = pltpu.make_async_copy(s.sent.at[which], s.sent.at[which], s.send_sem.at[which])
            drain.wait()
        all_of(2).wait_send()
        all_of(3).wait_send()
        push.wait()
        push_piece(1).wait()
        push_piece(0).wait()


def finish(factor, total_ref, field_ref, out_ref, w1_ref, b1_ref, w2t_ref):
    out_ref[...] = field_ref[...]
    for layer in range(2):
        value = total_ref[layer] * factor
        w1_ref[layer] = value[:, 0:64]
        w2t_ref[layer] = value.T[64:96, :]
        b1_ref[layer : layer + 1, :] = value.T[96:97, :]


def local(count, state, cotangent, elem_count, face_src, face_orient, send_face, vol_weight, w1, b1, w2):
    constant = np.zeros((128, 128), np.float32)
    for a in range(4):
        for k in range(4):
            constant[32 * k : 32 * k + 32, 32 * a : 32 * a + 32] = DERIV[a, k]
    vmem = pl.BlockSpec(memory_space=pltpu.VMEM)
    smem = pl.BlockSpec(memory_space=pltpu.SMEM)
    hbm = pl.BlockSpec(memory_space=pl.ANY)
    names = [*INPUTS, *OUTPUTS, *SCRATCH]
    scratch = [pltpu.VMEM(shape, dtype) for shape, dtype in SCRATCH.values()]
    extra = dict(
        part_sum=pltpu.VMEM((2, count // 8, 8, 128), F32),
        total_v=pltpu.VMEM((2, 64, 128), F32),
        live_v=pltpu.SMEM((1,), I32),
        out_sem=pltpu.SemaphoreType.DMA((3,)),
        in_sem=pltpu.SemaphoreType.DMA((11,)),
        send_sem=pltpu.SemaphoreType.DMA((4,)),
        near_sem=pltpu.SemaphoreType.DMA((2, NEIGH)),
        back_sem=pltpu.SemaphoreType.DMA((2,)),
        ar_send=pltpu.SemaphoreType.DMA((2, 3)),
        ar_recv=pltpu.SemaphoreType.DMA((2, 3)),
    )
    names += list(extra)
    scratch += list(extra.values())
    field, total = pl.pallas_call(
        functools.partial(kernel, count, names),
        out_shape=(jax.ShapeDtypeStruct(state.shape, F32), jax.ShapeDtypeStruct((2, 64, 128), F32)),
        in_specs=[hbm, hbm, hbm, hbm, hbm, hbm] + [hbm] * 5,
        out_specs=[hbm] * 2,
        scratch_shapes=scratch,
        compiler_params=pltpu.CompilerParams(
            collective_id=0, has_side_effects=True, vmem_limit_bytes=VMEM_LIMIT
        ),
    )(
        state, cotangent, elem_count, face_src, face_orient,
        send_face.reshape(1, -1), vol_weight, w1, b1, jnp.swapaxes(w2, 1, 2), jnp.asarray(constant),
    )
    factor = (2.0 * FACES * 8 * count) ** -0.5
    grad, grad_w1, grad_b1, grad_w2t = pl.pallas_call(
        functools.partial(finish, factor),
        out_shape=(
            jax.ShapeDtypeStruct(state.shape, F32),
            jax.ShapeDtypeStruct(w1.shape, F32),
            jax.ShapeDtypeStruct(b1.shape, F32),
            jax.ShapeDtypeStruct((2, 32, 64), F32),
        ),
        in_specs=[vmem] * 2,
        out_specs=[vmem] * 4,
    )(total, field)
    return grad, grad_w1, grad_b1, jnp.swapaxes(grad_w2t, 1, 2)


def solution(mesh):
    rows, flat, whole = P("dom", None), P("dom"), P()
    return jax.shard_map(
        functools.partial(local, mesh.shape["dom"]),
        mesh=mesh,
        in_specs=(rows, rows, flat, flat, flat, flat, whole, whole, whole, whole),
        out_specs=(rows, whole, whole, whole),
        check_vma=False,
    )
```
